256 devices in a mesh: seq: 256 (over y, x, z, core).
Axes of the slice: x: 4, y: 4, z: 8, core: 2. Of those that a mesh axis runs over, the one named last changes fastest.
Arguments:
- query_rows: bfloat16 [65536, 1024], P('seq'), may hold values from -64 to 64
- key_rows: bfloat16 [65536, 1024], P('seq'), may hold values from -64 to 64
- value_rows: bfloat16 [65536, 1024], P('seq'), may hold values from -8 to 8
- out_grad: bfloat16 [65536, 1024], P('seq'), may hold values from -6 to 6
Outputs:
- attended: bfloat16 [65536, 1024], P('seq')
- query_grad: bfloat16 [65536, 1024], P('seq')
- key_grad: bfloat16 [65536, 1024], P('seq')
- value_grad: bfloat16 [65536, 1024], P('seq')
The draws below stay inside these ranges and needn't reach their ends.
All inputs are finite; a program needn't handle non-finite values.
Results may differ from the reference program's by a relative error of at most 0.022.
Values may be sent and summed in bfloat16 or wider, within the bound.
No kernel may reach another device: no remote copies, remote signals or barrier semaphores. Data moves between devices by JAX's collectives and lax.ppermute only.
A program may use at most 128 MiB of HBM per device.

```python
import functools
import math
import jax
import jax.numpy as jnp
from jax import lax

H = 16
E = 64
B = 128
D = 1024
TOKENS = 65536


def position_waves(key, amplitude):
    waves = min(TOKENS.bit_length() - 4, (E - 2) // 2)
    offsets = jax.random.uniform(key, (H, waves), jnp.float32, 0.0, 2.0 * math.pi)
    places = jnp.arange(TOKENS, dtype=jnp.int32)
    periods = 8 * 2 ** jnp.arange(waves, dtype=jnp.int32)
    turns = (places[:, None] % periods[None, :]).astype(jnp.float32) / periods.astype(jnp.float32)[None, :]
    angles = 2.0 * math.pi * turns[:, None, :] + offsets[None, :, :]
    paired = jnp.stack([jnp.cos(angles), jnp.sin(angles)], axis=3).reshape(TOKENS, H, 2 * waves)
    return jnp.pad(paired * amplitude, ((0, 0), (0, 0), (0, E - 2 * waves)))


def draw_query_rows(key, part):
    smooth = position_waves(key, math.sqrt(0.55 * math.sqrt(E)))
    key = jax.random.fold_in(key, 1)
    rows = smooth + jax.random.normal(key, (TOKENS, H, E), jnp.float32)
    return rows.reshape(TOKENS, H * E).astype(jnp.bfloat16)


def draw_key_rows(key, part):
    smooth = position_waves(key, math.sqrt(0.55 * math.sqrt(E)))
    key = jax.random.fold_in(key, 2)
    rows = smooth + jax.random.normal(key, (TOKENS, H, E), jnp.float32)
    return rows.reshape(TOKENS, H * E).astype(jnp.bfloat16)


def draw_value_rows(key, part):
    key = jax.random.fold_in(key, 3)
    streams = jax.random.split(key, 3)
    periods = jnp.exp(jax.random.uniform(streams[0], (H * E,), jnp.float32, math.log(B), math.log(TOKENS)))
    phases = jax.random.uniform(streams[1], (H * E,), jnp.float32, 0.0, 2.0 * math.pi)
    places = jnp.arange(TOKENS, dtype=jnp.float32)
    smooth = 0.9 * jnp.cos(2.0 * math.pi * places[:, None] / periods[None, :] + phases[None, :])
    rows = smooth + 0.7 * jax.random.normal(streams[2], (TOKENS, H * E), jnp.float32)
    return rows.astype(jnp.bfloat16)


def steps_of(own_key, dims, shards, least, top_value):
    def one(dim, blocks):
        steps = jax.random.uniform(jax.random.fold_in(jax.random.fold_in(own_key, 6), dim), (blocks,), jnp.float32, least / len(shards), top_value / len(shards))
        return jnp.repeat(jnp.exp(steps), dims[dim] // blocks).reshape((-1,) + (1,) * (len(dims) - dim - 1))

    gain = one(*shards[0])
    for cut in shards[1:]:
        gain = gain * one(*cut)
    return gain


def centred(key, dims, scale, most, cuts=(), kind=jnp.bfloat16):
    level = steps_of(key, dims, cuts, -0.22, 0.18) if cuts else 1.0
    array = jax.random.normal(key, dims, jnp.float32) * scale * level
    return jnp.minimum(jnp.maximum(array, -most), most).astype(kind)


def setup_inputs(seed: int = 0) -> dict:
    seeds = jax.random.split(jax.random.key(seed), 5)
    return {
        "query_rows": draw_query_rows(jax.random.fold_in(seeds[4], 71), 0),
        "key_rows": draw_key_rows(jax.random.fold_in(seeds[4], 71), 0),
        "value_rows": draw_value_rows(jax.random.fold_in(seeds[4], 71), 0),
        "out_grad": centred(seeds[3], (TOKENS, D), 1.0, 6.0, ((0, 256),)),
    }


LOG_TWO = math.log(2.0)

def halve_rows(matrix):
    halves = matrix.shape[0] // 2
    paired = matrix.reshape((halves, 2) + matrix.shape[1:]).astype(jnp.float32)
    return ((paired[:, 0] + paired[:, 1]) * 0.5).astype(jnp.bfloat16)

def spread_rows(matrix, factor):
    rows_in = matrix.shape[0]
    widened = jnp.broadcast_to(matrix[:, None], (rows_in, factor) + matrix.shape[1:])
    return widened.reshape((rows_in * factor,) + matrix.shape[1:])

def fold_rows(matrix, factor):
    groups = matrix.shape[0] // factor
    return lax.optimization_barrier(jnp.sum(matrix.reshape((groups, factor) + matrix.shape[1:]), axis=1))

def heads_of(matrix, pieces):
    return matrix.reshape(pieces, matrix.shape[0] // pieces, H, E)

def flip_pairs(blocks):
    shaped = blocks.reshape((blocks.shape[0] // 2, 2) + blocks.shape[1:])
    return shaped[:, ::-1].reshape(blocks.shape)

def arrange(level_index, query_level, key_level, value_level):
    if level_index == 0:
        pieces = query_level.shape[0] // (2 * B)
        return (heads_of(query_level, pieces), heads_of(key_level, pieces), heads_of(value_level, pieces))
    pieces = query_level.shape[0] // B
    return (heads_of(query_level, pieces), flip_pairs(heads_of(key_level, pieces)), flip_pairs(heads_of(value_level, pieces)))

def restore_keys(level_index, grads):
    if level_index == 0:
        return grads.reshape(-1, H * E)
    return flip_pairs(grads).reshape(-1, H * E)

def stat_rows(statistic):
    return jnp.transpose(statistic, (0, 2, 1)).reshape(-1, H)

def stat_blocks(statistic, pieces):
    return jnp.transpose(statistic.reshape(pieces, -1, H), (0, 2, 1))

def scores_of(queries, key_block, level_index):
    products = jnp.einsum('pqhe,pkhe->phqk', queries.astype(jnp.float32), key_block.astype(jnp.float32))
    return products * (1.0 / math.sqrt(queries.shape[3])) + level_index * LOG_TWO

def attend_forward(queries, key_block, value_block, level_index):
    scores = scores_of(queries, key_block, level_index)
    row_max = lax.optimization_barrier(jnp.max(scores, axis=3))
    raised = jnp.exp(scores - row_max[..., None])
    row_sum = lax.optimization_barrier(jnp.sum(raised, axis=3))
    rounded = raised.astype(jnp.bfloat16)
    weighted = jnp.einsum('phqk,pkhe->pqhe', rounded.astype(jnp.float32), value_block.astype(jnp.float32))
    return (row_max, row_sum, weighted)

def attend_backward(queries, key_block, value_block, row_max, cograd, flow_sum, level_index):
    scores = scores_of(queries, key_block, level_index)
    raised = jnp.exp(scores - row_max[..., None])
    rounded = raised.astype(jnp.bfloat16)
    weight_grad = jnp.einsum('pqhe,pkhe->phqk', cograd.astype(jnp.float32), value_block.astype(jnp.float32))
    dscore = (raised * (weight_grad - flow_sum[..., None])).astype(jnp.bfloat16)
    factor = 1.0 / math.sqrt(queries.shape[3])
    query_part = jnp.einsum('phqk,pkhe->pqhe', dscore.astype(jnp.float32), key_block.astype(jnp.float32)) * factor
    key_part = jnp.einsum('phqk,pqhe->pkhe', dscore.astype(jnp.float32), queries.astype(jnp.float32)) * factor
    value_part = jnp.einsum('phqk,pqhe->pkhe', rounded.astype(jnp.float32), cograd.astype(jnp.float32))
    return (query_part, key_part, value_part)

def mapped(function, operands):

    def single(items):
        outcome = function(*[item[None] for item in items])
        return tuple((piece[0] for piece in outcome))
    return lax.map(single, operands)

def combine(records, tokens):
    highest = None
    for level_index, record in enumerate(records):
        spread = spread_rows(record[1], 2 ** level_index)
        highest = spread if highest is None else jnp.maximum(highest, spread)
    level_weights = [jnp.exp(spread_rows(record[1], 2 ** level_index) - highest) for level_index, record in enumerate(records)]
    denominator = jnp.zeros((tokens, H), jnp.float32)
    numerator = jnp.zeros((tokens, H, E), jnp.float32)
    for level_index, record in enumerate(records):
        factor = 2 ** level_index
        denominator = denominator + level_weights[level_index] * spread_rows(record[2], factor)
        numerator = numerator + level_weights[level_index][:, :, None] * spread_rows(record[3], factor)
    attended = (numerator / denominator[:, :, None]).astype(jnp.bfloat16)
    return (attended, level_weights, denominator)

def descend(parts):
    running = parts[-1]
    for level_index in range(len(parts) - 2, -1, -1):
        running = parts[level_index] + spread_rows(running, 2) * 0.5
    return running.astype(jnp.bfloat16)

def reference(query_rows, key_rows, value_rows, out_grad):
    tokens = query_rows.shape[0]
    levels = (tokens // B).bit_length() - 1
    query_levels = [query_rows]
    key_levels = [key_rows]
    value_levels = [value_rows]
    for level_index in range(1, levels):
        query_levels.append(halve_rows(query_levels[-1]))
        key_levels.append(halve_rows(key_levels[-1]))
        value_levels.append(halve_rows(value_levels[-1]))
    arranged = []
    records = []
    for level_index in range(levels):
        blocks = arrange(level_index, query_levels[level_index], key_levels[level_index], value_levels[level_index])
        arranged.append(blocks)
        row_max, row_sum, weighted = mapped(functools.partial(attend_forward, level_index=level_index), blocks)
        records.append((row_max, stat_rows(row_max), stat_rows(row_sum), weighted.reshape(-1, H, E)))
    attended, level_weights, denominator = combine(records, tokens)
    grad_heads = out_grad.reshape(tokens, H, E).astype(jnp.float32)
    alignment = lax.optimization_barrier(jnp.sum(grad_heads * attended.astype(jnp.float32), axis=2))
    query_parts = []
    key_parts = []
    value_parts = []
    for level_index in range(levels):
        factor = 2 ** level_index
        portion = level_weights[level_index] / denominator
        cograd = fold_rows(portion[:, :, None] * grad_heads, factor).astype(jnp.bfloat16)
        flow_sum = fold_rows(portion * alignment, factor)
        blocks = arranged[level_index]
        pieces = blocks[0].shape[0]
        operands = blocks + (records[level_index][0], cograd.reshape(blocks[0].shape), stat_blocks(flow_sum, pieces))
        query_part, key_part, value_part = mapped(functools.partial(attend_backward, level_index=level_index), operands)
        query_parts.append(query_part.reshape(-1, H * E))
        key_parts.append(restore_keys(level_index, key_part))
        value_parts.append(restore_keys(level_index, value_part))
    return (attended.reshape(tokens, H * E), descend(query_parts), descend(key_parts), descend(value_parts))
```

```python
import functools
import math

import jax
import jax.numpy as jnp
from jax import lax
from jax.experimental import pallas as pl
from jax.experimental.pallas import tpu as pltpu
from jax.sharding import PartitionSpec as P

H = 16
E = 64
B = 128
LANES = 128
PAIRS = 8
RING = 16
LN2 = math.log(2.0)
F32 = jnp.float32
BF16 = jnp.bfloat16

ROWS = {l: 1024 >> (l - 2) for l in range(2, 9)}
FIRST = {2: 0, 3: 1024, 4: 1536, 5: 1792, 6: 1920, 7: 1984, 8: 2016}
STACK = 2048


def dot(a, b):
    return lax.dot_general(a, b, (((1,), (0,)), ((), ())), preferred_element_type=F32)


def dot_nt(a, b):
    return lax.dot_general(a, b, (((1,), (1,)), ((), ())), preferred_element_type=F32)


def dot_tn(a, b):
    return lax.dot_general(a, b, (((0,), (0,)), ((), ())), preferred_element_type=F32)


def lane_of(rows):
    return lax.broadcasted_iota(jnp.int32, (rows, LANES), 1)


def low_lanes(rows):
    return lane_of(rows) < E


def swap_halves(x):
    return pltpu.roll(x, E, 1)


def pool_matrix(rows_out, factor=2):
    r = lax.broadcasted_iota(jnp.int32, (rows_out, rows_out * factor), 0)
    c = lax.broadcasted_iota(jnp.int32, (rows_out, rows_out * factor), 1)
    return jnp.where(c // factor == r, 1.0 / factor, 0.0).astype(BF16)


def spread_matrix(rows_in, factor, value=1.0):
    r = lax.broadcasted_iota(jnp.int32, (rows_in * factor, rows_in), 0)
    c = lax.broadcasted_iota(jnp.int32, (rows_in * factor, rows_in), 1)
    return jnp.where(r // factor == c, value, 0.0).astype(BF16)


def pieces(x, count):
    out = []
    for _ in range(count):
        part = x.astype(BF16)
        out.append(part)
        x = x - part.astype(F32)
    return out


def spread(matrix, x, count):
    total = None
    for part in pieces(x, count):
        term = dot(matrix, part)
        total = term if total is None else total + term
    return total


def whole(shape):
    return pl.BlockSpec(memory_space=pltpu.VMEM)


def call(kernel, outs, ins, scratch=(), flops=1e8, smem_first=False):
    specs = [pl.BlockSpec(memory_space=pltpu.VMEM) for _ in ins]
    if smem_first:
        specs[0] = pl.BlockSpec(memory_space=pltpu.SMEM)
    return pl.pallas_call(
        kernel,
        out_shape=[jax.ShapeDtypeStruct(s, d) for s, d in outs],
        in_specs=specs,
        out_specs=[pl.BlockSpec(memory_space=pltpu.VMEM) for _ in outs],
        scratch_shapes=list(scratch),
        compiler_params=pltpu.CompilerParams(vmem_limit_bytes=40 * 1024 * 1024),
        cost_estimate=pl.CostEstimate(
            flops=int(flops), bytes_accessed=2_000_000, transcendentals=0
        ),
    )(*ins)


def pool_kernel(q_ref, k_ref, v_ref, q1_ref, kv1_ref, send_ref):
    halve = pool_matrix(128)
    quarter = pool_matrix(64)
    low = low_lanes(64)
    low32 = low_lanes(32)
    for p in range(PAIRS):
        cols = slice(LANES * p, LANES * (p + 1))
        level2 = []
        for index, ref in enumerate((q_ref, k_ref, v_ref)):
            one = dot(halve, ref[:, cols]).astype(BF16)
            if index == 0:
                q1_ref[:, cols] = one
            else:
                kv1_ref[B * (index - 1) : B * index, cols] = one
            level2.append(dot(quarter, one).astype(BF16).astype(F32))
        q, k, v = level2
        qr, kr, vr = swap_halves(q), swap_halves(k), swap_halves(v)
        send_ref[2 * p, 0:64, :] = jnp.where(low, k, vr).astype(BF16)
        send_ref[2 * p + 1, 0:64, :] = jnp.where(low, kr, v).astype(BF16)
        send_ref[2 * p, 64:96, :] = jnp.where(low32, q[0:32], qr[32:64]).astype(BF16)
        send_ref[2 * p + 1, 64:96, :] = jnp.where(low32, qr[0:32], q[32:64]).astype(BF16)


def prepare_kernel(recv_ref, q_ref, kv_ref, kv5_ref):
    low32 = low_lanes(32)
    for d in range(RING):
        kv_ref[64 * d : 64 * d + 64, :] = recv_ref[d, 0:64, :]
        packed = recv_ref[d, 64:96, :].astype(F32) * 0.125
        q_ref[64 * d : 64 * d + 32, :] = jnp.where(low32, packed, 0.0).astype(BF16)
        q_ref[64 * d + 32 : 64 * d + 64, :] = jnp.where(
            low32, swap_halves(packed), 0.0
        ).astype(BF16)
    for level in range(2, 8):
        rows = ROWS[level]
        step = min(rows, 256)
        matrix = pool_matrix(step // 2)
        for start in range(0, rows, step):
            source = slice(FIRST[level] + start, FIRST[level] + start + step)
            at = FIRST[level + 1] + start // 2
            target = slice(at, at + step // 2)
            q_ref[target, :] = dot(matrix, q_ref[source, :]).astype(BF16)
            kv_ref[target, :] = dot(matrix, kv_ref[source, :]).astype(BF16)
    end = FIRST[8] + ROWS[8]
    q_ref[end:STACK, :] = jnp.zeros((STACK - end, LANES), BF16)
    kv_ref[end:STACK, :] = jnp.zeros((STACK - end, LANES), BF16)
    kv5_ref[...] = kv_ref[FIRST[5] : FIRST[5] + B, :]


def climb_kernel(flag_ref, own_ref, other_ref, out_ref):
    matrix = pool_matrix(64)
    own = dot(matrix, own_ref[...])
    other = dot(matrix, other_ref[...])
    is_lower = flag_ref[0] == 0
    out_ref[0:64, :] = jnp.where(is_lower, own, other).astype(BF16)
    out_ref[64:128, :] = jnp.where(is_lower, other, own).astype(BF16)


def local_forward_kernel(q_ref, k_ref, v_ref, q1_ref, k1_ref, v1_ref, att_ref, lse_ref):

    def one_level(q, k, v, bias):
        rows = q.shape[0]
        low_q = low_lanes(rows)
        low_v = low_lanes(v.shape[0])
        scaled = q.astype(F32) * 0.125
        values = v.astype(F32)
        tops = []
        sums = []
        for j in range(2):
            mine_q = low_q if j == 0 else jnp.logical_not(low_q)
            mine_v = low_v if j == 0 else jnp.logical_not(low_v)
            s = dot_nt(jnp.where(mine_q, scaled, 0.0).astype(BF16), k)
            top = jnp.max(s, axis=1, keepdims=True)
            raised = jnp.exp(s - top)
            sums.append(
                dot(raised.astype(BF16), jnp.where(mine_v, values, 1.0).astype(BF16))
            )
            tops.append(top)
        weighted = jnp.where(low_q, sums[0], sums[1])
        total = swap_halves(jnp.where(low_q, sums[1], sums[0]))
        top = jnp.where(low_q, tops[0], tops[1])
        return weighted / total, top + jnp.log(total) + bias

    att0, lse0 = one_level(q_ref[...], k_ref[...], v_ref[...], 0.0)
    att1, lse1 = one_level(q1_ref[...], k1_ref[...], v1_ref[...], LN2)
    double = spread_matrix(128, 2)
    att1 = spread(double, att1, 2)
    lse1 = spread(double, lse1, 3)
    high = jnp.maximum(lse0, lse1)
    e0 = jnp.exp(lse0 - high)
    e1 = jnp.exp(lse1 - high)
    den = e0 + e1
    att_ref[...] = (e0 * att0 + e1 * att1) / den
    lse_ref[...] = high + jnp.log(den)


def head_forward_kernel(q_ref, kv_ref, s5_ref, s6_ref, s7_ref, s8_ref, send_ref):

    def attend(q, kv):
        s = dot_nt(q, kv)
        top = jnp.max(s, axis=1, keepdims=True)
        raised = jnp.exp(s - top)
        ones = jnp.where(low_lanes(B), 1.0, kv.astype(F32)).astype(BF16)
        return jnp.broadcast_to(top, (q.shape[0], LANES)), dot(raised.astype(BF16), ones)

    siblings = {5: s5_ref, 6: s6_ref, 7: s7_ref, 8: s8_ref}
    tops, sums = None, None
    for level in (8, 7, 6, 5):
        rows = ROWS[level]
        q = q_ref[FIRST[level] : FIRST[level] + rows, :]
        top, total = attend(q, siblings[level][...])
        top = top + level * LN2
        if tops is None:
            tops, sums = top, total
            continue
        double = spread_matrix(rows // 2, 2)
        up_top = spread(double, tops, 3)
        up_sum = spread(double, sums, 2)
        high = jnp.maximum(top, up_top)
        sums = jnp.exp(top - high) * total + jnp.exp(up_top - high) * up_sum
        tops = high
    tops, sums = [tops], [sums]
    double = spread_matrix(64, 2)
    for level in (4, 3, 2):
        new_tops, new_sums = [], []
        for block in range(ROWS[level] // B):
            at = FIRST[level] + B * block
            beside = FIRST[level] + B * (block ^ 1)
            top, total = attend(q_ref[at : at + B, :], kv_ref[beside : beside + B, :])
            top = top + level * LN2
            half = slice(64 * (block % 2), 64 * (block % 2) + 64)
            up_top = spread(double, tops[block // 2][half], 3)
            up_sum = spread(double, sums[block // 2][half], 2)
            high = jnp.maximum(top, up_top)
            new_sums.append(jnp.exp(top - high) * total + jnp.exp(up_top - high) * up_sum)
            new_tops.append(high)
        tops, sums = new_tops, new_sums
    lane = lane_of(B)
    for block in range(8):
        total = sums[block]
        count = jnp.broadcast_to(total[:, 0:1], (B, LANES))
        att = total / count
        lse = tops[block] + jnp.log(count)
        hi, mid, lo = pieces(lse, 3)
        out = jnp.where(lane >= E, att, 0.0)
        for index, part in enumerate((hi, mid, lo)):
            out = jnp.where(lane == index, part.astype(F32), out)
        out = out.astype(BF16)
        send_ref[2 * block, :, :] = out[0:64]
        send_ref[2 * block + 1, :, :] = out[64:128]


def combine_kernel(
    att_ref, lse_ref, recv_ref, grad_ref,
    out_ref, full_ref, align_ref, r1_ref, g1_ref, f1_ref, send_ref,
    lse_s, grad_s, align_s, r_s, g_s, f_s,
):
    low = low_lanes(256)
    low64 = low_lanes(64)
    lane64 = lane_of(64)
    four = spread_matrix(64, 4)
    r = lax.broadcasted_iota(jnp.int32, (LANES, LANES), 0)
    c = lax.broadcasted_iota(jnp.int32, (LANES, LANES), 1)
    per_head = jnp.where(r // E == c // E, 1.0, 0.0).astype(BF16)

    def step(p, carry):
        cols = pl.ds(pl.multiple_of(p * LANES, LANES), LANES)
        first = dot(four, recv_ref[2 * p])
        second = dot(four, recv_ref[2 * p + 1])
        att2 = jnp.where(low, swap_halves(first), second)
        lse_a = first[:, 0:1] + first[:, 1:2] + first[:, 2:3]
        lse_b = second[:, 0:1] + second[:, 1:2] + second[:, 2:3]
        lse2 = jnp.where(low, lse_a, lse_b)
        lse01 = lse_ref[:, cols]
        high = jnp.maximum(lse01, lse2)
        e1 = jnp.exp(lse01 - high)
        e2 = jnp.exp(lse2 - high)
        den = e1 + e2
        attended = ((e1 * att_ref[:, cols] + e2 * att2) / den).astype(BF16)
        out_ref[:, cols] = attended
        full = high + jnp.log(den)
        grad = grad_ref[:, cols].astype(F32)
        product = grad * attended.astype(F32)
        align = None
        for part in pieces(product, 3):
            term = dot(part, per_head)
            align = term if align is None else align + term
        full_ref[:, cols] = full
        align_ref[:, cols] = align
        lse_s[...] = full
        grad_s[...] = grad
        align_s[...] = align

        def fold(lse, grads, aligns, rows):
            a, b = pl.ds(0, rows, stride=2), pl.ds(1, rows, stride=2)
            la, lb = lse[a, :], lse[b, :]
            least = jnp.minimum(la, lb)
            ea, eb = jnp.exp(least - la), jnp.exp(least - lb)
            return (
                least,
                ea * grads[a, :] + eb * grads[b, :],
                ea * aligns[a, :] + eb * aligns[b, :],
            )

        r1, g1, f1 = fold(lse_s, grad_s, align_s, 128)
        r1_ref[:, cols] = r1
        g1_ref[:, cols] = g1.astype(BF16)
        f1_ref[:, cols] = f1
        r_s[...] = r1
        g_s[...] = g1
        f_s[...] = f1
        r2, g2, f2 = fold(r_s, g_s, f_s, 64)
        for j in range(2):
            values = g2 if j == 1 else swap_halves(g2)
            packed = jnp.where(low64, 0.0, values)
            rc = jnp.broadcast_to(r2[:, E * j : E * j + 1], (64, LANES))
            fc = jnp.broadcast_to(f2[:, E * j : E * j + 1], (64, LANES))
            for index, part in enumerate(pieces(rc, 3) + pieces(fc, 3)):
                packed = jnp.where(lane64 == index, part.astype(F32), packed)
            send_ref[2 * p + j] = packed.astype(BF16)
        return carry

    lax.fori_loop(0, PAIRS, step, 0)


def level_backward(q, kv, least, grads, level):
    rows = q.shape[0]
    low = low_lanes(rows)
    s = dot_nt(q, kv)
    weight = jnp.exp(s + (level * LN2 - least[:, 0:1]))
    cograd = jnp.where(low, 0.0, grads).astype(BF16)
    slope = (weight * (dot_nt(cograd, kv) - grads[:, 0:1])).astype(BF16)
    query_part = dot(slope, kv) * 0.125
    other_part = dot_tn(slope, q) + dot_tn(weight.astype(BF16), cograd)
    return query_part, other_part


def head_top_kernel(
    recv_ref, q_ref, s5_ref, s6_ref, s7_ref, s8_ref,
    r_ref, g_ref, q5_ref, p5_ref, p6_ref, p7_ref, p8_ref,
):
    low = low_lanes(64)
    for d in range(RING):
        slot = recv_ref[d].astype(F32)
        least = slot[:, 0:1] + slot[:, 1:2] + slot[:, 2:3]
        flow = slot[:, 3:4] + slot[:, 4:5] + slot[:, 5:6]
        r_ref[64 * d : 64 * d + 64, :] = jnp.broadcast_to(least, (64, LANES))
        g_ref[64 * d : 64 * d + 64, :] = jnp.where(low, flow, slot)
    for level in range(2, 8):
        rows = ROWS[level + 1]
        a = pl.ds(FIRST[level], rows, stride=2)
        b = pl.ds(FIRST[level] + 1, rows, stride=2)
        la, lb = r_ref[a, :], r_ref[b, :]
        least = jnp.minimum(la, lb)
        to = slice(FIRST[level + 1], FIRST[level + 1] + rows)
        r_ref[to, :] = least
        g_ref[to, :] = jnp.exp(least - la) * g_ref[a, :] + jnp.exp(least - lb) * g_ref[b, :]
    end = FIRST[8] + ROWS[8]
    r_ref[end:STACK, :] = jnp.zeros((STACK - end, LANES), F32)
    g_ref[end:STACK, :] = jnp.zeros((STACK - end, LANES), F32)
    siblings = {5: s5_ref, 6: s6_ref, 7: s7_ref, 8: s8_ref}
    parts = {5: p5_ref, 6: p6_ref, 7: p7_ref, 8: p8_ref}
    running = None
    for level in (8, 7, 6, 5):
        at = slice(FIRST[level], FIRST[level] + ROWS[level])
        query_part, other_part = level_backward(
            q_ref[at, :], siblings[level][...], r_ref[at, :], g_ref[at, :], level
        )
        parts[level][...] = other_part
        if running is None:
            running = query_part
        else:
            running = query_part + spread(spread_matrix(ROWS[level] // 2, 2, 0.5), running, 2)
    q5_ref[...] = running


def descend_kernel(flag_ref, kept_ref, returned_ref, part_ref, kept_out, sent_out):
    back = kept_ref[...] + returned_ref[...].astype(F32)
    double = spread_matrix(64, 2, 0.5)
    first = spread(double, back[0:64], 2)
    second = spread(double, back[64:128], 2)
    is_lower = flag_ref[0] == 0
    kept_out[...] = jnp.where(is_lower, first, second)
    sent_out[...] = (jnp.where(is_lower, second, first) + part_ref[...]).astype(BF16)


def head_low_kernel(q_ref, kv_ref, r_ref, g_ref, q5_ref, kept_ref, returned_ref, send_ref):
    double = spread_matrix(64, 2, 0.5)
    low32 = low_lanes(32)
    query_up = [q5_ref[...]]
    other_up = [kept_ref[...] + returned_ref[...].astype(F32)]
    for level in (4, 3, 2):
        blocks = ROWS[level] // B
        query_parts = [None] * blocks
        other_parts = [None] * blocks
        for block in range(blocks):
            at = FIRST[level] + B * block
            beside = FIRST[level] + B * (block ^ 1)
            query_part, other_part = level_backward(
                q_ref[at : at + B, :],
                kv_ref[beside : beside + B, :],
                r_ref[at : at + B, :],
                g_ref[at : at + B, :],
                level,
            )
            query_parts[block] = query_part
            other_parts[block ^ 1] = other_part
        for block in range(blocks):
            half = slice(64 * (block % 2), 64 * (block % 2) + 64)
            query_parts[block] = query_parts[block] + spread(
                double, query_up[block // 2][half], 2
            )
            other_parts[block] = other_parts[block] + spread(
                double, other_up[block // 2][half], 2
            )
        query_up, other_up = query_parts, other_parts
    for block in range(8):
        moved = swap_halves(query_up[block])
        for j in range(2):
            d = 2 * block + j
            at = 64 * j
            send_ref[d, 0:64, :] = other_up[block][at : at + 64].astype(BF16)
            send_ref[d, 64:96, :] = jnp.where(
                low32, query_up[block][at : at + 32], moved[at + 32 : at + 64]
            ).astype(BF16)


def local_backward_kernel(
    q_ref, k_ref, v_ref, grad_ref, lse_ref, align_ref,
    q1_ref, k1_ref, v1_ref, r1_ref, g1_ref, f1_ref,
    dq_ref, dk_ref, dv_ref, dk1_ref, dv1_ref,
):

    def one_level(q, k, v, grads, lse, align, bias):
        rows = q.shape[0]
        low_q = low_lanes(rows)
        low_k = low_lanes(k.shape[0])
        scaled = q.astype(F32) * 0.125
        wide = grads.astype(F32)
        scaled_b = scaled.astype(BF16)
        results = []
        for j in range(2):
            mine = low_q if j == 0 else jnp.logical_not(low_q)
            s = dot_nt(jnp.where(mine, scaled, 0.0).astype(BF16), k)
            weight = jnp.exp(s + (bias - lse[:, E * j : E * j + 1]))
            through = dot_nt(jnp.where(mine, wide, 0.0).astype(BF16), v)
            slope = (weight * (through - align[:, E * j : E * j + 1])).astype(BF16)
            results.append(
                (dot(slope, k), dot_tn(slope, scaled_b), dot_tn(weight.astype(BF16), grads))
            )
        return (
            jnp.where(low_q, results[0][0], results[1][0]) * 0.125,
            jnp.where(low_k, results[0][1], results[1][1]),
            jnp.where(low_k, results[0][2], results[1][2]),
        )

    dq1, dk1, dv1 = one_level(
        q1_ref[...], k1_ref[...], v1_ref[...], g1_ref[...], r1_ref[...], f1_ref[...], LN2
    )
    dk1_ref[...] = dk1.astype(BF16)
    dv1_ref[...] = dv1.astype(BF16)
    dq, dk, dv = one_level(
        q_ref[...], k_ref[...], v_ref[...], grad_ref[...], lse_ref[...], align_ref[...], 0.0
    )
    dq_ref[...] = dq + spread(spread_matrix(128, 2, 0.5), dq1, 2)
    dk_ref[...] = dk
    dv_ref[...] = dv


def final_kernel(dq_ref, dk_ref, dv_ref, kv1_ref, recv_ref, q_out, k_out, v_out):
    low = low_lanes(64)
    low32 = low_lanes(32)
    two = spread_matrix(128, 2, 0.5)
    four = spread_matrix(64, 4, 0.25)

    def step(p, carry):
        cols = pl.ds(pl.multiple_of(p * LANES, LANES), LANES)
        a = recv_ref[2 * p].astype(F32)
        b = recv_ref[2 * p + 1].astype(F32)
        ar, br = swap_halves(a), swap_halves(b)
        g2k = jnp.where(low, a[0:64], br[0:64]).astype(BF16)
        g2v = jnp.where(low, ar[0:64], b[0:64]).astype(BF16)
        g2q = jnp.concatenate(
            [
                jnp.where(low32, a[64:96], br[64:96]),
                jnp.where(low32, ar[64:96], b[64:96]),
            ],
            axis=0,
        ).astype(BF16)
        q_out[:, cols] = (dq_ref[:, cols] + dot(four, g2q)).astype(BF16)
        k_out[:, cols] = (
            dk_ref[:, cols] + dot(two, kv1_ref[0:B, cols]) + dot(four, g2k)
        ).astype(BF16)
        v_out[:, cols] = (
            dv_ref[:, cols] + dot(two, kv1_ref[B : 2 * B, cols]) + dot(four, g2v)
        ).astype(BF16)
        return carry

    lax.fori_loop(0, PAIRS, step, 0)


def pairs_of(mask, size):
    return [(source, source ^ mask) for source in range(size)]


def per_device(q, k, v, grad):
    size = lax.axis_size("seq")
    groups = [[RING * g + i for i in range(RING)] for g in range(size // RING)]
    position = lax.axis_index("seq")
    rows, width = q.shape

    def exchange(x):
        return lax.all_to_all(x, "seq", 0, 0, axis_index_groups=groups, tiled=True)

    def swapped(x, mask):
        return lax.ppermute(x, "seq", pairs_of(mask, size))

    def flag(bit):
        return (position // (RING << bit) % 2).astype(jnp.int32).reshape(1)

    q1, kv1, send1 = call(
        pool_kernel,
        [((B, width), BF16), ((2 * B, width), BF16), ((RING, 96, LANES), BF16)],
        (q, k, v),
    )
    kv1s = swapped(kv1, 1)
    recv1 = exchange(send1)
    qh, kvh, block = call(
        prepare_kernel,
        [((STACK, LANES), BF16), ((STACK, LANES), BF16), ((B, LANES), BF16)],
        (recv1,),
    )
    siblings = []
    for bit in range(4):
        other = swapped(block, RING << bit)
        siblings.append(other)
        if bit < 3:
            (block,) = call(
                climb_kernel,
                [((B, LANES), BF16)],
                (flag(bit), block, other),
                smem_first=True,
                flops=1e6,
            )

    def tall(n):
        return pl.BlockSpec((n, LANES), lambda p: (0, p))

    second = pl.BlockSpec((B, LANES), lambda p: (1, p))
    params = pltpu.CompilerParams(vmem_limit_bytes=40 * 1024 * 1024)
    full = jax.ShapeDtypeStruct((rows, width), F32)
    att01, lse01 = pl.pallas_call(
        local_forward_kernel,
        grid=(PAIRS,),
        out_shape=[full, full],
        in_specs=[tall(256), tall(256), tall(256), tall(B), tall(B), second],
        out_specs=[tall(256), tall(256)],
        compiler_params=params,
        cost_estimate=pl.CostEstimate(
            flops=4_000_000_000, bytes_accessed=5_000_000, transcendentals=1_500_000
        ),
    )(q, k, v, q1, kv1s, kv1s)
    (send2,) = call(
        head_forward_kernel, [((RING, 64, LANES), BF16)], (qh, kvh, *siblings)
    )
    recv2 = exchange(send2)
    half = (B, width)
    attended, lse, align, r1, g1, f1, send3 = call(
        combine_kernel,
        [
            ((rows, width), BF16),
            ((rows, width), F32),
            ((rows, width), F32),
            (half, F32),
            (half, BF16),
            (half, F32),
            ((RING, 64, LANES), BF16),
        ],
        (att01, lse01, recv2, grad),
        scratch=[pltpu.VMEM((256, LANES), F32)] * 3 + [pltpu.VMEM((B, LANES), F32)] * 3,
    )
    recv3 = exchange(send3)
    tile = ((B, LANES), F32)
    rh, gh, q5, *parts = call(
        head_top_kernel,
        [((STACK, LANES), F32), ((STACK, LANES), F32)] + [tile] * 5,
        (recv3, qh, *siblings),
    )
    kept = jnp.zeros((B, LANES), F32)
    returned = swapped(parts[3].astype(BF16), RING << 3)
    for bit in (2, 1, 0):
        kept, sent = call(
            descend_kernel,
            [tile, ((B, LANES), BF16)],
            (flag(bit), kept, returned, parts[bit]),
            smem_first=True,
            flops=1e6,
        )
        returned = swapped(sent, RING << bit)
    dq, dk, dv, dk1, dv1 = pl.pallas_call(
        local_backward_kernel,
        grid=(PAIRS,),
        out_shape=[full, full, full]
        + [jax.ShapeDtypeStruct(half, BF16), jax.ShapeDtypeStruct(half, BF16)],
        in_specs=[tall(256)] * 6 + [tall(B), tall(B), second] + [tall(B)] * 3,
        out_specs=[tall(256)] * 3 + [tall(B)] * 2,
        compiler_params=params,
        cost_estimate=pl.CostEstimate(
            flops=8_000_000_000, bytes_accessed=9_000_000, transcendentals=1_500_000
        ),
    )(q, k, v, grad, lse, align, q1, kv1s, kv1s, r1, g1, f1)
    back1 = swapped(jnp.concatenate([dk1, dv1]), 1)
    (send4,) = call(
        head_low_kernel,
        [((RING, 96, LANES), BF16)],
        (qh, kvh, rh, gh, q5, kept, returned),
    )
    recv4 = exchange(send4)
    query_grad, key_grad, value_grad = call(
        final_kernel, [((rows, width), BF16)] * 3, (dq, dk, dv, back1, recv4)
    )
    return attended, query_grad, key_grad, value_grad


def solution(mesh):
    return jax.shard_map(
        per_device,
        mesh=mesh,
        in_specs=(P("seq", None),) * 4,
        out_specs=(P("seq", None),) * 4,
        check_vma=False,
    )
```

```python
import functools
import math

import jax
import jax.numpy as jnp
from jax import lax
from jax.experimental import pallas as pl
from jax.experimental.pallas import tpu as pltpu
from jax.sharding import PartitionSpec as P

H = 16
E = 64
B = 128
LANES = 128
PAIRS = 8
RING = 16
LN2 = math.log(2.0)
F32 = jnp.float32
BF16 = jnp.bfloat16

ROWS = {l: 1024 >> (l - 2) for l in range(2, 9)}
FIRST = {2: 0, 3: 1024, 4: 1536, 5: 1792, 6: 1920, 7: 1984, 8: 2016}
STACK = 2048


def dot(a, b):
    return lax.dot_general(a, b, (((1,), (0,)), ((), ())), preferred_element_type=F32)


def dot_nt(a, b):
    return lax.dot_general(a, b, (((1,), (1,)), ((), ())), preferred_element_type=F32)


def dot_tn(a, b):
    return lax.dot_general(a, b, (((0,), (0,)), ((), ())), preferred_element_type=F32)


def lane_of(rows):
    return lax.broadcasted_iota(jnp.int32, (rows, LANES), 1)


def low_lanes(rows):
    return lane_of(rows) < E


def swap_halves(x):
    return pltpu.roll(x, E, 1)


def shift_of(factor):
    return factor.bit_length() - 1


def pool_matrix(rows_out, factor=2):
    r = lax.broadcasted_iota(jnp.int32, (rows_out, rows_out * factor), 0)
    c = lax.broadcasted_iota(jnp.int32, (rows_out, rows_out * factor), 1)
    return jnp.where(c >> shift_of(factor) == r, 1.0 / factor, 0.0).astype(BF16)


def spread_matrix(rows_in, factor, value=1.0):
    r = lax.broadcasted_iota(jnp.int32, (rows_in * factor, rows_in), 0)
    c = lax.broadcasted_iota(jnp.int32, (rows_in * factor, rows_in), 1)
    return jnp.where(r >> shift_of(factor) == c, value, 0.0).astype(BF16)


def pieces(x, count):
    out = []
    for _ in range(count):
        part = x.astype(BF16)
        out.append(part)
        x = x - part.astype(F32)
    return out


def spread(matrix, x, count):
    total = None
    for part in pieces(x, count):
        term = dot(matrix, part)
        total = term if total is None else total + term
    return total


def halved(scratch, x):
    rows = x.shape[0]
    scratch[0:rows, :] = x
    first = scratch[pl.ds(0, rows // 2, stride=2), :]
    second = scratch[pl.ds(1, rows // 2, stride=2), :]
    return ((first + second) * 0.5).astype(BF16)


def repeated(scratch, x, factor):
    rows = x.shape[0]
    for i in range(factor):
        scratch[pl.ds(i, rows, stride=factor), :] = x
    return scratch[0 : rows * factor, :]


def call(kernel, outs, ins, scratch=(), flops=1e8, smem_first=False):
    specs = [pl.BlockSpec(memory_space=pltpu.VMEM) for _ in ins]
    if smem_first:
        specs[0] = pl.BlockSpec(memory_space=pltpu.SMEM)
    return pl.pallas_call(
        kernel,
        out_shape=[jax.ShapeDtypeStruct(s, d) for s, d in outs],
        in_specs=specs,
        out_specs=[pl.BlockSpec(memory_space=pltpu.VMEM) for _ in outs],
        scratch_shapes=list(scratch),
        compiler_params=pltpu.CompilerParams(vmem_limit_bytes=40 * 1024 * 1024),
        cost_estimate=pl.CostEstimate(
            flops=int(flops), bytes_accessed=2_000_000, transcendentals=0
        ),
    )(*ins)


def place(x, diagonal):
    return jnp.sum(jnp.where(diagonal, x, 0.0), axis=0, keepdims=True)


def pool_kernel(q_ref, k_ref, v_ref, q1_ref, kv1_ref, send_ref, one_s, two_s):
    low = low_lanes(64)
    low32 = low_lanes(32)
    level2 = []
    for index, ref in enumerate((q_ref, k_ref, v_ref)):
        one = halved(one_s.at[index], ref[...].astype(F32))
        if index == 0:
            q1_ref[...] = one
        else:
            kv1_ref[index - 1] = one
        level2.append(halved(two_s.at[index], one.astype(F32)).astype(F32))
    q, k, v = level2
    qr, kr, vr = swap_halves(q), swap_halves(k), swap_halves(v)
    send_ref[0, 0:64, :] = jnp.where(low, k, vr).astype(BF16)
    send_ref[1, 0:64, :] = jnp.where(low, kr, v).astype(BF16)
    send_ref[0, 64:96, :] = jnp.where(low32, q[0:32], qr[32:64]).astype(BF16)
    send_ref[1, 64:96, :] = jnp.where(low32, qr[0:32], q[32:64]).astype(BF16)


def sibling_slots(me, level):
    bit = level - 5
    first = ((me >> bit) ^ 1) << bit
    return [first + i for i in range(1 << bit)]


def prepare_kernel(me_ref, recv_ref, q_ref, kv_ref, block_ref, send_ref):
    me = me_ref[0]
    low32 = low_lanes(32)
    for d in range(RING):
        kv_ref[64 * d : 64 * d + 64, :] = recv_ref[d, 0:64, :]
        packed = recv_ref[d, 64:96, :].astype(F32) * 0.125
        q_ref[64 * d : 64 * d + 32, :] = jnp.where(low32, packed, 0.0).astype(BF16)
        q_ref[64 * d + 32 : 64 * d + 64, :] = jnp.where(
            low32, swap_halves(packed), 0.0
        ).astype(BF16)
    for level in range(2, 8):
        rows = ROWS[level]
        step = min(rows, 256)
        matrix = pool_matrix(step // 2)
        for start in range(0, rows, step):
            source = slice(FIRST[level] + start, FIRST[level] + start + step)
            at = FIRST[level + 1] + start // 2
            target = slice(at, at + step // 2)
            q_ref[target, :] = dot(matrix, q_ref[source, :]).astype(BF16)
            kv_ref[target, :] = dot(matrix, kv_ref[source, :]).astype(BF16)
    end = FIRST[8] + ROWS[8]
    q_ref[end:STACK, :] = jnp.zeros((STACK - end, LANES), BF16)
    kv_ref[end:STACK, :] = jnp.zeros((STACK - end, LANES), BF16)
    block_ref[...] = kv_ref[FIRST[5] : FIRST[5] + B, :]
    send_ref[...] = jnp.zeros_like(send_ref)
    for level in range(6, 9):
        rows = ROWS[level]
        block = kv_ref[FIRST[level] : FIRST[level] + rows, :]
        for slot in sibling_slots(me, level):
            send_ref[slot, 0:rows, :] = block


def two_heads_forward(q, k, v, bias):
    rows = q.shape[0]
    low_q = low_lanes(rows)
    low_v = low_lanes(v.shape[0])
    scaled = q.astype(F32) * 0.125
    values = v.astype(F32)
    tops = []
    sums = []
    for j in range(2):
        mine_q = low_q if j == 0 else jnp.logical_not(low_q)
        mine_v = low_v if j == 0 else jnp.logical_not(low_v)
        s = dot_nt(jnp.where(mine_q, scaled, 0.0).astype(BF16), k)
        top = jnp.max(s, axis=1, keepdims=True)
        raised = jnp.exp(s - top)
        sums.append(dot(raised.astype(BF16), jnp.where(mine_v, values, 1.0).astype(BF16)))
        tops.append(top)
    weighted = jnp.where(low_q, sums[0], sums[1])
    total = swap_halves(jnp.where(low_q, sums[1], sums[0]))
    top = jnp.where(low_q, tops[0], tops[1])
    return weighted / total, top + jnp.log(total) + bias


def own_forward_kernel(q_ref, k_ref, v_ref, att_ref, lse_ref):
    att_ref[...], lse_ref[...] = two_heads_forward(q_ref[...], k_ref[...], v_ref[...], 0.0)


def core_forward_kernel(q_ref, kv_ref, att_ref, lse_ref):
    att_ref[...], lse_ref[...] = two_heads_forward(q_ref[...], kv_ref[0], kv_ref[1], LN2)


def attend(q, kv, level):
    s = dot_nt(q, kv)
    top = jnp.max(s, axis=1, keepdims=True)
    raised = jnp.exp(s - top)
    ones = jnp.where(low_lanes(B), 1.0, kv.astype(F32)).astype(BF16)
    tops = jnp.broadcast_to(top + level * LN2, (q.shape[0], LANES))
    return tops, dot(raised.astype(BF16), ones)


def join(top_a, sum_a, top_b, sum_b):
    high = jnp.maximum(top_a, top_b)
    return high, jnp.exp(top_a - high) * sum_a + jnp.exp(top_b - high) * sum_b


def head_forward_kernel(q_ref, kv_ref, top_ref, sum_ref):
    tops, sums = None, None
    double = spread_matrix(64, 2)
    for level in (4, 3, 2):
        new_tops, new_sums = [], []
        for block in range(ROWS[level] // B):
            at = FIRST[level] + B * block
            beside = FIRST[level] + B * (block ^ 1)
            top, total = attend(q_ref[at : at + B, :], kv_ref[beside : beside + B, :], level)
            if tops is not None:
                half = slice(64 * (block % 2), 64 * (block % 2) + 64)
                up_top = spread(double, tops[block // 2][half], 3)
                up_sum = spread(double, sums[block // 2][half], 2)
                top, total = join(top, total, up_top, up_sum)
            new_sums.append(total)
            new_tops.append(top)
        tops, sums = new_tops, new_sums
    for block in range(8):
        top_ref[B * block : B * block + B, :] = tops[block]
        sum_ref[B * block : B * block + B, :] = sums[block]


def head_merge_kernel(
    me_ref, beside_ref, recv_ref, q_ref, top_ref, sum_ref, send_ref, sibling_ref
):
    me = me_ref[0]
    sibling_ref[0] = beside_ref[...]
    tops, sums = None, None
    for level in (8, 7, 6, 5):
        rows = ROWS[level]
        for index, slot in enumerate(sibling_slots(me, level) if level > 5 else ()):
            sibling_ref[level - 5, rows * index : rows * index + rows, :] = recv_ref[
                slot, 0:rows, :
            ]
        top, total = attend(
            q_ref[FIRST[level] : FIRST[level] + rows, :], sibling_ref[level - 5], level
        )
        if tops is not None:
            double = spread_matrix(rows // 2, 2)
            top, total = join(top, total, spread(double, tops, 3), spread(double, sums, 2))
        tops, sums = top, total
    low = low_lanes(64)
    low32 = low_lanes(32)
    row64 = lax.broadcasted_iota(jnp.int32, (64, LANES), 0)
    diagonal = row64 == lane_of(64)
    eight = spread_matrix(8, 8)
    tail = jnp.zeros((13, LANES), F32)
    for d in range(RING):
        at = slice(64 * d, 64 * d + 64)
        up = slice(8 * d, 8 * d + 8)
        high, total = join(
            top_ref[at, :],
            sum_ref[at, :],
            spread(eight, tops[up], 3),
            spread(eight, sums[up], 2),
        )
        moved = swap_halves(total)
        count = jnp.where(low, total, moved)
        att = total / count
        lse = high + jnp.log(count)
        send_ref[d, 0:32, :] = jnp.where(low32, swap_halves(att)[0:32], att[32:64]).astype(BF16)
        line = place(lse, diagonal)
        parts = [part.astype(F32) for part in pieces(line, 3)]
        send_ref[d, 32:48, :] = jnp.concatenate(parts + [tail], axis=0).astype(BF16)


def combine_kernel(
    att0_ref, lse0_ref, att1_ref, lse1_ref, recv_ref, grad_ref,
    out_ref, full_ref, align_ref, r1_ref, g1_ref, f1_ref, send_ref,
    lse_s, grad_s, align_s, r_s, g_s, f_s, att_s, up_s, att2_s,
):
    low = low_lanes(256)
    low64 = low_lanes(64)
    low32 = low_lanes(32)
    r = lax.broadcasted_iota(jnp.int32, (LANES, LANES), 0)
    c = lax.broadcasted_iota(jnp.int32, (LANES, LANES), 1)
    per_head = jnp.where(r >> 6 == c >> 6, 1.0, 0.0).astype(BF16)
    own = lax.broadcasted_iota(jnp.int32, (256, LANES), 0) >> 2 == lane_of(256)

    packed_a = recv_ref[0].astype(F32)
    packed_b = recv_ref[1].astype(F32)
    rows_a, rows_b = packed_a[0:32], packed_b[0:32]
    att2 = jnp.concatenate(
        [
            jnp.where(low32, rows_a, swap_halves(rows_b)),
            jnp.where(low32, swap_halves(rows_a), rows_b),
        ],
        axis=0,
    )
    att2 = repeated(att2_s, att2, 4)
    columns = []
    for packed in (packed_a, packed_b):
        line = packed[32:33] + packed[33:34] + packed[34:35]
        columns.append(jnp.sum(jnp.where(own, line, 0.0), axis=1, keepdims=True))
    lse2 = jnp.where(low, columns[0], columns[1])
    lse0 = lse0_ref[...]
    lse1 = repeated(up_s, lse1_ref[...], 2)
    att1 = repeated(att_s, att1_ref[...], 2)
    high = jnp.maximum(jnp.maximum(lse0, lse1), lse2)
    e0 = jnp.exp(lse0 - high)
    e1 = jnp.exp(lse1 - high)
    e2 = jnp.exp(lse2 - high)
    den = e0 + e1 + e2
    attended = ((e0 * att0_ref[...] + e1 * att1 + e2 * att2) / den).astype(BF16)
    out_ref[...] = attended
    full = high + jnp.log(den)
    grad = grad_ref[...].astype(F32)
    product = grad * attended.astype(F32)
    align = None
    for part in pieces(product, 3):
        term = dot(part, per_head)
        align = term if align is None else align + term
    full_ref[...] = full
    align_ref[...] = align
    lse_s[...] = full
    grad_s[...] = grad
    align_s[...] = align

    def fold(lse, grads, aligns, rows):
        a, b = pl.ds(0, rows, stride=2), pl.ds(1, rows, stride=2)
        la, lb = lse[a, :], lse[b, :]
        least = jnp.minimum(la, lb)
        ea, eb = jnp.exp(least - la), jnp.exp(least - lb)
        return (
            least,
            ea * grads[a, :] + eb * grads[b, :],
            ea * aligns[a, :] + eb * aligns[b, :],
        )

    r1, g1, f1 = fold(lse_s, grad_s, align_s, 128)
    r1_ref[...] = r1
    g1_ref[...] = g1.astype(BF16)
    f1_ref[...] = f1
    r_s[...] = r1
    g_s[...] = g1
    f_s[...] = f1
    r2, g2, f2 = fold(r_s, g_s, f_s, 64)
    row64 = lax.broadcasted_iota(jnp.int32, (64, LANES), 0)
    diagonal = row64 == (lane_of(64) & (E - 1))
    line_r = place(r2, diagonal)
    line_f = place(f2, diagonal)
    low1 = low_lanes(1)
    wide_r = jnp.broadcast_to(line_r, (8, LANES))
    wide_f = jnp.broadcast_to(line_f, (8, LANES))
    lines = (
        jnp.where(low1, line_r, swap_halves(wide_f)[0:1]),
        jnp.where(low1, swap_halves(wide_r)[0:1], line_f),
    )
    moved = swap_halves(g2)
    tail = jnp.zeros((13, LANES), F32)
    send_ref[0, 0:32, :] = jnp.where(low32, g2[0:32], moved[32:64]).astype(BF16)
    send_ref[1, 0:32, :] = jnp.where(low32, moved[0:32], g2[32:64]).astype(BF16)
    for j in range(2):
        parts = [part.astype(F32) for part in pieces(lines[j], 3)]
        send_ref[j, 32:48, :] = jnp.concatenate(parts + [tail], axis=0).astype(BF16)


def level_backward(q, kv, least, grads, level):
    rows = q.shape[0]
    low = low_lanes(rows)
    s = dot_nt(q, kv)
    weight = jnp.exp(s + (level * LN2 - least[:, 0:1]))
    cograd = jnp.where(low, 0.0, grads).astype(BF16)
    slope = (weight * (dot_nt(cograd, kv) - grads[:, 0:1])).astype(BF16)
    query_part = dot(slope, kv) * 0.125
    other_part = dot_tn(slope, q) + dot_tn(weight.astype(BF16), cograd)
    return query_part, other_part


def head_top_kernel(
    me_ref, recv_ref, q_ref, sibling_ref, r_ref, g_ref, q5_ref, beside_ref, send_ref
):
    me = me_ref[0]
    low = low_lanes(64)
    row64 = lax.broadcasted_iota(jnp.int32, (64, LANES), 0)
    first = row64 == lane_of(64)
    second = row64 + E == lane_of(64)
    for d in range(RING):
        packed = recv_ref[d].astype(F32)
        line = packed[32:33] + packed[33:34] + packed[34:35]
        least = jnp.sum(jnp.where(first, line, 0.0), axis=1, keepdims=True)
        flow = jnp.sum(jnp.where(second, line, 0.0), axis=1, keepdims=True)
        grads = jnp.concatenate([swap_halves(packed[0:32]), packed[0:32]], axis=0)
        r_ref[64 * d : 64 * d + 64, :] = jnp.broadcast_to(least, (64, LANES))
        g_ref[64 * d : 64 * d + 64, :] = jnp.where(low, flow, grads)
    for level in range(2, 8):
        rows = ROWS[level + 1]
        a = pl.ds(FIRST[level], rows, stride=2)
        b = pl.ds(FIRST[level] + 1, rows, stride=2)
        la, lb = r_ref[a, :], r_ref[b, :]
        least = jnp.minimum(la, lb)
        to = slice(FIRST[level + 1], FIRST[level + 1] + rows)
        r_ref[to, :] = least
        g_ref[to, :] = jnp.exp(least - la) * g_ref[a, :] + jnp.exp(least - lb) * g_ref[b, :]
    end = FIRST[8] + ROWS[8]
    r_ref[end:STACK, :] = jnp.zeros((STACK - end, LANES), F32)
    g_ref[end:STACK, :] = jnp.zeros((STACK - end, LANES), F32)
    send_ref[...] = jnp.zeros_like(send_ref)
    running = None
    for level in (8, 7, 6, 5):
        rows = ROWS[level]
        at = slice(FIRST[level], FIRST[level] + rows)
        query_part, other_part = level_backward(
            q_ref[at, :], sibling_ref[level - 5], r_ref[at, :], g_ref[at, :], level
        )
        other_part = other_part.astype(BF16)
        if level == 5:
            beside_ref[...] = other_part
        for index, slot in enumerate(sibling_slots(me, level) if level > 5 else ()):
            send_ref[slot, 0:rows, :] = other_part[rows * index : rows * index + rows]
        if running is None:
            running = query_part
        else:
            running = query_part + spread(spread_matrix(rows // 2, 2, 0.5), running, 2)
    q5_ref[...] = running


def head_low_kernel(q_ref, kv_ref, r_ref, g_ref, q5_ref, query_ref, other_ref):
    double = spread_matrix(64, 2, 0.5)
    query_up = [q5_ref[...]]
    other_up = None
    for level in (4, 3, 2):
        blocks = ROWS[level] // B
        query_parts = [None] * blocks
        other_parts = [None] * blocks
        for block in range(blocks):
            at = FIRST[level] + B * block
            beside = FIRST[level] + B * (block ^ 1)
            query_part, other_part = level_backward(
                q_ref[at : at + B, :],
                kv_ref[beside : beside + B, :],
                r_ref[at : at + B, :],
                g_ref[at : at + B, :],
                level,
            )
            query_parts[block] = query_part
            other_parts[block ^ 1] = other_part
        for block in range(blocks):
            half = slice(64 * (block % 2), 64 * (block % 2) + 64)
            query_parts[block] = query_parts[block] + spread(
                double, query_up[block // 2][half], 2
            )
            if other_up is not None:
                other_parts[block] = other_parts[block] + spread(
                    double, other_up[block // 2][half], 2
                )
        query_up, other_up = query_parts, other_parts
    for block in range(8):
        query_ref[B * block : B * block + B, :] = query_up[block]
        other_ref[B * block : B * block + B, :] = other_up[block]


def head_last_kernel(me_ref, beside_ref, recv_ref, query_ref, other_ref, send_ref):
    me = me_ref[0]
    running = None
    for level in (8, 7, 6):
        rows = ROWS[level]
        total = None
        for slot in sibling_slots(me, level):
            term = recv_ref[slot, 0:rows, :].astype(F32)
            total = term if total is None else total + term
        if running is not None:
            total = total + spread(spread_matrix(rows // 2, 2, 0.5), running, 2)
        running = total
    running = beside_ref[...].astype(F32) + spread(spread_matrix(64, 2, 0.5), running, 2)
    eight = spread_matrix(8, 8, 0.125)
    low32 = low_lanes(32)
    for d in range(RING):
        at = slice(64 * d, 64 * d + 64)
        other = other_ref[at, :] + spread(eight, running[8 * d : 8 * d + 8], 2)
        query = query_ref[at, :]
        send_ref[d, 0:64, :] = other.astype(BF16)
        send_ref[d, 64:96, :] = jnp.where(
            low32, query[0:32], swap_halves(query)[32:64]
        ).astype(BF16)


def two_heads_backward(q, k, v, grads, lse, align, bias):
    rows = q.shape[0]
    low_q = low_lanes(rows)
    low_k = low_lanes(k.shape[0])
    scaled = q.astype(F32) * 0.125
    wide = grads.astype(F32)
    scaled_b = scaled.astype(BF16)
    results = []
    for j in range(2):
        mine = low_q if j == 0 else jnp.logical_not(low_q)
        s = dot_nt(jnp.where(mine, scaled, 0.0).astype(BF16), k)
        weight = jnp.exp(s + (bias - lse[:, E * j : E * j + 1]))
        through = dot_nt(jnp.where(mine, wide, 0.0).astype(BF16), v)
        slope = (weight * (through - align[:, E * j : E * j + 1])).astype(BF16)
        results.append(
            (dot(slope, k), dot_tn(slope, scaled_b), dot_tn(weight.astype(BF16), grads))
        )
    return (
        jnp.where(low_q, results[0][0], results[1][0]) * 0.125,
        jnp.where(low_k, results[0][1], results[1][1]),
        jnp.where(low_k, results[0][2], results[1][2]),
    )


def own_backward_kernel(
    q_ref, k_ref, v_ref, grad_ref, lse_ref, align_ref, dq_ref, dk_ref, dv_ref
):
    dq_ref[...], dk_ref[...], dv_ref[...] = two_heads_backward(
        q_ref[...], k_ref[...], v_ref[...], grad_ref[...], lse_ref[...], align_ref[...], 0.0
    )


def core_backward_kernel(q_ref, kv_ref, r_ref, g_ref, f_ref, dq_ref, dkv_ref):
    dq, dk, dv = two_heads_backward(
        q_ref[...], kv_ref[0], kv_ref[1], g_ref[...], r_ref[...], f_ref[...], LN2
    )
    dq_ref[...] = dq
    dkv_ref[0] = dk.astype(BF16)
    dkv_ref[1] = dv.astype(BF16)


def final_kernel(
    dq_ref, dk_ref, dv_ref, dq1_ref, kv1_ref, recv_ref, q_out, k_out, v_out, half_s, full_s
):
    low = low_lanes(64)
    low32 = low_lanes(32)
    a = recv_ref[0].astype(F32)
    b = recv_ref[1].astype(F32)
    ar, br = swap_halves(a), swap_halves(b)
    g2k = jnp.where(low, a[0:64], br[0:64])
    g2v = jnp.where(low, ar[0:64], b[0:64])
    g2q = jnp.concatenate(
        [
            jnp.where(low32, a[64:96], br[64:96]),
            jnp.where(low32, ar[64:96], b[64:96]),
        ],
        axis=0,
    )
    work = (
        (dq_ref, dq1_ref[...], g2q, q_out),
        (dk_ref, kv1_ref[0].astype(F32), g2k, k_out),
        (dv_ref, kv1_ref[1].astype(F32), g2v, v_out),
    )
    for index, (own, one, two, out) in enumerate(work):
        one = one + repeated(half_s.at[index], two * 0.5, 2)
        out[...] = (own[...] + repeated(full_s.at[index], one * 0.5, 2)).astype(BF16)


def pairs_of(mask, size):
    return [(source, source ^ mask) for source in range(size)]


class Tall:
    def __init__(self, rows):
        self.rows = rows

    def spec(self, step):
        return pl.BlockSpec((self.rows, LANES * step), lambda p: (0, p))

    def view(self, ref, i):
        return ref.at[:, LANES * i : LANES * (i + 1)]


class TwoTall(Tall):
    def spec(self, step):
        return pl.BlockSpec((2, self.rows, LANES * step), lambda p: (0, 0, p))

    def view(self, ref, i):
        return ref.at[:, :, LANES * i : LANES * (i + 1)]


class Slots(Tall):
    def spec(self, step):
        return pl.BlockSpec((2 * step, self.rows, LANES), lambda p: (p, 0, 0))

    def view(self, ref, i):
        return ref.at[2 * i : 2 * i + 2]


def over_pairs(
    kernel, outs, out_kinds, ins, in_kinds, scratch=(), step=2, flops=1e9, moved=5e6
):
    kinds = in_kinds + out_kinds

    def body(*refs):
        for i in range(step):
            views = [kind.view(ref, i) for kind, ref in zip(kinds, refs)]
            kernel(*views, *[ref.at[i] for ref in refs[len(kinds) :]])

    return pl.pallas_call(
        body,
        grid=(PAIRS // step,),
        out_shape=[jax.ShapeDtypeStruct(s, d) for s, d in outs],
        in_specs=[kind.spec(step) for kind in in_kinds],
        out_specs=[kind.spec(step) for kind in out_kinds],
        scratch_shapes=[pltpu.VMEM((step,) + shape + (LANES,), F32) for shape in scratch],
        compiler_params=pltpu.CompilerParams(vmem_limit_bytes=58 * 1024 * 1024),
        cost_estimate=pl.CostEstimate(
            flops=int(flops), bytes_accessed=int(moved), transcendentals=0
        ),
    )(*ins)


STEPS = {"pool": 4, "local_forward": 2, "combine": 4, "local_backward": 2, "final": 4}


def per_device(q, k, v, grad):
    size = lax.axis_size("seq")
    planes = size // RING
    rings = [[RING * g + i for i in range(RING)] for g in range(planes)]
    columns = [[RING * g + i for g in range(planes)] for i in range(RING)]
    me = (lax.axis_index("seq") // RING).astype(jnp.int32).reshape(1)
    rows, width = q.shape

    def exchange(x, groups):
        return lax.all_to_all(x, "seq", 0, 0, axis_index_groups=groups, tiled=True)

    def swapped(x, mask):
        return lax.ppermute(x, "seq", pairs_of(mask, size))

    q1, kv1, send1 = over_pairs(
        pool_kernel,
        [((B, width), BF16), ((2, B, width), BF16), ((RING, 96, LANES), BF16)],
        [Tall(B), TwoTall(B), Slots(96)],
        (q, k, v),
        [Tall(rows)] * 3,
        scratch=((3, 256), (3, B)),
        step=STEPS["pool"],
    )
    kv1s = swapped(kv1, 1)
    recv1 = exchange(send1, rings)
    full = ((rows, width), F32)
    att0, lse0 = over_pairs(
        own_forward_kernel,
        [full, full],
        [Tall(rows)] * 2,
        (q, k, v),
        [Tall(rows)] * 3,
        step=STEPS["local_forward"],
        flops=6e9,
        moved=1e7,
    )
    recv1, att0 = lax.optimization_barrier((recv1, att0))
    qh, kvh, block, sendx = call(
        prepare_kernel,
        [((STACK, LANES), BF16)] * 2 + [((B, LANES), BF16), ((RING, 64, LANES), BF16)],
        (me, recv1),
        smem_first=True,
    )
    beside = swapped(block, RING)
    recvx = exchange(sendx, columns)
    half = (B, width)
    att1, lse1 = over_pairs(
        core_forward_kernel,
        [(half, F32)] * 2,
        [Tall(B)] * 2,
        (q1, kv1s),
        [Tall(B), TwoTall(B)],
        step=STEPS["local_forward"],
        flops=2e9,
    )
    tops, sums = call(
        head_forward_kernel, [((1024, LANES), F32)] * 2, (qh, kvh), flops=1e9
    )
    recvx, att1 = lax.optimization_barrier((recvx, att1))
    send2, siblings = call(
        head_merge_kernel,
        [((RING, 48, LANES), BF16), ((4, B, LANES), BF16)],
        (me, beside, recvx, qh, tops, sums),
        smem_first=True,
    )
    recv2 = exchange(send2, rings)
    attended, lse, align, r1, g1, f1, send3 = over_pairs(
        combine_kernel,
        [
            ((rows, width), BF16),
            full,
            full,
            (half, F32),
            (half, BF16),
            (half, F32),
            ((RING, 48, LANES), BF16),
        ],
        [Tall(rows)] * 3 + [Tall(B)] * 3 + [Slots(48)],
        (att0, lse0, att1, lse1, recv2, grad),
        [Tall(rows)] * 2 + [Tall(B)] * 2 + [Slots(48), Tall(rows)],
        scratch=((256,),) * 3 + ((B,),) * 3 + ((256,),) * 3,
        step=STEPS["combine"],
    )
    recv3 = exchange(send3, rings)
    dq1, dkv1 = over_pairs(
        core_backward_kernel,
        [(half, F32), ((2, B, width), BF16)],
        [Tall(B), TwoTall(B)],
        (q1, kv1s, r1, g1, f1),
        [Tall(B), TwoTall(B)] + [Tall(B)] * 3,
        step=STEPS["local_backward"],
        flops=3e9,
    )
    back1 = swapped(dkv1, 1)
    recv3, dq1 = lax.optimization_barrier((recv3, dq1))
    rh, gh, q5, part5, sendy = call(
        head_top_kernel,
        [((STACK, LANES), F32)] * 2
        + [((B, LANES), F32), ((B, LANES), BF16), ((RING, 64, LANES), BF16)],
        (me, recv3, qh, siblings),
        smem_first=True,
    )
    beside_grad = swapped(part5, RING)
    recvy = exchange(sendy, columns)
    query_low, other_low = call(
        head_low_kernel, [((1024, LANES), F32)] * 2, (qh, kvh, rh, gh, q5), flops=2e9
    )
    (send4,) = call(
        head_last_kernel,
        [((RING, 96, LANES), BF16)],
        (me, beside_grad, recvy, query_low, other_low),
        smem_first=True,
    )
    recv4 = exchange(send4, rings)
    dq, dk, dv = over_pairs(
        own_backward_kernel,
        [full] * 3,
        [Tall(rows)] * 3,
        (q, k, v, grad, lse, align),
        [Tall(rows)] * 6,
        step=STEPS["local_backward"],
        flops=9e9,
        moved=1e7,
    )
    query_grad, key_grad, value_grad = over_pairs(
        final_kernel,
        [((rows, width), BF16)] * 3,
        [Tall(rows)] * 3,
        (dq, dk, dv, dq1, back1, recv4),
        [Tall(rows)] * 3 + [Tall(B), TwoTall(B), Slots(96)],
        scratch=((3, B), (3, 256)),
        step=STEPS["final"],
    )
    return attended, query_grad, key_grad, value_grad


def solution(mesh):
    return jax.shard_map(
        per_device,
        mesh=mesh,
        in_specs=(P("seq", None),) * 4,
        out_specs=(P("seq", None),) * 4,
        check_vma=False,
    )
```

```python
import functools
import math

import jax
import jax.numpy as jnp
from jax import lax
from jax.experimental import pallas as pl
from jax.experimental.pallas import tpu as pltpu
from jax.sharding import PartitionSpec as P

H = 16
E = 64
B = 128
LANES = 128
PAIRS = 8
RING = 16
LN2 = math.log(2.0)
F32 = jnp.float32
BF16 = jnp.bfloat16

ROWS = {l: 1024 >> (l - 2) for l in range(3, 9)}
FIRST = {3: 0, 4: 512, 5: 768, 6: 896, 7: 960, 8: 992}
STACK = 1024


def dot(a, b):
    return lax.dot_general(a, b, (((1,), (0,)), ((), ())), preferred_element_type=F32)


def dot_nt(a, b):
    return lax.dot_general(a, b, (((1,), (1,)), ((), ())), preferred_element_type=F32)


def dot_tn(a, b):
    return lax.dot_general(a, b, (((0,), (0,)), ((), ())), preferred_element_type=F32)


def lane_of(rows):
    return lax.broadcasted_iota(jnp.int32, (rows, LANES), 1)


def low_lanes(rows):
    return lane_of(rows) < E


def swap_halves(x):
    return pltpu.roll(x, E, 1)


def shift_of(factor):
    return factor.bit_length() - 1


def pool_matrix(rows_out, factor=2):
    r = lax.broadcasted_iota(jnp.int32, (rows_out, rows_out * factor), 0)
    c = lax.broadcasted_iota(jnp.int32, (rows_out, rows_out * factor), 1)
    return jnp.where(c >> shift_of(factor) == r, 1.0 / factor, 0.0).astype(BF16)


def spread_matrix(rows_in, factor, value=1.0):
    r = lax.broadcasted_iota(jnp.int32, (rows_in * factor, rows_in), 0)
    c = lax.broadcasted_iota(jnp.int32, (rows_in * factor, rows_in), 1)
    return jnp.where(r >> shift_of(factor) == c, value, 0.0).astype(BF16)


def pieces(x, count):
    out = []
    for _ in range(count):
        part = x.astype(BF16)
        out.append(part)
        x = x - part.astype(F32)
    return out


def spread(matrix, x, count):
    total = None
    for part in pieces(x, count):
        term = dot(matrix, part)
        total = term if total is None else total + term
    return total


def halved(scratch, x):
    rows = x.shape[0]
    scratch[0:rows, :] = x
    first = scratch[pl.ds(0, rows // 2, stride=2), :]
    second = scratch[pl.ds(1, rows // 2, stride=2), :]
    return ((first + second) * 0.5).astype(BF16)


def repeated(scratch, x, factor):
    rows = x.shape[0]
    for i in range(factor):
        scratch[pl.ds(i, rows, stride=factor), :] = x
    return scratch[0 : rows * factor, :]


def call(kernel, outs, ins, scratch=(), flops=1e8, smem_first=False):
    specs = [pl.BlockSpec(memory_space=pltpu.VMEM) for _ in ins]
    if smem_first:
        specs[0] = pl.BlockSpec(memory_space=pltpu.SMEM)
    return pl.pallas_call(
        kernel,
        out_shape=[jax.ShapeDtypeStruct(s, d) for s, d in outs],
        in_specs=specs,
        out_specs=[pl.BlockSpec(memory_space=pltpu.VMEM) for _ in outs],
        scratch_shapes=list(scratch),
        compiler_params=pltpu.CompilerParams(vmem_limit_bytes=40 * 1024 * 1024),
        cost_estimate=pl.CostEstimate(
            flops=int(flops), bytes_accessed=2_000_000, transcendentals=0
        ),
    )(*ins)


def place(x, diagonal):
    return jnp.sum(jnp.where(diagonal, x, 0.0), axis=0, keepdims=True)


def pool_kernel(
    q_ref, k_ref, v_ref, q1_ref, kv1_ref, q2_ref, kv2_ref, send_ref, one_s, two_s, three_s
):
    low = low_lanes(32)
    low16 = low_lanes(16)
    level3 = []
    for index, ref in enumerate((q_ref, k_ref, v_ref)):
        one = halved(one_s.at[index], ref[...].astype(F32))
        two = halved(two_s.at[index], one.astype(F32))
        if index == 0:
            q1_ref[...] = one
            q2_ref[...] = two
        else:
            kv1_ref[index - 1] = one
            kv2_ref[index - 1] = two
        level3.append(halved(three_s.at[index], two.astype(F32)).astype(F32))
    q, k, v = level3
    qr, kr, vr = swap_halves(q), swap_halves(k), swap_halves(v)
    send_ref[0, 0:32, :] = jnp.where(low, k, vr).astype(BF16)
    send_ref[1, 0:32, :] = jnp.where(low, kr, v).astype(BF16)
    send_ref[0, 32:48, :] = jnp.where(low16, q[0:16], qr[16:32]).astype(BF16)
    send_ref[1, 32:48, :] = jnp.where(low16, qr[0:16], q[16:32]).astype(BF16)


def sibling_slots(me, level):
    bit = level - 5
    first = ((me >> bit) ^ 1) << bit
    return [first + i for i in range(1 << bit)]


def prepare_kernel(me_ref, recv_ref, q_ref, kv_ref, block_ref, send_ref):
    me = me_ref[0]
    low16 = low_lanes(16)
    for d in range(RING):
        kv_ref[32 * d : 32 * d + 32, :] = recv_ref[d, 0:32, :]
        packed = recv_ref[d, 32:48, :].astype(F32) * 0.125
        q_ref[32 * d : 32 * d + 16, :] = jnp.where(low16, packed, 0.0).astype(BF16)
        q_ref[32 * d + 16 : 32 * d + 32, :] = jnp.where(
            low16, swap_halves(packed), 0.0
        ).astype(BF16)
    for level in range(3, 8):
        rows = ROWS[level]
        step = min(rows, 256)
        matrix = pool_matrix(step // 2)
        for start in range(0, rows, step):
            source = slice(FIRST[level] + start, FIRST[level] + start + step)
            at = FIRST[level + 1] + start // 2
            target = slice(at, at + step // 2)
            q_ref[target, :] = dot(matrix, q_ref[source, :]).astype(BF16)
            kv_ref[target, :] = dot(matrix, kv_ref[source, :]).astype(BF16)
    end = FIRST[8] + ROWS[8]
    q_ref[end:STACK, :] = jnp.zeros((STACK - end, LANES), BF16)
    kv_ref[end:STACK, :] = jnp.zeros((STACK - end, LANES), BF16)
    block_ref[...] = kv_ref[FIRST[5] : FIRST[5] + B, :]
    send_ref[...] = jnp.zeros_like(send_ref)
    for level in range(6, 9):
        rows = ROWS[level]
        block = kv_ref[FIRST[level] : FIRST[level] + rows, :]
        for slot in sibling_slots(me, level):
            send_ref[slot, 0:rows, :] = block


def heads_forward(pairs, bias):
    heads = []
    for q, k, v in pairs:
        low_q = low_lanes(q.shape[0])
        low_v = low_lanes(v.shape[0])
        scaled = q.astype(F32) * 0.125
        values = v.astype(F32)
        for mine_q, mine_v in (
            (low_q, low_v),
            (jnp.logical_not(low_q), jnp.logical_not(low_v)),
        ):
            heads.append(
                (
                    jnp.where(mine_q, scaled, 0.0).astype(BF16),
                    k,
                    jnp.where(mine_v, values, 1.0).astype(BF16),
                )
            )
    scores = [dot_nt(q, k) for q, k, _ in heads]
    tops = [jnp.max(s, axis=1, keepdims=True) for s in scores]
    raised = [jnp.exp(s - top).astype(BF16) for s, top in zip(scores, tops)]
    sums = [dot(r, head[2]) for r, head in zip(raised, heads)]
    results = []
    for p, (q, _, _) in enumerate(pairs):
        low = low_lanes(q.shape[0])
        weighted = jnp.where(low, sums[2 * p], sums[2 * p + 1])
        total = swap_halves(jnp.where(low, sums[2 * p + 1], sums[2 * p]))
        top = jnp.where(low, tops[2 * p], tops[2 * p + 1])
        results.append((weighted / total, top + jnp.log(total) + bias))
    return results


def own_forward_kernel(steps):
    pairs = [(q[...], k[...], v[...]) for q, k, v, _, _ in steps]
    for views, (att, lse) in zip(steps, heads_forward(pairs, 0.0)):
        views[3][...] = att
        views[4][...] = lse


def core_forward_kernel(steps):
    pairs = [(q[...], kv[0], kv[1]) for q, kv, _, _ in steps]
    for views, (att, lse) in zip(steps, heads_forward(pairs, LN2)):
        views[2][...] = att
        views[3][...] = lse


def ring_pair(kva, kvb):
    return (
        jnp.concatenate([kva[0], kvb[0]], axis=0),
        jnp.concatenate([kva[1], kvb[1]], axis=0),
    )


def ring_forward_kernel(steps):
    pairs = [(q[...],) + ring_pair(kva, kvb) for q, kva, kvb, _, _ in steps]
    for views, (att, lse) in zip(steps, heads_forward(pairs, 2.0 * LN2)):
        views[3][...] = att
        views[4][...] = lse


def attend(q, kv, level):
    s = dot_nt(q, kv)
    top = jnp.max(s, axis=1, keepdims=True)
    raised = jnp.exp(s - top)
    ones = jnp.where(low_lanes(B), 1.0, kv.astype(F32)).astype(BF16)
    tops = jnp.broadcast_to(top + level * LN2, (q.shape[0], LANES))
    return tops, dot(raised.astype(BF16), ones)


def join(top_a, sum_a, top_b, sum_b):
    high = jnp.maximum(top_a, top_b)
    return high, jnp.exp(top_a - high) * sum_a + jnp.exp(top_b - high) * sum_b


def head_forward_kernel(q_ref, kv_ref, top_ref, sum_ref):
    tops, sums = None, None
    double = spread_matrix(64, 2)
    for level in (4, 3):
        new_tops, new_sums = [], []
        for block in range(ROWS[level] // B):
            at = FIRST[level] + B * block
            beside = FIRST[level] + B * (block ^ 1)
            top, total = attend(q_ref[at : at + B, :], kv_ref[beside : beside + B, :], level)
            if tops is not None:
                half = slice(64 * (block % 2), 64 * (block % 2) + 64)
                up_top = spread(double, tops[block // 2][half], 3)
                up_sum = spread(double, sums[block // 2][half], 2)
                top, total = join(top, total, up_top, up_sum)
            new_sums.append(total)
            new_tops.append(top)
        tops, sums = new_tops, new_sums
    for block in range(4):
        top_ref[B * block : B * block + B, :] = tops[block]
        sum_ref[B * block : B * block + B, :] = sums[block]


def head_merge_kernel(
    me_ref, beside_ref, recv_ref, q_ref, top_ref, sum_ref, send_ref, sibling_ref
):
    me = me_ref[0]
    sibling_ref[0] = beside_ref[...]
    levels = (8, 7, 6, 5)
    for level in levels[:3]:
        rows = ROWS[level]
        for index, slot in enumerate(sibling_slots(me, level)):
            sibling_ref[level - 5, rows * index : rows * index + rows, :] = recv_ref[
                slot, 0:rows, :
            ]
    keys = [sibling_ref[level - 5] for level in levels]
    scores = [
        dot_nt(q_ref[FIRST[level] : FIRST[level] + ROWS[level], :], kv)
        for level, kv in zip(levels, keys)
    ]
    highest = [jnp.max(s, axis=1, keepdims=True) for s in scores]
    raised = [jnp.exp(s - top).astype(BF16) for s, top in zip(scores, highest)]
    totals = [
        dot(r, jnp.where(low_lanes(B), 1.0, kv.astype(F32)).astype(BF16))
        for r, kv in zip(raised, keys)
    ]
    tops, sums = None, None
    for level, top, total in zip(levels, highest, totals):
        rows = ROWS[level]
        top = jnp.broadcast_to(top + level * LN2, (rows, LANES))
        if tops is not None:
            double = spread_matrix(rows // 2, 2)
            top, total = join(top, total, spread(double, tops, 3), spread(double, sums, 2))
        tops, sums = top, total
    low = low_lanes(B)
    low16 = low_lanes(16)
    diagonal = lax.broadcasted_iota(jnp.int32, (32, LANES), 0) == lane_of(32)
    four = spread_matrix(32, 4)
    tail = jnp.zeros((13, LANES), F32)
    spreads = [
        (spread(four, tops[32 * i : 32 * i + 32], 3), spread(four, sums[32 * i : 32 * i + 32], 2))
        for i in range(4)
    ]
    for i, (up_top, up_sum) in enumerate(spreads):
        at = slice(B * i, B * i + B)
        high, total = join(top_ref[at, :], sum_ref[at, :], up_top, up_sum)
        count = jnp.where(low, total, swap_halves(total))
        att = total / count
        lse = high + jnp.log(count)
        moved = swap_halves(att)
        for j in range(4):
            d = 4 * i + j
            r = 32 * j
            send_ref[d, 0:16, :] = jnp.where(
                low16, moved[r : r + 16], att[r + 16 : r + 32]
            ).astype(BF16)
            line = place(lse[r : r + 32], diagonal)
            parts = [part.astype(F32) for part in pieces(line, 3)]
            send_ref[d, 16:32, :] = jnp.concatenate(parts + [tail], axis=0).astype(BF16)


def combine_kernel(
    att0_ref, lse0_ref, att1_ref, lse1_ref, att2_ref, lse2_ref, recv_ref, grad_ref,
    out_ref, stat_ref, stat1_ref, g1_ref, stat2_ref, g2_ref, send_ref,
    lse_s, grad_s, align_s, r_s, g_s, f_s, r2_s, g2_s, f2_s, up_s,
):
    low16 = low_lanes(16)
    r = lax.broadcasted_iota(jnp.int32, (LANES, LANES), 0)
    c = lax.broadcasted_iota(jnp.int32, (LANES, LANES), 1)
    per_head = jnp.where(r >> 6 == c >> 6, 1.0, 0.0).astype(BF16)
    own = lax.broadcasted_iota(jnp.int32, (32, LANES), 0) == lane_of(32)

    packed_a = recv_ref[0].astype(F32)
    packed_b = recv_ref[1].astype(F32)
    rows_a, rows_b = packed_a[0:16], packed_b[0:16]
    att3 = jnp.concatenate(
        [
            jnp.where(low16, rows_a, swap_halves(rows_b)),
            jnp.where(low16, swap_halves(rows_a), rows_b),
        ],
        axis=0,
    )
    columns = []
    for packed in (packed_a, packed_b):
        line = packed[16:17] + packed[17:18] + packed[18:19]
        columns.append(jnp.sum(jnp.where(own, line, 0.0), axis=1, keepdims=True))
    lse = jnp.where(low_lanes(32), columns[0], columns[1])
    att = att3
    for index, (att_ref, lse_ref) in enumerate(
        ((att2_ref, lse2_ref), (att1_ref, lse1_ref), (att0_ref, lse0_ref))
    ):
        att = repeated(up_s.at[2 * index], att, 2)
        lse = repeated(up_s.at[2 * index + 1], lse, 2)
        own_lse = lse_ref[...]
        high = jnp.maximum(lse, own_lse)
        e_up = jnp.exp(lse - high)
        e_own = jnp.exp(own_lse - high)
        den = e_up + e_own
        att = (e_up * att + e_own * att_ref[...]) / den
        lse = high + jnp.log(den)
    attended = att.astype(BF16)
    full = lse
    out_ref[...] = attended
    grad = grad_ref[...].astype(F32)
    product = grad * attended.astype(F32)
    align = None
    for part in pieces(product, 3):
        term = dot(part, per_head)
        align = term if align is None else align + term
    stat_ref[...] = jnp.where(lane_of(256) & 32 == 0, full, align)
    lse_s[...] = full
    grad_s[...] = grad
    align_s[...] = align

    def fold(lse, grads, aligns, rows):
        a, b = pl.ds(0, rows, stride=2), pl.ds(1, rows, stride=2)
        la, lb = lse[a, :], lse[b, :]
        least = jnp.minimum(la, lb)
        ea, eb = jnp.exp(least - la), jnp.exp(least - lb)
        return (
            least,
            ea * grads[a, :] + eb * grads[b, :],
            ea * aligns[a, :] + eb * aligns[b, :],
        )

    r1, g1, f1 = fold(lse_s, grad_s, align_s, 128)
    stat1_ref[...] = jnp.where(lane_of(B) & 32 == 0, r1, f1)
    g1_ref[...] = g1.astype(BF16)
    r_s[...] = r1
    g_s[...] = g1
    f_s[...] = f1
    r2, g2, f2 = fold(r_s, g_s, f_s, 64)
    stat2_ref[...] = jnp.where(lane_of(64) & 32 == 0, r2, f2)
    g2_ref[...] = g2.astype(BF16)
    r2_s[...] = r2
    g2_s[...] = g2
    f2_s[...] = f2
    r3, g3, f3 = fold(r2_s, g2_s, f2_s, 32)
    row32 = lax.broadcasted_iota(jnp.int32, (32, LANES), 0)
    diagonal = row32 == (lane_of(32) & (E - 1))
    line_r = place(r3, diagonal)
    line_f = place(f3, diagonal)
    low1 = low_lanes(1)
    wide_r = jnp.broadcast_to(line_r, (8, LANES))
    wide_f = jnp.broadcast_to(line_f, (8, LANES))
    lines = (
        jnp.where(low1, line_r, swap_halves(wide_f)[0:1]),
        jnp.where(low1, swap_halves(wide_r)[0:1], line_f),
    )
    moved = swap_halves(g3)
    tail = jnp.zeros((13, LANES), F32)
    send_ref[0, 0:16, :] = jnp.where(low16, g3[0:16], moved[16:32]).astype(BF16)
    send_ref[1, 0:16, :] = jnp.where(low16, moved[0:16], g3[16:32]).astype(BF16)
    for j in range(2):
        parts = [part.astype(F32) for part in pieces(lines[j], 3)]
        send_ref[j, 16:32, :] = jnp.concatenate(parts + [tail], axis=0).astype(BF16)


def level_backward(q, kv, least, grads, level):
    rows = q.shape[0]
    low = low_lanes(rows)
    s = dot_nt(q, kv)
    weight = jnp.exp(s + (level * LN2 - least[:, 0:1]))
    cograd = jnp.where(low, 0.0, grads).astype(BF16)
    slope = (weight * (dot_nt(cograd, kv) - grads[:, 0:1])).astype(BF16)
    query_part = dot(slope, kv) * 0.125
    other_part = dot_tn(slope, q) + dot_tn(weight.astype(BF16), cograd)
    return query_part, other_part


def unpack_and_fold(recv_ref, r_ref, g_ref, last):
    low = low_lanes(32)
    row32 = lax.broadcasted_iota(jnp.int32, (32, LANES), 0)
    first = row32 == lane_of(32)
    second = row32 + E == lane_of(32)
    for d in range(RING):
        packed = recv_ref[d].astype(F32)
        line = packed[16:17] + packed[17:18] + packed[18:19]
        least = jnp.sum(jnp.where(first, line, 0.0), axis=1, keepdims=True)
        flow = jnp.sum(jnp.where(second, line, 0.0), axis=1, keepdims=True)
        grads = jnp.concatenate([swap_halves(packed[0:16]), packed[0:16]], axis=0)
        r_ref[32 * d : 32 * d + 32, :] = jnp.broadcast_to(least, (32, LANES))
        g_ref[32 * d : 32 * d + 32, :] = jnp.where(low, flow, grads)
    for level in range(3, last):
        rows = ROWS[level + 1]
        a = pl.ds(FIRST[level], rows, stride=2)
        b = pl.ds(FIRST[level] + 1, rows, stride=2)
        la, lb = r_ref[a, :], r_ref[b, :]
        least = jnp.minimum(la, lb)
        to = slice(FIRST[level + 1], FIRST[level + 1] + rows)
        r_ref[to, :] = least
        g_ref[to, :] = jnp.exp(least - la) * g_ref[a, :] + jnp.exp(least - lb) * g_ref[b, :]


def head_top_kernel(
    me_ref, recv_ref, q_ref, sibling_ref, q5_ref, beside_ref, send_ref, r_ref, g_ref
):
    me = me_ref[0]
    unpack_and_fold(recv_ref, r_ref, g_ref, 8)
    send_ref[...] = jnp.zeros_like(send_ref)
    running = None
    for level in (8, 7, 6, 5):
        rows = ROWS[level]
        at = slice(FIRST[level], FIRST[level] + rows)
        query_part, other_part = level_backward(
            q_ref[at, :], sibling_ref[level - 5], r_ref[at, :], g_ref[at, :], level
        )
        other_part = other_part.astype(BF16)
        if level == 5:
            beside_ref[...] = other_part
        for index, slot in enumerate(sibling_slots(me, level) if level > 5 else ()):
            send_ref[slot, 0:rows, :] = other_part[rows * index : rows * index + rows]
        if running is None:
            running = query_part
        else:
            running = query_part + spread(spread_matrix(rows // 2, 2, 0.5), running, 2)
    q5_ref[...] = running


def head_low_kernel(q_ref, kv_ref, recv_ref, q5_ref, query_ref, other_ref, r_ref, g_ref):
    unpack_and_fold(recv_ref, r_ref, g_ref, 4)
    double = spread_matrix(64, 2, 0.5)
    query_up = [q5_ref[...]]
    other_up = None
    for level in (4, 3):
        blocks = ROWS[level] // B
        query_parts = [None] * blocks
        other_parts = [None] * blocks
        for block in range(blocks):
            at = FIRST[level] + B * block
            beside = FIRST[level] + B * (block ^ 1)
            query_part, other_part = level_backward(
                q_ref[at : at + B, :],
                kv_ref[beside : beside + B, :],
                r_ref[at : at + B, :],
                g_ref[at : at + B, :],
                level,
            )
            query_parts[block] = query_part
            other_parts[block ^ 1] = other_part
        for block in range(blocks):
            half = slice(64 * (block % 2), 64 * (block % 2) + 64)
            query_parts[block] = query_parts[block] + spread(
                double, query_up[block // 2][half], 2
            )
            if other_up is not None:
                other_parts[block] = other_parts[block] + spread(
                    double, other_up[block // 2][half], 2
                )
        query_up, other_up = query_parts, other_parts
    for block in range(4):
        query_ref[B * block : B * block + B, :] = query_up[block]
        other_ref[B * block : B * block + B, :] = other_up[block]


def head_last_kernel(me_ref, beside_ref, recv_ref, query_ref, other_ref, send_ref):
    me = me_ref[0]
    running = None
    for level in (8, 7, 6):
        rows = ROWS[level]
        total = None
        for slot in sibling_slots(me, level):
            term = recv_ref[slot, 0:rows, :].astype(F32)
            total = term if total is None else total + term
        if running is not None:
            total = total + spread(spread_matrix(rows // 2, 2, 0.5), running, 2)
        running = total
    running = beside_ref[...].astype(F32) + spread(spread_matrix(64, 2, 0.5), running, 2)
    four = spread_matrix(8, 4, 0.25)
    low16 = low_lanes(16)
    for d in range(RING):
        at = slice(32 * d, 32 * d + 32)
        other = other_ref[at, :] + spread(four, running[8 * d : 8 * d + 8], 2)
        query = query_ref[at, :]
        send_ref[d, 0:32, :] = other.astype(BF16)
        send_ref[d, 32:48, :] = jnp.where(
            low16, query[0:16], swap_halves(query)[16:32]
        ).astype(BF16)


def heads_backward(pairs, bias):
    heads = []
    scaled_pairs = []
    for q, k, v, grads, stat in pairs:
        low_q = low_lanes(q.shape[0])
        scaled = q.astype(F32) * 0.125
        wide = grads.astype(F32)
        scaled_pairs.append(scaled.astype(BF16))
        for j in range(2):
            mine = low_q if j == 0 else jnp.logical_not(low_q)
            heads.append(
                (
                    jnp.where(mine, scaled, 0.0).astype(BF16),
                    k,
                    jnp.where(mine, wide, 0.0).astype(BF16),
                    v,
                    bias - stat[:, E * j : E * j + 1],
                    stat[:, E * j + 32 : E * j + 33],
                )
            )
    scores = [dot_nt(head[0], head[1]) for head in heads]
    through = [dot_nt(head[2], head[3]) for head in heads]
    weights = [jnp.exp(s + head[4]) for s, head in zip(scores, heads)]
    slopes = [
        (w * (t - head[5])).astype(BF16) for w, t, head in zip(weights, through, heads)
    ]
    weights = [w.astype(BF16) for w in weights]
    results = []
    for p, (q, k, _, grads, _) in enumerate(pairs):
        low_q = low_lanes(q.shape[0])
        low_k = low_lanes(k.shape[0])
        one, two = slopes[2 * p : 2 * p + 2]
        results.append(
            (
                jnp.where(low_q, dot(one, k), dot(two, k)) * 0.125,
                jnp.where(
                    low_k, dot_tn(one, scaled_pairs[p]), dot_tn(two, scaled_pairs[p])
                ),
                jnp.where(
                    low_k, dot_tn(weights[2 * p], grads), dot_tn(weights[2 * p + 1], grads)
                ),
            )
        )
    return results


def own_backward_kernel(steps):
    pairs = [tuple(view[...] for view in views[:5]) for views in steps]
    for views, grads in zip(steps, heads_backward(pairs, 0.0)):
        for view, value in zip(views[5:], grads):
            view[...] = value


def core_backward_kernel(steps):
    pairs = [(q[...], kv[0], kv[1], g[...], stat[...]) for q, kv, stat, g, _, _ in steps]
    for views, (dq, dk, dv) in zip(steps, heads_backward(pairs, LN2)):
        views[4][...] = dq
        views[5][0] = dk.astype(BF16)
        views[5][1] = dv.astype(BF16)


def ring_backward_kernel(steps):
    pairs = [
        (views[0][...],) + ring_pair(views[1], views[2]) + (views[4][...], views[3][...])
        for views in steps
    ]
    for views, (dq, dk, dv) in zip(steps, heads_backward(pairs, 2.0 * LN2)):
        views[5][...] = dq
        views[6][0] = dk[0:64]
        views[6][1] = dv[0:64]
        views[7][0] = dk[64:128].astype(BF16)
        views[7][1] = dv[64:128].astype(BF16)


def final_kernel(
    dq_ref, dk_ref, dv_ref, dq1_ref, kv1_ref, dq2_ref, kv2_ref, recv_ref,
    q_out, k_out, v_out, quarter_s, half_s, full_s,
):
    low = low_lanes(32)
    low16 = low_lanes(16)
    a = recv_ref[0].astype(F32)
    b = recv_ref[1].astype(F32)
    ar, br = swap_halves(a), swap_halves(b)
    g3k = jnp.where(low, a[0:32], br[0:32])
    g3v = jnp.where(low, ar[0:32], b[0:32])
    g3q = jnp.concatenate(
        [
            jnp.where(low16, a[32:48], br[32:48]),
            jnp.where(low16, ar[32:48], b[32:48]),
        ],
        axis=0,
    )
    work = (
        (dq_ref, dq1_ref[...], dq2_ref[...], g3q, q_out),
        (dk_ref, kv1_ref[0].astype(F32), kv2_ref[0].astype(F32), g3k, k_out),
        (dv_ref, kv1_ref[1].astype(F32), kv2_ref[1].astype(F32), g3v, v_out),
    )
    for index, (own, one, two, three, out) in enumerate(work):
        two = two + repeated(quarter_s.at[index], three * 0.5, 2)
        one = one + repeated(half_s.at[index], two * 0.5, 2)
        out[...] = (own[...] + repeated(full_s.at[index], one * 0.5, 2)).astype(BF16)


def pairs_of(mask, size):
    return [(source, source ^ mask) for source in range(size)]


class Tall:
    def __init__(self, rows):
        self.rows = rows

    def spec(self, step):
        return pl.BlockSpec((self.rows, LANES * step), lambda p: (0, p))

    def view(self, ref, i):
        return ref.at[:, LANES * i : LANES * (i + 1)]


class TwoTall(Tall):
    def spec(self, step):
        return pl.BlockSpec((2, self.rows, LANES * step), lambda p: (0, 0, p))

    def view(self, ref, i):
        return ref.at[:, :, LANES * i : LANES * (i + 1)]


class Slots(Tall):
    def spec(self, step):
        return pl.BlockSpec((2 * step, self.rows, LANES), lambda p: (p, 0, 0))

    def view(self, ref, i):
        return ref.at[2 * i : 2 * i + 2]


def over_pairs(
    kernel, outs, out_kinds, ins, in_kinds, scratch=(), step=2, flops=1e9, moved=5e6,
    joint=False,
):
    kinds = in_kinds + out_kinds

    def body(*refs):
        if joint:
            kernel([[kind.view(ref, i) for kind, ref in zip(kinds, refs)] for i in range(step)])
            return
        for i in range(step):
            views = [kind.view(ref, i) for kind, ref in zip(kinds, refs)]
            kernel(*views, *[ref.at[i] for ref in refs[len(kinds) :]])

    return pl.pallas_call(
        body,
        grid=(PAIRS // step,),
        out_shape=[jax.ShapeDtypeStruct(s, d) for s, d in outs],
        in_specs=[kind.spec(step) for kind in in_kinds],
        out_specs=[kind.spec(step) for kind in out_kinds],
        scratch_shapes=[pltpu.VMEM((step,) + shape + (LANES,), F32) for shape in scratch],
        compiler_params=pltpu.CompilerParams(vmem_limit_bytes=58 * 1024 * 1024),
        cost_estimate=pl.CostEstimate(
            flops=int(flops), bytes_accessed=int(moved), transcendentals=0
        ),
    )(*ins)


STEPS = {
    "pool": 4,
    "local_forward": 2,
    "combine": 4,
    "local_backward": 2,
    "final": 4,
    "core_forward": 4,
    "core_backward": 4,
}


def per_device(q, k, v, grad):
    size = lax.axis_size("seq")
    planes = size // RING
    rings = [[RING * g + i for i in range(RING)] for g in range(planes)]
    columns = [[RING * g + i for g in range(planes)] for i in range(RING)]
    me = (lax.axis_index("seq") // RING).astype(jnp.int32).reshape(1)
    rows, width = q.shape

    def exchange(x, groups):
        return lax.all_to_all(x, "seq", 0, 0, axis_index_groups=groups, tiled=True)

    def swapped(x, mask):
        return lax.ppermute(x, "seq", pairs_of(mask, size))

    quarter = (rows // 4, width)
    q1, kv1, q2, kv2, send1 = over_pairs(
        pool_kernel,
        [
            ((B, width), BF16),
            ((2, B, width), BF16),
            (quarter, BF16),
            ((2,) + quarter, BF16),
            ((RING, 48, LANES), BF16),
        ],
        [Tall(B), TwoTall(B), Tall(64), TwoTall(64), Slots(48)],
        (q, k, v),
        [Tall(rows)] * 3,
        scratch=((3, 256), (3, B), (3, 64)),
        step=STEPS["pool"],
    )
    kv1s = swapped(kv1, 1)
    recv1 = exchange(send1, rings)
    full = ((rows, width), F32)
    att0, lse0 = over_pairs(
        own_forward_kernel,
        [full, full],
        [Tall(rows)] * 2,
        (q, k, v),
        [Tall(rows)] * 3,
        step=STEPS["local_forward"],
        joint=True,
        flops=6e9,
        moved=1e7,
    )
    recv1, att0 = lax.optimization_barrier((recv1, att0))
    qh, kvh, block, sendx = call(
        prepare_kernel,
        [((STACK, LANES), BF16)] * 2 + [((B, LANES), BF16), ((RING, 64, LANES), BF16)],
        (me, recv1),
        smem_first=True,
    )
    sendx, kv2 = lax.optimization_barrier((sendx, kv2))
    beside = swapped(block, RING)
    kv2a = swapped(kv2, 2)
    kv2b = swapped(kv2a, 1)
    recvx = exchange(sendx, columns)
    half = (B, width)
    att1, lse1 = over_pairs(
        core_forward_kernel,
        [(half, F32)] * 2,
        [Tall(B)] * 2,
        (q1, kv1s),
        [Tall(B), TwoTall(B)],
        step=STEPS["core_forward"],
        joint=True,
        flops=2e9,
    )
    tops, sums = call(
        head_forward_kernel, [((512, LANES), F32)] * 2, (qh, kvh), flops=1e9
    )
    recvx, att1 = lax.optimization_barrier((recvx, att1))
    send2, siblings = call(
        head_merge_kernel,
        [((RING, 32, LANES), BF16), ((4, B, LANES), BF16)],
        (me, beside, recvx, qh, tops, sums),
        smem_first=True,
    )
    send2, q2_later = lax.optimization_barrier((send2, q2))
    recv2 = exchange(send2, rings)
    att2, lse2 = over_pairs(
        ring_forward_kernel,
        [(quarter, F32)] * 2,
        [Tall(64)] * 2,
        (q2_later, kv2a, kv2b),
        [Tall(64), TwoTall(64), TwoTall(64)],
        step=STEPS["core_forward"],
        joint=True,
        flops=2e9,
    )
    attended, stat, stat1, g1, stat2, g2, send3 = over_pairs(
        combine_kernel,
        [
            ((rows, width), BF16),
            full,
            (half, F32),
            (half, BF16),
            (quarter, F32),
            (quarter, BF16),
            ((RING, 32, LANES), BF16),
        ],
        [Tall(rows)] * 2 + [Tall(B)] * 2 + [Tall(64)] * 2 + [Slots(32)],
        (att0, lse0, att1, lse1, att2, lse2, recv2, grad),
        [Tall(rows)] * 2 + [Tall(B)] * 2 + [Tall(64)] * 2 + [Slots(32), Tall(rows)],
        scratch=((256,),) * 3 + ((B,),) * 3 + ((64,),) * 3 + ((6, 256),),
        step=STEPS["combine"],
    )
    recv3 = exchange(send3, rings)
    dq2, same, across = over_pairs(
        ring_backward_kernel,
        [(quarter, F32), ((2,) + quarter, F32), ((2,) + quarter, BF16)],
        [Tall(64), TwoTall(64), TwoTall(64)],
        (q2, kv2a, kv2b, stat2, g2),
        [Tall(64), TwoTall(64), TwoTall(64), Tall(64), Tall(64)],
        step=STEPS["core_backward"],
        joint=True,
        flops=3e9,
    )
    recv3, dq2 = lax.optimization_barrier((recv3, dq2))
    partner = swapped(across, 1)
    back2 = swapped((same + partner.astype(F32)).astype(BF16), 2)
    stack = [pltpu.VMEM((STACK, LANES), F32)] * 2
    q5, part5, sendy = call(
        head_top_kernel,
        [((B, LANES), F32), ((B, LANES), BF16), ((RING, 64, LANES), BF16)],
        (me, recv3, qh, siblings),
        scratch=stack,
        smem_first=True,
    )
    part5, q1_late = lax.optimization_barrier((part5, q1))
    beside_grad = swapped(part5, RING)
    recvy = exchange(sendy, columns)
    query_low, other_low = call(
        head_low_kernel,
        [((512, LANES), F32)] * 2,
        (qh, kvh, recv3, q5),
        scratch=stack,
        flops=2e9,
    )
    dq1, dkv1 = over_pairs(
        core_backward_kernel,
        [(half, F32), ((2, B, width), BF16)],
        [Tall(B), TwoTall(B)],
        (q1_late, kv1s, stat1, g1),
        [Tall(B), TwoTall(B)] + [Tall(B)] * 2,
        step=STEPS["core_backward"],
        joint=True,
        flops=3e9,
    )
    back1 = swapped(dkv1, 1)
    recvy, dq1 = lax.optimization_barrier((recvy, dq1))
    (send4,) = call(
        head_last_kernel,
        [((RING, 48, LANES), BF16)],
        (me, beside_grad, recvy, query_low, other_low),
        smem_first=True,
    )
    recv4 = exchange(send4, rings)
    dq, dk, dv = over_pairs(
        own_backward_kernel,
        [full] * 3,
        [Tall(rows)] * 3,
        (q, k, v, grad, stat),
        [Tall(rows)] * 5,
        step=STEPS["local_backward"],
        joint=True,
        flops=9e9,
        moved=1e7,
    )
    query_grad, key_grad, value_grad = over_pairs(
        final_kernel,
        [((rows, width), BF16)] * 3,
        [Tall(rows)] * 3,
        (dq, dk, dv, dq1, back1, dq2, back2, recv4),
        [Tall(rows)] * 3 + [Tall(B), TwoTall(B), Tall(64), TwoTall(64), Slots(48)],
        scratch=((3, 64), (3, B), (3, 256)),
        step=STEPS["final"],
    )
    return attended, query_grad, key_grad, value_grad


def solution(mesh):
    return jax.shard_map(
        per_device,
        mesh=mesh,
        in_specs=(P("seq", None),) * 4,
        out_specs=(P("seq", None),) * 4,
        check_vma=False,
    )
```

```python
import functools
import math

import jax
import jax.numpy as jnp
from jax import lax
from jax.experimental import pallas as pl
from jax.experimental.pallas import tpu as pltpu
from jax.sharding import PartitionSpec as P

H = 16
E = 64
B = 128
LANES = 128
PAIRS = 8
RING = 16
LN2 = math.log(2.0)
F32 = jnp.float32
BF16 = jnp.bfloat16

ROWS = {l: 1024 >> (l - 2) for l in range(3, 9)}
FIRST = {3: 0, 4: 512, 5: 768, 6: 896, 7: 960, 8: 992}
STACK = 1024


def dot(a, b):
    return lax.dot_general(a, b, (((1,), (0,)), ((), ())), preferred_element_type=F32)


def dot_nt(a, b):
    return lax.dot_general(a, b, (((1,), (1,)), ((), ())), preferred_element_type=F32)


def dot_tn(a, b):
    return lax.dot_general(a, b, (((0,), (0,)), ((), ())), preferred_element_type=F32)


def lane_of(rows):
    return lax.broadcasted_iota(jnp.int32, (rows, LANES), 1)


def low_lanes(rows):
    return lane_of(rows) < E


def swap_halves(x):
    return pltpu.roll(x, E, 1)


def shift_of(factor):
    return factor.bit_length() - 1


def pool_matrix(rows_out, factor=2):
    r = lax.broadcasted_iota(jnp.int32, (rows_out, rows_out * factor), 0)
    c = lax.broadcasted_iota(jnp.int32, (rows_out, rows_out * factor), 1)
    return jnp.where(c >> shift_of(factor) == r, 1.0 / factor, 0.0).astype(BF16)


def spread_matrix(rows_in, factor, value=1.0):
    r = lax.broadcasted_iota(jnp.int32, (rows_in * factor, rows_in), 0)
    c = lax.broadcasted_iota(jnp.int32, (rows_in * factor, rows_in), 1)
    return jnp.where(r >> shift_of(factor) == c, value, 0.0).astype(BF16)


def pieces(x, count):
    out = []
    for _ in range(count):
        part = x.astype(BF16)
        out.append(part)
        x = x - part.astype(F32)
    return out


def spread(matrix, x, count):
    total = None
    for part in pieces(x, count):
        term = dot(matrix, part)
        total = term if total is None else total + term
    return total


def halved(scratch, x):
    rows = x.shape[0]
    scratch[0:rows, :] = x
    first = scratch[pl.ds(0, rows // 2, stride=2), :]
    second = scratch[pl.ds(1, rows // 2, stride=2), :]
    return ((first + second) * 0.5).astype(BF16)


def repeated(scratch, x, factor):
    rows = x.shape[0]
    for i in range(factor):
        scratch[pl.ds(i, rows, stride=factor), :] = x
    return scratch[0 : rows * factor, :]


def call(kernel, outs, ins, scratch=(), flops=1e8, smem_first=False):
    specs = [pl.BlockSpec(memory_space=pltpu.VMEM) for _ in ins]
    if smem_first:
        specs[0] = pl.BlockSpec(memory_space=pltpu.SMEM)
    return pl.pallas_call(
        kernel,
        out_shape=[jax.ShapeDtypeStruct(s, d) for s, d in outs],
        in_specs=specs,
        out_specs=[pl.BlockSpec(memory_space=pltpu.VMEM) for _ in outs],
        scratch_shapes=list(scratch),
        compiler_params=pltpu.CompilerParams(vmem_limit_bytes=40 * 1024 * 1024),
        cost_estimate=pl.CostEstimate(
            flops=int(flops), bytes_accessed=2_000_000, transcendentals=0
        ),
    )(*ins)


def place(x, diagonal):
    return jnp.sum(jnp.where(diagonal, x, 0.0), axis=0, keepdims=True)


def pool_kernel(
    q_ref, k_ref, v_ref, q1_ref, kv1_ref, q2_ref, kv2_ref, send_ref, one_s, two_s, three_s
):
    low = low_lanes(32)
    low16 = low_lanes(16)
    level3 = []
    for index, ref in enumerate((q_ref, k_ref, v_ref)):
        yield
        one = halved(one_s.at[index], ref[...].astype(F32))
        two = halved(two_s.at[index], one.astype(F32))
        if index == 0:
            q1_ref[...] = one
            q2_ref[...] = two
        else:
            kv1_ref[index - 1] = one
            kv2_ref[index - 1] = two
        level3.append(halved(three_s.at[index], two.astype(F32)).astype(F32))
    q, k, v = level3
    qr, kr, vr = swap_halves(q), swap_halves(k), swap_halves(v)
    send_ref[0, 0:32, :] = jnp.where(low, k, vr).astype(BF16)
    send_ref[1, 0:32, :] = jnp.where(low, kr, v).astype(BF16)
    send_ref[0, 32:48, :] = jnp.where(low16, q[0:16], qr[16:32]).astype(BF16)
    send_ref[1, 32:48, :] = jnp.where(low16, qr[0:16], q[16:32]).astype(BF16)


def sibling_slots(me, level):
    bit = level - 5
    first = ((me >> bit) ^ 1) << bit
    return [first + i for i in range(1 << bit)]


def prepare_kernel(me_ref, recv_ref, q_ref, kv_ref, block_ref, send_ref):
    me = me_ref[0]
    low16 = low_lanes(16)
    for d in range(RING):
        kv_ref[32 * d : 32 * d + 32, :] = recv_ref[d, 0:32, :]
        packed = recv_ref[d, 32:48, :].astype(F32) * 0.125
        q_ref[32 * d : 32 * d + 16, :] = jnp.where(low16, packed, 0.0).astype(BF16)
        q_ref[32 * d + 16 : 32 * d + 32, :] = jnp.where(
            low16, swap_halves(packed), 0.0
        ).astype(BF16)
    for level in range(3, 8):
        rows = ROWS[level]
        step = min(rows, 256)
        matrix = pool_matrix(step // 2)
        for start in range(0, rows, step):
            source = slice(FIRST[level] + start, FIRST[level] + start + step)
            at = FIRST[level + 1] + start // 2
            target = slice(at, at + step // 2)
            q_ref[target, :] = dot(matrix, q_ref[source, :]).astype(BF16)
            kv_ref[target, :] = dot(matrix, kv_ref[source, :]).astype(BF16)
    end = FIRST[8] + ROWS[8]
    q_ref[end:STACK, :] = jnp.zeros((STACK - end, LANES), BF16)
    kv_ref[end:STACK, :] = jnp.zeros((STACK - end, LANES), BF16)
    block_ref[...] = kv_ref[FIRST[5] : FIRST[5] + B, :]
    send_ref[...] = jnp.zeros_like(send_ref)
    for level in range(6, 9):
        rows = ROWS[level]
        block = kv_ref[FIRST[level] : FIRST[level] + rows, :]
        for slot in sibling_slots(me, level):
            send_ref[slot, 0:rows, :] = block


def heads_forward(pairs, bias):
    heads = []
    for q, k, v in pairs:
        low_q = low_lanes(q.shape[0])
        low_v = low_lanes(v.shape[0])
        scaled = q.astype(F32) * 0.125
        values = v.astype(F32)
        for mine_q, mine_v in (
            (low_q, low_v),
            (jnp.logical_not(low_q), jnp.logical_not(low_v)),
        ):
            heads.append(
                (
                    jnp.where(mine_q, scaled, 0.0).astype(BF16),
                    k,
                    jnp.where(mine_v, values, 1.0).astype(BF16),
                )
            )
    scores = [dot_nt(q, k) for q, k, _ in heads]
    tops = [jnp.max(s, axis=1, keepdims=True) for s in scores]
    raised = [jnp.exp(s - top).astype(BF16) for s, top in zip(scores, tops)]
    sums = [dot(r, head[2]) for r, head in zip(raised, heads)]
    results = []
    for p, (q, _, _) in enumerate(pairs):
        low = low_lanes(q.shape[0])
        weighted = jnp.where(low, sums[2 * p], sums[2 * p + 1])
        total = swap_halves(jnp.where(low, sums[2 * p + 1], sums[2 * p]))
        top = jnp.where(low, tops[2 * p], tops[2 * p + 1])
        results.append((weighted / total, top + jnp.log(total) + bias))
    return results


def own_forward_kernel(steps):
    pairs = [(q[...], k[...], v[...]) for q, k, v, _, _ in steps]
    for views, (att, lse) in zip(steps, heads_forward(pairs, 0.0)):
        views[3][...] = att.astype(BF16)
        views[4][...] = lse


def core_forward_kernel(steps):
    pairs = [(q[...], kv[0], kv[1]) for q, kv, _, _ in steps]
    for views, (att, lse) in zip(steps, heads_forward(pairs, LN2)):
        views[2][...] = att.astype(BF16)
        views[3][...] = lse


def ring_pair(kva, kvb):
    return (
        jnp.concatenate([kva[0], kvb[0]], axis=0),
        jnp.concatenate([kva[1], kvb[1]], axis=0),
    )


def ring_forward_kernel(steps):
    pairs = [(q[...],) + ring_pair(kva, kvb) for q, kva, kvb, _, _ in steps]
    for views, (att, lse) in zip(steps, heads_forward(pairs, 2.0 * LN2)):
        views[3][...] = att.astype(BF16)
        views[4][...] = lse


def attend(q, kv, level):
    s = dot_nt(q, kv)
    top = jnp.max(s, axis=1, keepdims=True)
    raised = jnp.exp(s - top)
    ones = jnp.where(low_lanes(B), 1.0, kv.astype(F32)).astype(BF16)
    tops = jnp.broadcast_to(top + level * LN2, (q.shape[0], LANES))
    return tops, dot(raised.astype(BF16), ones)


def join(top_a, sum_a, top_b, sum_b):
    high = jnp.maximum(top_a, top_b)
    return high, jnp.exp(top_a - high) * sum_a + jnp.exp(top_b - high) * sum_b


def head_forward_kernel(q_ref, kv_ref, top_ref, sum_ref):
    tops, sums = None, None
    double = spread_matrix(64, 2)
    for level in (4, 3):
        new_tops, new_sums = [], []
        for block in range(ROWS[level] // B):
            at = FIRST[level] + B * block
            beside = FIRST[level] + B * (block ^ 1)
            top, total = attend(q_ref[at : at + B, :], kv_ref[beside : beside + B, :], level)
            if tops is not None:
                half = slice(64 * (block % 2), 64 * (block % 2) + 64)
                up_top = spread(double, tops[block // 2][half], 3)
                up_sum = spread(double, sums[block // 2][half], 2)
                top, total = join(top, total, up_top, up_sum)
            new_sums.append(total)
            new_tops.append(top)
        tops, sums = new_tops, new_sums
    for block in range(4):
        top_ref[B * block : B * block + B, :] = tops[block]
        sum_ref[B * block : B * block + B, :] = sums[block]


def head_merge_kernel(
    me_ref, beside_ref, recv_ref, q_ref, top_ref, sum_ref, send_ref, sibling_ref
):
    me = me_ref[0]
    sibling_ref[0] = beside_ref[...]
    levels = (8, 7, 6, 5)
    for level in levels[:3]:
        rows = ROWS[level]
        for index, slot in enumerate(sibling_slots(me, level)):
            sibling_ref[level - 5, rows * index : rows * index + rows, :] = recv_ref[
                slot, 0:rows, :
            ]
    keys = [sibling_ref[level - 5] for level in levels]
    scores = [
        dot_nt(q_ref[FIRST[level] : FIRST[level] + ROWS[level], :], kv)
        for level, kv in zip(levels, keys)
    ]
    highest = [jnp.max(s, axis=1, keepdims=True) for s in scores]
    raised = [jnp.exp(s - top).astype(BF16) for s, top in zip(scores, highest)]
    totals = [
        dot(r, jnp.where(low_lanes(B), 1.0, kv.astype(F32)).astype(BF16))
        for r, kv in zip(raised, keys)
    ]
    tops, sums = None, None
    for level, top, total in zip(levels, highest, totals):
        rows = ROWS[level]
        top = jnp.broadcast_to(top + level * LN2, (rows, LANES))
        if tops is not None:
            double = spread_matrix(rows // 2, 2)
            top, total = join(top, total, spread(double, tops, 3), spread(double, sums, 2))
        tops, sums = top, total
    low = low_lanes(B)
    low16 = low_lanes(16)
    diagonal = lax.broadcasted_iota(jnp.int32, (32, LANES), 0) == lane_of(32)
    four = spread_matrix(32, 4)
    tail = jnp.zeros((13, LANES), F32)
    spreads = [
        (spread(four, tops[32 * i : 32 * i + 32], 3), spread(four, sums[32 * i : 32 * i + 32], 2))
        for i in range(4)
    ]
    for i, (up_top, up_sum) in enumerate(spreads):
        at = slice(B * i, B * i + B)
        high, total = join(top_ref[at, :], sum_ref[at, :], up_top, up_sum)
        count = jnp.where(low, total, swap_halves(total))
        att = total / count
        lse = high + jnp.log(count)
        moved = swap_halves(att)
        for j in range(4):
            d = 4 * i + j
            r = 32 * j
            send_ref[d, 0:16, :] = jnp.where(
                low16, moved[r : r + 16], att[r + 16 : r + 32]
            ).astype(BF16)
            line = place(lse[r : r + 32], diagonal)
            parts = [part.astype(F32) for part in pieces(line, 3)]
            send_ref[d, 16:32, :] = jnp.concatenate(parts + [tail], axis=0).astype(BF16)


def combine_kernel(
    att0_ref, lse0_ref, att1_ref, lse1_ref, att2_ref, lse2_ref, recv_ref, grad_ref,
    out_ref, stat_ref, stat1_ref, g1_ref, stat2_ref, g2_ref, send_ref,
    lse_s, grad_s, align_s, r_s, g_s, f_s, r2_s, g2_s, f2_s, up_s,
):
    low16 = low_lanes(16)
    r = lax.broadcasted_iota(jnp.int32, (LANES, LANES), 0)
    c = lax.broadcasted_iota(jnp.int32, (LANES, LANES), 1)
    per_head = jnp.where(r >> 6 == c >> 6, 1.0, 0.0).astype(BF16)
    own = lax.broadcasted_iota(jnp.int32, (32, LANES), 0) == lane_of(32)

    packed_a = recv_ref[0].astype(F32)
    packed_b = recv_ref[1].astype(F32)
    rows_a, rows_b = packed_a[0:16], packed_b[0:16]
    att3 = jnp.concatenate(
        [
            jnp.where(low16, rows_a, swap_halves(rows_b)),
            jnp.where(low16, swap_halves(rows_a), rows_b),
        ],
        axis=0,
    )
    columns = []
    for packed in (packed_a, packed_b):
        line = packed[16:17] + packed[17:18] + packed[18:19]
        columns.append(jnp.sum(jnp.where(own, line, 0.0), axis=1, keepdims=True))
    lse = jnp.where(low_lanes(32), columns[0], columns[1])
    att = att3
    yield
    for index, (att_ref, lse_ref) in enumerate(
        ((att2_ref, lse2_ref), (att1_ref, lse1_ref), (att0_ref, lse0_ref))
    ):
        att = repeated(up_s.at[2 * index], att, 2)
        lse = repeated(up_s.at[2 * index + 1], lse, 2)
        own_lse = lse_ref[...]
        high = jnp.maximum(lse, own_lse)
        e_up = jnp.exp(lse - high)
        e_own = jnp.exp(own_lse - high)
        den = e_up + e_own
        att = (e_up * att + e_own * att_ref[...].astype(F32)) / den
        lse = high + jnp.log(den)
        yield
    attended = att.astype(BF16)
    full = lse
    out_ref[...] = attended
    grad = grad_ref[...].astype(F32)
    product = grad * attended.astype(F32)
    align = None
    for part in pieces(product, 2):
        term = dot(part, per_head)
        align = term if align is None else align + term
    yield
    stat_ref[...] = jnp.where(lane_of(256) & 32 == 0, full, align)
    lse_s[...] = full
    grad_s[...] = grad
    align_s[...] = align

    def fold(lse, grads, aligns, rows):
        a, b = pl.ds(0, rows, stride=2), pl.ds(1, rows, stride=2)
        la, lb = lse[a, :], lse[b, :]
        least = jnp.minimum(la, lb)
        ea, eb = jnp.exp(least - la), jnp.exp(least - lb)
        return (
            least,
            ea * grads[a, :] + eb * grads[b, :],
            ea * aligns[a, :] + eb * aligns[b, :],
        )

    r1, g1, f1 = fold(lse_s, grad_s, align_s, 128)
    stat1_ref[...] = jnp.where(lane_of(B) & 32 == 0, r1, f1)
    g1_ref[...] = g1.astype(BF16)
    yield
    r_s[...] = r1
    g_s[...] = g1
    f_s[...] = f1
    r2, g2, f2 = fold(r_s, g_s, f_s, 64)
    stat2_ref[...] = jnp.where(lane_of(64) & 32 == 0, r2, f2)
    g2_ref[...] = g2.astype(BF16)
    yield
    r2_s[...] = r2
    g2_s[...] = g2
    f2_s[...] = f2
    r3, g3, f3 = fold(r2_s, g2_s, f2_s, 32)
    row32 = lax.broadcasted_iota(jnp.int32, (32, LANES), 0)
    diagonal = row32 == (lane_of(32) & (E - 1))
    line_r = place(r3, diagonal)
    line_f = place(f3, diagonal)
    yield
    low1 = low_lanes(1)
    wide_r = jnp.broadcast_to(line_r, (8, LANES))
    wide_f = jnp.broadcast_to(line_f, (8, LANES))
    lines = (
        jnp.where(low1, line_r, swap_halves(wide_f)[0:1]),
        jnp.where(low1, swap_halves(wide_r)[0:1], line_f),
    )
    moved = swap_halves(g3)
    tail = jnp.zeros((13, LANES), F32)
    send_ref[0, 0:16, :] = jnp.where(low16, g3[0:16], moved[16:32]).astype(BF16)
    send_ref[1, 0:16, :] = jnp.where(low16, moved[0:16], g3[16:32]).astype(BF16)
    for j in range(2):
        parts = [part.astype(F32) for part in pieces(lines[j], 3)]
        send_ref[j, 16:32, :] = jnp.concatenate(parts + [tail], axis=0).astype(BF16)


def level_backward(q, kv, least, grads, level):
    rows = q.shape[0]
    low = low_lanes(rows)
    s = dot_nt(q, kv)
    weight = jnp.exp(s + (level * LN2 - least[:, 0:1]))
    cograd = jnp.where(low, 0.0, grads).astype(BF16)
    slope = (weight * (dot_nt(cograd, kv) - grads[:, 0:1])).astype(BF16)
    query_part = dot(slope, kv) * 0.125
    other_part = dot_tn(slope, q) + dot_tn(weight.astype(BF16), cograd)
    return query_part, other_part


def unpack_and_fold(recv_ref, r_ref, g_ref, last):
    low = low_lanes(32)
    row32 = lax.broadcasted_iota(jnp.int32, (32, LANES), 0)
    first = row32 == lane_of(32)
    second = row32 + E == lane_of(32)
    for d in range(RING):
        packed = recv_ref[d].astype(F32)
        line = packed[16:17] + packed[17:18] + packed[18:19]
        least = jnp.sum(jnp.where(first, line, 0.0), axis=1, keepdims=True)
        flow = jnp.sum(jnp.where(second, line, 0.0), axis=1, keepdims=True)
        grads = jnp.concatenate([swap_halves(packed[0:16]), packed[0:16]], axis=0)
        r_ref[32 * d : 32 * d + 32, :] = jnp.broadcast_to(least, (32, LANES))
        g_ref[32 * d : 32 * d + 32, :] = jnp.where(low, flow, grads)
    for level in range(3, last):
        rows = ROWS[level + 1]
        a = pl.ds(FIRST[level], rows, stride=2)
        b = pl.ds(FIRST[level] + 1, rows, stride=2)
        la, lb = r_ref[a, :], r_ref[b, :]
        least = jnp.minimum(la, lb)
        to = slice(FIRST[level + 1], FIRST[level + 1] + rows)
        r_ref[to, :] = least
        g_ref[to, :] = jnp.exp(least - la) * g_ref[a, :] + jnp.exp(least - lb) * g_ref[b, :]


def head_top_kernel(
    me_ref, recv_ref, q_ref, sibling_ref, q5_ref, beside_ref, send_ref, r_ref, g_ref
):
    me = me_ref[0]
    unpack_and_fold(recv_ref, r_ref, g_ref, 8)
    send_ref[...] = jnp.zeros_like(send_ref)
    running = None
    for level in (8, 7, 6, 5):
        rows = ROWS[level]
        at = slice(FIRST[level], FIRST[level] + rows)
        query_part, other_part = level_backward(
            q_ref[at, :], sibling_ref[level - 5], r_ref[at, :], g_ref[at, :], level
        )
        other_part = other_part.astype(BF16)
        if level == 5:
            beside_ref[...] = other_part
        for index, slot in enumerate(sibling_slots(me, level) if level > 5 else ()):
            send_ref[slot, 0:rows, :] = other_part[rows * index : rows * index + rows]
        if running is None:
            running = query_part
        else:
            running = query_part + spread(spread_matrix(rows // 2, 2, 0.5), running, 2)
    q5_ref[...] = running


def head_low_kernel(q_ref, kv_ref, recv_ref, q5_ref, query_ref, other_ref, r_ref, g_ref):
    unpack_and_fold(recv_ref, r_ref, g_ref, 4)
    double = spread_matrix(64, 2, 0.5)
    query_up = [q5_ref[...]]
    other_up = None
    for level in (4, 3):
        blocks = ROWS[level] // B
        query_parts = [None] * blocks
        other_parts = [None] * blocks
        for block in range(blocks):
            at = FIRST[level] + B * block
            beside = FIRST[level] + B * (block ^ 1)
            query_part, other_part = level_backward(
                q_ref[at : at + B, :],
                kv_ref[beside : beside + B, :],
                r_ref[at : at + B, :],
                g_ref[at : at + B, :],
                level,
            )
            query_parts[block] = query_part
            other_parts[block ^ 1] = other_part
        for block in range(blocks):
            half = slice(64 * (block % 2), 64 * (block % 2) + 64)
            query_parts[block] = query_parts[block] + spread(
                double, query_up[block // 2][half], 2
            )
            if other_up is not None:
                other_parts[block] = other_parts[block] + spread(
                    double, other_up[block // 2][half], 2
                )
        query_up, other_up = query_parts, other_parts
    for block in range(4):
        query_ref[B * block : B * block + B, :] = query_up[block]
        other_ref[B * block : B * block + B, :] = other_up[block]


def head_last_kernel(me_ref, beside_ref, recv_ref, query_ref, other_ref, send_ref):
    me = me_ref[0]
    running = None
    for level in (8, 7, 6):
        rows = ROWS[level]
        total = None
        for slot in sibling_slots(me, level):
            term = recv_ref[slot, 0:rows, :].astype(F32)
            total = term if total is None else total + term
        if running is not None:
            total = total + spread(spread_matrix(rows // 2, 2, 0.5), running, 2)
        running = total
    running = beside_ref[...].astype(F32) + spread(spread_matrix(64, 2, 0.5), running, 2)
    four = spread_matrix(8, 4, 0.25)
    low16 = low_lanes(16)
    for d in range(RING):
        at = slice(32 * d, 32 * d + 32)
        other = other_ref[at, :] + spread(four, running[8 * d : 8 * d + 8], 2)
        query = query_ref[at, :]
        send_ref[d, 0:32, :] = other.astype(BF16)
        send_ref[d, 32:48, :] = jnp.where(
            low16, query[0:16], swap_halves(query)[16:32]
        ).astype(BF16)


def heads_backward(pairs, bias):
    heads = []
    scaled_pairs = []
    for q, k, v, grads, stat in pairs:
        low_q = low_lanes(q.shape[0])
        scaled = q.astype(F32) * 0.125
        wide = grads.astype(F32)
        scaled_pairs.append(scaled.astype(BF16))
        for j in range(2):
            mine = low_q if j == 0 else jnp.logical_not(low_q)
            heads.append(
                (
                    jnp.where(mine, scaled, 0.0).astype(BF16),
                    k,
                    jnp.where(mine, wide, 0.0).astype(BF16),
                    v,
                    bias - stat[:, E * j : E * j + 1],
                    stat[:, E * j + 32 : E * j + 33],
                )
            )
    scores = [dot_nt(head[0], head[1]) for head in heads]
    through = [dot_nt(head[2], head[3]) for head in heads]
    weights = [jnp.exp(s + head[4]) for s, head in zip(scores, heads)]
    slopes = [
        (w * (t - head[5])).astype(BF16) for w, t, head in zip(weights, through, heads)
    ]
    weights = [w.astype(BF16) for w in weights]
    results = []
    for p, (q, k, _, grads, _) in enumerate(pairs):
        low_q = low_lanes(q.shape[0])
        low_k = low_lanes(k.shape[0])
        one, two = slopes[2 * p : 2 * p + 2]
        results.append(
            (
                jnp.where(low_q, dot(one, k), dot(two, k)) * 0.125,
                jnp.where(
                    low_k, dot_tn(one, scaled_pairs[p]), dot_tn(two, scaled_pairs[p])
                ),
                jnp.where(
                    low_k, dot_tn(weights[2 * p], grads), dot_tn(weights[2 * p + 1], grads)
                ),
            )
        )
    return results


def own_backward_kernel(steps):
    pairs = [tuple(view[...] for view in views[:5]) for views in steps]
    for views, grads in zip(steps, heads_backward(pairs, 0.0)):
        for view, value in zip(views[5:], grads):
            view[...] = value.astype(BF16)


def core_backward_kernel(steps):
    pairs = [(q[...], kv[0], kv[1], g[...], stat[...]) for q, kv, stat, g, _, _ in steps]
    for views, (dq, dk, dv) in zip(steps, heads_backward(pairs, LN2)):
        views[4][...] = dq.astype(BF16)
        views[5][0] = dk.astype(BF16)
        views[5][1] = dv.astype(BF16)


def ring_backward_kernel(steps):
    pairs = [
        (views[0][...],) + ring_pair(views[1], views[2]) + (views[4][...], views[3][...])
        for views in steps
    ]
    for views, (dq, dk, dv) in zip(steps, heads_backward(pairs, 2.0 * LN2)):
        views[5][...] = dq.astype(BF16)
        views[6][0] = dk[0:64]
        views[6][1] = dv[0:64]
        views[7][0] = dk[64:128].astype(BF16)
        views[7][1] = dv[64:128].astype(BF16)


def final_kernel(
    dq_ref, dk_ref, dv_ref, dq1_ref, kv1_ref, dq2_ref, kv2_ref, recv_ref,
    q_out, k_out, v_out, quarter_s, half_s, full_s,
):
    low = low_lanes(32)
    low16 = low_lanes(16)
    a = recv_ref[0].astype(F32)
    b = recv_ref[1].astype(F32)
    ar, br = swap_halves(a), swap_halves(b)
    g3k = jnp.where(low, a[0:32], br[0:32])
    g3v = jnp.where(low, ar[0:32], b[0:32])
    g3q = jnp.concatenate(
        [
            jnp.where(low16, a[32:48], br[32:48]),
            jnp.where(low16, ar[32:48], b[32:48]),
        ],
        axis=0,
    )
    work = (
        (dq_ref, dq1_ref[...].astype(F32), dq2_ref[...].astype(F32), g3q, q_out),
        (dk_ref, kv1_ref[0].astype(F32), kv2_ref[0].astype(F32), g3k, k_out),
        (dv_ref, kv1_ref[1].astype(F32), kv2_ref[1].astype(F32), g3v, v_out),
    )
    for index, (own, one, two, three, out) in enumerate(work):
        yield
        two = two + repeated(quarter_s.at[index], three * 0.5, 2)
        one = one + repeated(half_s.at[index], two * 0.5, 2)
        out[...] = (own[...].astype(F32) + repeated(full_s.at[index], one * 0.5, 2)).astype(BF16)


def pairs_of(mask, size):
    return [(source, source ^ mask) for source in range(size)]


def in_turn(kernel, steps):
    running = [kernel(*views) for views in steps]
    while running:
        running = [g for g in running if next(g, 0) is None]


class Tall:
    def __init__(self, rows):
        self.rows = rows

    def spec(self, step):
        return pl.BlockSpec((self.rows, LANES * step), lambda p: (0, p))

    def view(self, ref, i):
        return ref.at[:, LANES * i : LANES * (i + 1)]


class TwoTall(Tall):
    def spec(self, step):
        return pl.BlockSpec((2, self.rows, LANES * step), lambda p: (0, 0, p))

    def view(self, ref, i):
        return ref.at[:, :, LANES * i : LANES * (i + 1)]


class Slots(Tall):
    def spec(self, step):
        return pl.BlockSpec((2 * step, self.rows, LANES), lambda p: (p, 0, 0))

    def view(self, ref, i):
        return ref.at[2 * i : 2 * i + 2]


def over_pairs(
    kernel, outs, out_kinds, ins, in_kinds, scratch=(), step=2, flops=1e9, moved=5e6,
    joint=False,
):
    kinds = in_kinds + out_kinds

    def body(*refs):
        steps = [
            [kind.view(ref, i) for kind, ref in zip(kinds, refs)]
            + [ref.at[i] for ref in refs[len(kinds) :]]
            for i in range(step)
        ]
        if joint:
            kernel(steps)
        else:
            in_turn(kernel, steps)

    return pl.pallas_call(
        body,
        grid=(PAIRS // step,),
        out_shape=[jax.ShapeDtypeStruct(s, d) for s, d in outs],
        in_specs=[kind.spec(step) for kind in in_kinds],
        out_specs=[kind.spec(step) for kind in out_kinds],
        scratch_shapes=[pltpu.VMEM((step,) + shape + (LANES,), F32) for shape in scratch],
        compiler_params=pltpu.CompilerParams(vmem_limit_bytes=STEPS["limit"] * 1024 * 1024),
        cost_estimate=pl.CostEstimate(
            flops=int(flops), bytes_accessed=int(moved), transcendentals=0
        ),
    )(*ins)


STEPS = {"pool": 4, "local_forward": 4, "combine": 4, "local_backward": 4, "final": 4, "core_forward": 8, "core_backward": 4, "limit": 60}


def per_device(q, k, v, grad):
    size = lax.axis_size("seq")
    planes = size // RING
    rings = [[RING * g + i for i in range(RING)] for g in range(planes)]
    columns = [[RING * g + i for g in range(planes)] for i in range(RING)]
    me = (lax.axis_index("seq") // RING).astype(jnp.int32).reshape(1)
    rows, width = q.shape

    def exchange(x, groups):
        return lax.all_to_all(x, "seq", 0, 0, axis_index_groups=groups, tiled=True)

    def swapped(x, mask):
        return lax.ppermute(x, "seq", pairs_of(mask, size))

    quarter = (rows // 4, width)
    q1, kv1, q2, kv2, send1 = over_pairs(
        pool_kernel,
        [
            ((B, width), BF16),
            ((2, B, width), BF16),
            (quarter, BF16),
            ((2,) + quarter, BF16),
            ((RING, 48, LANES), BF16),
        ],
        [Tall(B), TwoTall(B), Tall(64), TwoTall(64), Slots(48)],
        (q, k, v),
        [Tall(rows)] * 3,
        scratch=((3, 256), (3, B), (3, 64)),
        step=STEPS["pool"],
    )
    kv1s = swapped(kv1, 1)
    recv1 = exchange(send1, rings)
    full = ((rows, width), F32)
    att0, lse0 = over_pairs(
        own_forward_kernel,
        [((rows, width), BF16), full],
        [Tall(rows)] * 2,
        (q, k, v),
        [Tall(rows)] * 3,
        step=STEPS["local_forward"],
        joint=True,
        flops=6e9,
        moved=1e7,
    )
    recv1, att0 = lax.optimization_barrier((recv1, att0))
    qh, kvh, block, sendx = call(
        prepare_kernel,
        [((STACK, LANES), BF16)] * 2 + [((B, LANES), BF16), ((RING, 64, LANES), BF16)],
        (me, recv1),
        smem_first=True,
    )
    sendx, kv2 = lax.optimization_barrier((sendx, kv2))
    beside = swapped(block, RING)
    kv2a = swapped(kv2, 2)
    kv2b = swapped(kv2a, 1)
    recvx = exchange(sendx, columns)
    half = (B, width)
    att1, lse1 = over_pairs(
        core_forward_kernel,
        [(half, BF16), (half, F32)],
        [Tall(B)] * 2,
        (q1, kv1s),
        [Tall(B), TwoTall(B)],
        step=STEPS["core_forward"],
        joint=True,
        flops=2e9,
    )
    tops, sums = call(
        head_forward_kernel, [((512, LANES), F32)] * 2, (qh, kvh), flops=1e9
    )
    recvx, att1 = lax.optimization_barrier((recvx, att1))
    send2, siblings = call(
        head_merge_kernel,
        [((RING, 32, LANES), BF16), ((4, B, LANES), BF16)],
        (me, beside, recvx, qh, tops, sums),
        smem_first=True,
    )
    send2, q2_later = lax.optimization_barrier((send2, q2))
    recv2 = exchange(send2, rings)
    att2, lse2 = over_pairs(
        ring_forward_kernel,
        [(quarter, BF16), (quarter, F32)],
        [Tall(64)] * 2,
        (q2_later, kv2a, kv2b),
        [Tall(64), TwoTall(64), TwoTall(64)],
        step=STEPS["core_forward"],
        joint=True,
        flops=2e9,
    )
    attended, stat, stat1, g1, stat2, g2, send3 = over_pairs(
        combine_kernel,
        [
            ((rows, width), BF16),
            full,
            (half, F32),
            (half, BF16),
            (quarter, F32),
            (quarter, BF16),
            ((RING, 32, LANES), BF16),
        ],
        [Tall(rows)] * 2 + [Tall(B)] * 2 + [Tall(64)] * 2 + [Slots(32)],
        (att0, lse0, att1, lse1, att2, lse2, recv2, grad),
        [Tall(rows)] * 2 + [Tall(B)] * 2 + [Tall(64)] * 2 + [Slots(32), Tall(rows)],
        scratch=((256,),) * 3 + ((B,),) * 3 + ((64,),) * 3 + ((6, 256),),
        step=STEPS["combine"],
    )
    recv3 = exchange(send3, rings)
    dq2, same, across = over_pairs(
        ring_backward_kernel,
        [(quarter, BF16), ((2,) + quarter, F32), ((2,) + quarter, BF16)],
        [Tall(64), TwoTall(64), TwoTall(64)],
        (q2, kv2a, kv2b, stat2, g2),
        [Tall(64), TwoTall(64), TwoTall(64), Tall(64), Tall(64)],
        step=STEPS["core_backward"],
        joint=True,
        flops=3e9,
    )
    recv3, dq2 = lax.optimization_barrier((recv3, dq2))
    partner = swapped(across, 1)
    back2 = swapped((same + partner.astype(F32)).astype(BF16), 2)
    stack = [pltpu.VMEM((STACK, LANES), F32)] * 2
    q5, part5, sendy = call(
        head_top_kernel,
        [((B, LANES), F32), ((B, LANES), BF16), ((RING, 64, LANES), BF16)],
        (me, recv3, qh, siblings),
        scratch=stack,
        smem_first=True,
    )
    part5, q1_late = lax.optimization_barrier((part5, q1))
    beside_grad = swapped(part5, RING)
    recvy = exchange(sendy, columns)
    query_low, other_low = call(
        head_low_kernel,
        [((512, LANES), F32)] * 2,
        (qh, kvh, recv3, q5),
        scratch=stack,
        flops=2e9,
    )
    dq1, dkv1 = over_pairs(
        core_backward_kernel,
        [(half, BF16), ((2, B, width), BF16)],
        [Tall(B), TwoTall(B)],
        (q1_late, kv1s, stat1, g1),
        [Tall(B), TwoTall(B)] + [Tall(B)] * 2,
        step=STEPS["core_backward"],
        joint=True,
        flops=3e9,
    )
    back1 = swapped(dkv1, 1)
    recvy, dq1 = lax.optimization_barrier((recvy, dq1))
    (send4,) = call(
        head_last_kernel,
        [((RING, 48, LANES), BF16)],
        (me, beside_grad, recvy, query_low, other_low),
        smem_first=True,
    )
    recv4 = exchange(send4, rings)
    dq, dk, dv = over_pairs(
        own_backward_kernel,
        [((rows, width), BF16)] * 3,
        [Tall(rows)] * 3,
        (q, k, v, grad, stat),
        [Tall(rows)] * 5,
        step=STEPS["local_backward"],
        joint=True,
        flops=9e9,
        moved=1e7,
    )
    query_grad, key_grad, value_grad = over_pairs(
        final_kernel,
        [((rows, width), BF16)] * 3,
        [Tall(rows)] * 3,
        (dq, dk, dv, dq1, back1, dq2, back2, recv4),
        [Tall(rows)] * 3 + [Tall(B), TwoTall(B), Tall(64), TwoTall(64), Slots(48)],
        scratch=((3, 64), (3, B), (3, 256)),
        step=STEPS["final"],
    )
    return attended, query_grad, key_grad, value_grad


def solution(mesh):
    return jax.shard_map(
        per_device,
        mesh=mesh,
        in_specs=(P("seq", None),) * 4,
        out_specs=(P("seq", None),) * 4,
        check_vma=False,
    )
```

```python
import functools
import math

import jax
import jax.numpy as jnp
from jax import lax
from jax.experimental import pallas as pl
from jax.experimental.pallas import tpu as pltpu
from jax.sharding import PartitionSpec as P

H = 16
E = 64
B = 128
LANES = 128
PAIRS = 8
RING = 16
LN2 = math.log(2.0)
F32 = jnp.float32
BF16 = jnp.bfloat16

ROWS = {l: 1024 >> (l - 2) for l in range(3, 9)}
FIRST = {3: 0, 4: 512, 5: 768, 6: 896, 7: 960, 8: 992}
STACK = 1024


def dot(a, b):
    return lax.dot_general(a, b, (((1,), (0,)), ((), ())), preferred_element_type=F32)


def dot_nt(a, b):
    return lax.dot_general(a, b, (((1,), (1,)), ((), ())), preferred_element_type=F32)


def dot_tn(a, b):
    return lax.dot_general(a, b, (((0,), (0,)), ((), ())), preferred_element_type=F32)


def lane_of(rows):
    return lax.broadcasted_iota(jnp.int32, (rows, LANES), 1)


def low_lanes(rows):
    return lane_of(rows) < E


def swap_halves(x):
    return pltpu.roll(x, E, 1)


def shift_of(factor):
    return factor.bit_length() - 1


def pool_matrix(rows_out, factor=2):
    r = lax.broadcasted_iota(jnp.int32, (rows_out, rows_out * factor), 0)
    c = lax.broadcasted_iota(jnp.int32, (rows_out, rows_out * factor), 1)
    return jnp.where(c >> shift_of(factor) == r, 1.0 / factor, 0.0).astype(BF16)


def spread_matrix(rows_in, factor, value=1.0):
    r = lax.broadcasted_iota(jnp.int32, (rows_in * factor, rows_in), 0)
    c = lax.broadcasted_iota(jnp.int32, (rows_in * factor, rows_in), 1)
    return jnp.where(r >> shift_of(factor) == c, value, 0.0).astype(BF16)


def pieces(x, count):
    out = []
    for _ in range(count):
        part = x.astype(BF16)
        out.append(part)
        x = x - part.astype(F32)
    return out


def spread(matrix, x, count):
    total = None
    for part in pieces(x, count):
        term = dot(matrix, part)
        total = term if total is None else total + term
    return total


def halved(scratch, x):
    rows = x.shape[0]
    scratch[0:rows, :] = x
    first = scratch[pl.ds(0, rows // 2, stride=2), :]
    second = scratch[pl.ds(1, rows // 2, stride=2), :]
    return ((first + second) * 0.5).astype(BF16)


def repeated(scratch, x, factor):
    rows = x.shape[0]
    for i in range(factor):
        scratch[pl.ds(i, rows, stride=factor), :] = x
    return scratch[0 : rows * factor, :]


def call(kernel, outs, ins, scratch=(), flops=1e8, smem_first=False):
    specs = [pl.BlockSpec(memory_space=pltpu.VMEM) for _ in ins]
    if smem_first:
        specs[0] = pl.BlockSpec(memory_space=pltpu.SMEM)
    return pl.pallas_call(
        kernel,
        out_shape=[jax.ShapeDtypeStruct(s, d) for s, d in outs],
        in_specs=specs,
        out_specs=[pl.BlockSpec(memory_space=pltpu.VMEM) for _ in outs],
        scratch_shapes=list(scratch),
        compiler_params=pltpu.CompilerParams(vmem_limit_bytes=40 * 1024 * 1024),
        cost_estimate=pl.CostEstimate(
            flops=int(flops), bytes_accessed=2_000_000, transcendentals=0
        ),
    )(*ins)


def place(x, diagonal):
    return jnp.sum(jnp.where(diagonal, x, 0.0), axis=0, keepdims=True)


def pool_kernel(
    q_ref, k_ref, v_ref, q1_ref, kv1_ref, q2_ref, kv2_ref, send_ref, one_s, two_s, three_s
):
    low = low_lanes(32)
    low16 = low_lanes(16)
    level3 = []
    for index, ref in enumerate((q_ref, k_ref, v_ref)):
        yield
        one = halved(one_s.at[index], ref[...].astype(F32))
        two = halved(two_s.at[index], one.astype(F32))
        if index == 0:
            q1_ref[...] = one
            q2_ref[...] = two
        else:
            kv1_ref[index - 1] = one
            kv2_ref[index - 1] = two
        level3.append(halved(three_s.at[index], two.astype(F32)).astype(F32))
    q, k, v = level3
    qr, kr, vr = swap_halves(q), swap_halves(k), swap_halves(v)
    send_ref[0, 0:32, :] = jnp.where(low, k, vr).astype(BF16)
    send_ref[1, 0:32, :] = jnp.where(low, kr, v).astype(BF16)
    send_ref[0, 32:48, :] = jnp.where(low16, q[0:16], qr[16:32]).astype(BF16)
    send_ref[1, 32:48, :] = jnp.where(low16, qr[0:16], q[16:32]).astype(BF16)


def sibling_slots(me, level):
    bit = level - 5
    first = ((me >> bit) ^ 1) << bit
    return [first + i for i in range(1 << bit)]


def pool_stack(ref):
    for level in range(3, 8):
        rows = ROWS[level]
        step = min(rows, 256)
        matrix = pool_matrix(step // 2)
        for start in range(0, rows, step):
            source = slice(FIRST[level] + start, FIRST[level] + start + step)
            at = FIRST[level + 1] + start // 2
            ref[at : at + step // 2, :] = dot(matrix, ref[source, :]).astype(BF16)
    end = FIRST[8] + ROWS[8]
    ref[end:STACK, :] = jnp.zeros((STACK - end, LANES), BF16)


def prepare_keys_kernel(me_ref, recv_ref, kv_ref, block_ref, send_ref):
    me = me_ref[0]
    for d in range(RING):
        kv_ref[32 * d : 32 * d + 32, :] = recv_ref[d, 0:32, :]
    pool_stack(kv_ref)
    block_ref[...] = kv_ref[FIRST[5] : FIRST[5] + B, :]
    send_ref[...] = jnp.zeros_like(send_ref)
    for level in range(6, 9):
        rows = ROWS[level]
        block = kv_ref[FIRST[level] : FIRST[level] + rows, :]
        for slot in sibling_slots(me, level):
            send_ref[slot, 0:rows, :] = block


def prepare_queries_kernel(recv_ref, q_ref):
    low16 = low_lanes(16)
    for d in range(RING):
        packed = recv_ref[d, 32:48, :].astype(F32) * 0.125
        q_ref[32 * d : 32 * d + 16, :] = jnp.where(low16, packed, 0.0).astype(BF16)
        q_ref[32 * d + 16 : 32 * d + 32, :] = jnp.where(
            low16, swap_halves(packed), 0.0
        ).astype(BF16)
    pool_stack(q_ref)


def heads_forward(pairs, bias):
    heads = []
    for q, k, v in pairs:
        low_q = low_lanes(q.shape[0])
        low_v = low_lanes(v.shape[0])
        scaled = q.astype(F32) * 0.125
        values = v.astype(F32)
        for mine_q, mine_v in (
            (low_q, low_v),
            (jnp.logical_not(low_q), jnp.logical_not(low_v)),
        ):
            heads.append(
                (
                    jnp.where(mine_q, scaled, 0.0).astype(BF16),
                    k,
                    jnp.where(mine_v, values, 1.0).astype(BF16),
                )
            )
    scores = [dot_nt(q, k) for q, k, _ in heads]
    tops = [jnp.max(s, axis=1, keepdims=True) for s in scores]
    raised = [jnp.exp(s - top).astype(BF16) for s, top in zip(scores, tops)]
    sums = [dot(r, head[2]) for r, head in zip(raised, heads)]
    results = []
    for p, (q, _, _) in enumerate(pairs):
        low = low_lanes(q.shape[0])
        weighted = jnp.where(low, sums[2 * p], sums[2 * p + 1])
        total = swap_halves(jnp.where(low, sums[2 * p + 1], sums[2 * p]))
        top = jnp.where(low, tops[2 * p], tops[2 * p + 1])
        results.append((weighted / total, top + jnp.log(total) + bias))
    return results


def own_forward_kernel(steps):
    pairs = [(q[...], k[...], v[...]) for q, k, v, _, _ in steps]
    for views, (att, lse) in zip(steps, heads_forward(pairs, 0.0)):
        views[3][...] = att
        views[4][...] = lse


def core_forward_kernel(steps):
    pairs = [(q[...], kv[0], kv[1]) for q, kv, _, _ in steps]
    for views, (att, lse) in zip(steps, heads_forward(pairs, LN2)):
        views[2][...] = att
        views[3][...] = lse


def ring_pair(kva, kvb):
    return (
        jnp.concatenate([kva[0], kvb[0]], axis=0),
        jnp.concatenate([kva[1], kvb[1]], axis=0),
    )


def ring_forward_kernel(steps):
    pairs = [(q[...],) + ring_pair(kva, kvb) for q, kva, kvb, _, _ in steps]
    for views, (att, lse) in zip(steps, heads_forward(pairs, 2.0 * LN2)):
        views[3][...] = att
        views[4][...] = lse


def attend(q, kv, level):
    s = dot_nt(q, kv)
    top = jnp.max(s, axis=1, keepdims=True)
    raised = jnp.exp(s - top)
    ones = jnp.where(low_lanes(B), 1.0, kv.astype(F32)).astype(BF16)
    tops = jnp.broadcast_to(top + level * LN2, (q.shape[0], LANES))
    return tops, dot(raised.astype(BF16), ones)


def join(top_a, sum_a, top_b, sum_b):
    high = jnp.maximum(top_a, top_b)
    return high, jnp.exp(top_a - high) * sum_a + jnp.exp(top_b - high) * sum_b


def head_forward_kernel(q_ref, kv_ref, top_ref, sum_ref):
    tops, sums = None, None
    double = spread_matrix(64, 2)
    for level in (4, 3):
        new_tops, new_sums = [], []
        for block in range(ROWS[level] // B):
            at = FIRST[level] + B * block
            beside = FIRST[level] + B * (block ^ 1)
            top, total = attend(q_ref[at : at + B, :], kv_ref[beside : beside + B, :], level)
            if tops is not None:
                half = slice(64 * (block % 2), 64 * (block % 2) + 64)
                up_top = spread(double, tops[block // 2][half], 3)
                up_sum = spread(double, sums[block // 2][half], 2)
                top, total = join(top, total, up_top, up_sum)
            new_sums.append(total)
            new_tops.append(top)
        tops, sums = new_tops, new_sums
    for block in range(4):
        top_ref[B * block : B * block + B, :] = tops[block]
        sum_ref[B * block : B * block + B, :] = sums[block]


def head_merge_kernel(
    me_ref, beside_ref, recv_ref, q_ref, top_ref, sum_ref, send_ref, sibling_ref
):
    me = me_ref[0]
    sibling_ref[0] = beside_ref[...]
    levels = (8, 7, 6, 5)
    for level in levels[:3]:
        rows = ROWS[level]
        for index, slot in enumerate(sibling_slots(me, level)):
            sibling_ref[level - 5, rows * index : rows * index + rows, :] = recv_ref[
                slot, 0:rows, :
            ]
    keys = [sibling_ref[level - 5] for level in levels]
    scores = [
        dot_nt(q_ref[FIRST[level] : FIRST[level] + ROWS[level], :], kv)
        for level, kv in zip(levels, keys)
    ]
    highest = [jnp.max(s, axis=1, keepdims=True) for s in scores]
    raised = [jnp.exp(s - top).astype(BF16) for s, top in zip(scores, highest)]
    totals = [
        dot(r, jnp.where(low_lanes(B), 1.0, kv.astype(F32)).astype(BF16))
        for r, kv in zip(raised, keys)
    ]
    tops, sums = None, None
    for level, top, total in zip(levels, highest, totals):
        rows = ROWS[level]
        top = jnp.broadcast_to(top + level * LN2, (rows, LANES))
        if tops is not None:
            double = spread_matrix(rows // 2, 2)
            top, total = join(top, total, spread(double, tops, 3), spread(double, sums, 2))
        tops, sums = top, total
    low = low_lanes(B)
    low16 = low_lanes(16)
    diagonal = lax.broadcasted_iota(jnp.int32, (32, LANES), 0) == lane_of(32)
    four = spread_matrix(32, 4)
    tail = jnp.zeros((13, LANES), F32)
    spreads = [
        (spread(four, tops[32 * i : 32 * i + 32], 3), spread(four, sums[32 * i : 32 * i + 32], 2))
        for i in range(4)
    ]
    for i, (up_top, up_sum) in enumerate(spreads):
        at = slice(B * i, B * i + B)
        high, total = join(top_ref[at, :], sum_ref[at, :], up_top, up_sum)
        count = jnp.where(low, total, swap_halves(total))
        att = total / count
        lse = high + jnp.log(count)
        moved = swap_halves(att)
        for j in range(4):
            d = 4 * i + j
            r = 32 * j
            send_ref[d, 0:16, :] = jnp.where(
                low16, moved[r : r + 16], att[r + 16 : r + 32]
            ).astype(BF16)
            line = place(lse[r : r + 32], diagonal)
            parts = [part.astype(F32) for part in pieces(line, 3)]
            send_ref[d, 16:32, :] = jnp.concatenate(parts + [tail], axis=0).astype(BF16)


def combine_kernel(
    att0_ref, lse0_ref, att1_ref, lse1_ref, att2_ref, lse2_ref, recv_ref, grad_ref,
    out_ref, stat_ref, stat1_ref, g1_ref, stat2_ref, g2_ref, send_ref,
    lse_s, grad_s, align_s, r_s, g_s, f_s, r2_s, g2_s, f2_s, up_s,
):
    low16 = low_lanes(16)
    r = lax.broadcasted_iota(jnp.int32, (LANES, LANES), 0)
    c = lax.broadcasted_iota(jnp.int32, (LANES, LANES), 1)
    per_head = jnp.where(r >> 6 == c >> 6, 1.0, 0.0).astype(BF16)
    own = lax.broadcasted_iota(jnp.int32, (32, LANES), 0) == lane_of(32)

    packed_a = recv_ref[0].astype(F32)
    packed_b = recv_ref[1].astype(F32)
    rows_a, rows_b = packed_a[0:16], packed_b[0:16]
    att3 = jnp.concatenate(
        [
            jnp.where(low16, rows_a, swap_halves(rows_b)),
            jnp.where(low16, swap_halves(rows_a), rows_b),
        ],
        axis=0,
    )
    columns = []
    for packed in (packed_a, packed_b):
        line = packed[16:17] + packed[17:18] + packed[18:19]
        columns.append(jnp.sum(jnp.where(own, line, 0.0), axis=1, keepdims=True))
    lse = jnp.where(low_lanes(32), columns[0], columns[1])
    att = att3
    yield
    for index, (att_ref, lse_ref) in enumerate(
        ((att2_ref, lse2_ref), (att1_ref, lse1_ref), (att0_ref, lse0_ref))
    ):
        att = repeated(up_s.at[2 * index], att, 2)
        lse = repeated(up_s.at[2 * index + 1], lse, 2)
        own_lse = lse_ref[...]
        high = jnp.maximum(lse, own_lse)
        e_up = jnp.exp(lse - high)
        e_own = jnp.exp(own_lse - high)
        den = e_up + e_own
        att = (e_up * att + e_own * att_ref[...]) / den
        lse = high + jnp.log(den)
        yield
    attended = att.astype(BF16)
    full = lse
    out_ref[...] = attended
    grad = grad_ref[...].astype(F32)
    product = grad * attended.astype(F32)
    align = None
    for part in pieces(product, 2):
        term = dot(part, per_head)
        align = term if align is None else align + term
    yield
    stat_ref[...] = jnp.where(lane_of(256) & 32 == 0, full, align)
    lse_s[...] = full
    grad_s[...] = grad
    align_s[...] = align

    def fold(lse, grads, aligns, rows):
        a, b = pl.ds(0, rows, stride=2), pl.ds(1, rows, stride=2)
        la, lb = lse[a, :], lse[b, :]
        least = jnp.minimum(la, lb)
        ea, eb = jnp.exp(least - la), jnp.exp(least - lb)
        return (
            least,
            ea * grads[a, :] + eb * grads[b, :],
            ea * aligns[a, :] + eb * aligns[b, :],
        )

    r1, g1, f1 = fold(lse_s, grad_s, align_s, 128)
    stat1_ref[...] = jnp.where(lane_of(B) & 32 == 0, r1, f1)
    g1_ref[...] = g1.astype(BF16)
    yield
    r_s[...] = r1
    g_s[...] = g1
    f_s[...] = f1
    r2, g2, f2 = fold(r_s, g_s, f_s, 64)
    stat2_ref[...] = jnp.where(lane_of(64) & 32 == 0, r2, f2)
    g2_ref[...] = g2.astype(BF16)
    yield
    r2_s[...] = r2
    g2_s[...] = g2
    f2_s[...] = f2
    r3, g3, f3 = fold(r2_s, g2_s, f2_s, 32)
    row32 = lax.broadcasted_iota(jnp.int32, (32, LANES), 0)
    diagonal = row32 == (lane_of(32) & (E - 1))
    line_r = place(r3, diagonal)
    line_f = place(f3, diagonal)
    yield
    low1 = low_lanes(1)
    wide_r = jnp.broadcast_to(line_r, (8, LANES))
    wide_f = jnp.broadcast_to(line_f, (8, LANES))
    lines = (
        jnp.where(low1, line_r, swap_halves(wide_f)[0:1]),
        jnp.where(low1, swap_halves(wide_r)[0:1], line_f),
    )
    moved = swap_halves(g3)
    tail = jnp.zeros((13, LANES), F32)
    send_ref[0, 0:16, :] = jnp.where(low16, g3[0:16], moved[16:32]).astype(BF16)
    send_ref[1, 0:16, :] = jnp.where(low16, moved[0:16], g3[16:32]).astype(BF16)
    for j in range(2):
        parts = [part.astype(F32) for part in pieces(lines[j], 3)]
        send_ref[j, 16:32, :] = jnp.concatenate(parts + [tail], axis=0).astype(BF16)


def levels_backward(items):
    scores = [dot_nt(q, kv) for q, kv, _, _, _ in items]
    cograds = [
        jnp.where(low_lanes(q.shape[0]), 0.0, grads).astype(BF16)
        for q, _, _, grads, _ in items
    ]
    through = [dot_nt(c, item[1]) for c, item in zip(cograds, items)]
    weights = [
        jnp.exp(s + (level * LN2 - least[:, 0:1]))
        for s, (_, _, least, _, level) in zip(scores, items)
    ]
    slopes = [
        (w * (t - item[3][:, 0:1])).astype(BF16)
        for w, t, item in zip(weights, through, items)
    ]
    return [
        (
            dot(slope, item[1]) * 0.125,
            dot_tn(slope, item[0]) + dot_tn(w.astype(BF16), c),
        )
        for slope, w, c, item in zip(slopes, weights, cograds, items)
    ]


def unpack_and_fold(recv_ref, r_ref, g_ref, last):
    low = low_lanes(32)
    row32 = lax.broadcasted_iota(jnp.int32, (32, LANES), 0)
    first = row32 == lane_of(32)
    second = row32 + E == lane_of(32)
    for d in range(RING):
        packed = recv_ref[d].astype(F32)
        line = packed[16:17] + packed[17:18] + packed[18:19]
        least = jnp.sum(jnp.where(first, line, 0.0), axis=1, keepdims=True)
        flow = jnp.sum(jnp.where(second, line, 0.0), axis=1, keepdims=True)
        grads = jnp.concatenate([swap_halves(packed[0:16]), packed[0:16]], axis=0)
        r_ref[32 * d : 32 * d + 32, :] = jnp.broadcast_to(least, (32, LANES))
        g_ref[32 * d : 32 * d + 32, :] = jnp.where(low, flow, grads)
    for level in range(3, last):
        rows = ROWS[level + 1]
        a = pl.ds(FIRST[level], rows, stride=2)
        b = pl.ds(FIRST[level] + 1, rows, stride=2)
        la, lb = r_ref[a, :], r_ref[b, :]
        least = jnp.minimum(la, lb)
        to = slice(FIRST[level + 1], FIRST[level + 1] + rows)
        r_ref[to, :] = least
        g_ref[to, :] = jnp.exp(least - la) * g_ref[a, :] + jnp.exp(least - lb) * g_ref[b, :]


def head_top_kernel(
    me_ref, recv_ref, q_ref, sibling_ref, q5_ref, beside_ref, send_ref, r_ref, g_ref
):
    me = me_ref[0]
    unpack_and_fold(recv_ref, r_ref, g_ref, 8)
    send_ref[...] = jnp.zeros_like(send_ref)
    running = None
    levels = (8, 7, 6, 5)
    spans = [slice(FIRST[level], FIRST[level] + ROWS[level]) for level in levels]
    results = levels_backward(
        [
            (q_ref[at, :], sibling_ref[level - 5], r_ref[at, :], g_ref[at, :], level)
            for level, at in zip(levels, spans)
        ]
    )
    for level, (query_part, other_part) in zip(levels, results):
        rows = ROWS[level]
        other_part = other_part.astype(BF16)
        if level == 5:
            beside_ref[...] = other_part
        for index, slot in enumerate(sibling_slots(me, level) if level > 5 else ()):
            send_ref[slot, 0:rows, :] = other_part[rows * index : rows * index + rows]
        if running is None:
            running = query_part
        else:
            running = query_part + spread(spread_matrix(rows // 2, 2, 0.5), running, 2)
    q5_ref[...] = running


def head_low_kernel(q_ref, kv_ref, recv_ref, q5_ref, query_ref, other_ref, r_ref, g_ref):
    unpack_and_fold(recv_ref, r_ref, g_ref, 4)
    double = spread_matrix(64, 2, 0.5)
    query_up = [q5_ref[...]]
    other_up = None
    for level in (4, 3):
        blocks = ROWS[level] // B
        query_parts = [None] * blocks
        other_parts = [None] * blocks
        results = levels_backward(
            [
                (
                    q_ref[FIRST[level] + B * i : FIRST[level] + B * i + B, :],
                    kv_ref[FIRST[level] + B * (i ^ 1) : FIRST[level] + B * (i ^ 1) + B, :],
                    r_ref[FIRST[level] + B * i : FIRST[level] + B * i + B, :],
                    g_ref[FIRST[level] + B * i : FIRST[level] + B * i + B, :],
                    level,
                )
                for i in range(blocks)
            ]
        )
        for block, (query_part, other_part) in enumerate(results):
            query_parts[block] = query_part
            other_parts[block ^ 1] = other_part
        for block in range(blocks):
            half = slice(64 * (block % 2), 64 * (block % 2) + 64)
            query_parts[block] = query_parts[block] + spread(
                double, query_up[block // 2][half], 2
            )
            if other_up is not None:
                other_parts[block] = other_parts[block] + spread(
                    double, other_up[block // 2][half], 2
                )
        query_up, other_up = query_parts, other_parts
    for block in range(4):
        query_ref[B * block : B * block + B, :] = query_up[block]
        other_ref[B * block : B * block + B, :] = other_up[block]


def head_last_kernel(me_ref, beside_ref, recv_ref, query_ref, other_ref, send_ref):
    me = me_ref[0]
    running = None
    for level in (8, 7, 6):
        rows = ROWS[level]
        total = None
        for slot in sibling_slots(me, level):
            term = recv_ref[slot, 0:rows, :].astype(F32)
            total = term if total is None else total + term
        if running is not None:
            total = total + spread(spread_matrix(rows // 2, 2, 0.5), running, 2)
        running = total
    running = beside_ref[...].astype(F32) + spread(spread_matrix(64, 2, 0.5), running, 2)
    four = spread_matrix(8, 4, 0.25)
    low16 = low_lanes(16)
    for d in range(RING):
        at = slice(32 * d, 32 * d + 32)
        other = other_ref[at, :] + spread(four, running[8 * d : 8 * d + 8], 2)
        query = query_ref[at, :]
        send_ref[d, 0:32, :] = other.astype(BF16)
        send_ref[d, 32:48, :] = jnp.where(
            low16, query[0:16], swap_halves(query)[16:32]
        ).astype(BF16)


def heads_backward(pairs, bias):
    heads = []
    scaled_pairs = []
    for q, k, v, grads, stat in pairs:
        low_q = low_lanes(q.shape[0])
        scaled = q.astype(F32) * 0.125
        wide = grads.astype(F32)
        scaled_pairs.append(scaled.astype(BF16))
        for j in range(2):
            mine = low_q if j == 0 else jnp.logical_not(low_q)
            heads.append(
                (
                    jnp.where(mine, scaled, 0.0).astype(BF16),
                    k,
                    jnp.where(mine, wide, 0.0).astype(BF16),
                    v,
                    bias - stat[:, E * j : E * j + 1],
                    stat[:, E * j + 32 : E * j + 33],
                )
            )
    scores = [dot_nt(head[0], head[1]) for head in heads]
    through = [dot_nt(head[2], head[3]) for head in heads]
    weights = [jnp.exp(s + head[4]) for s, head in zip(scores, heads)]
    slopes = [
        (w * (t - head[5])).astype(BF16) for w, t, head in zip(weights, through, heads)
    ]
    weights = [w.astype(BF16) for w in weights]
    results = []
    for p, (q, k, _, grads, _) in enumerate(pairs):
        low_q = low_lanes(q.shape[0])
        low_k = low_lanes(k.shape[0])
        one, two = slopes[2 * p : 2 * p + 2]
        results.append(
            (
                jnp.where(low_q, dot(one, k), dot(two, k)) * 0.125,
                jnp.where(
                    low_k, dot_tn(one, scaled_pairs[p]), dot_tn(two, scaled_pairs[p])
                ),
                jnp.where(
                    low_k, dot_tn(weights[2 * p], grads), dot_tn(weights[2 * p + 1], grads)
                ),
            )
        )
    return results


def own_backward_kernel(steps):
    pairs = [tuple(view[...] for view in views[:5]) for views in steps]
    for views, grads in zip(steps, heads_backward(pairs, 0.0)):
        for view, value in zip(views[5:], grads):
            view[...] = value.astype(BF16)


def core_backward_kernel(steps):
    pairs = [(q[...], kv[0], kv[1], g[...], stat[...]) for q, kv, stat, g, _, _ in steps]
    for views, (dq, dk, dv) in zip(steps, heads_backward(pairs, LN2)):
        views[4][...] = dq.astype(BF16)
        views[5][0] = dk.astype(BF16)
        views[5][1] = dv.astype(BF16)


def ring_backward_kernel(steps):
    pairs = [
        (views[0][...],) + ring_pair(views[1], views[2]) + (views[4][...], views[3][...])
        for views in steps
    ]
    for views, (dq, dk, dv) in zip(steps, heads_backward(pairs, 2.0 * LN2)):
        views[5][...] = dq.astype(BF16)
        views[6][0] = dk[0:64]
        views[6][1] = dv[0:64]
        views[7][0] = dk[64:128].astype(BF16)
        views[7][1] = dv[64:128].astype(BF16)


def final_kernel(
    dq_ref, dk_ref, dv_ref, dq1_ref, kv1_ref, dq2_ref, kv2_ref, recv_ref,
    q_out, k_out, v_out, quarter_s, half_s, full_s,
):
    low = low_lanes(32)
    low16 = low_lanes(16)
    a = recv_ref[0].astype(F32)
    b = recv_ref[1].astype(F32)
    ar, br = swap_halves(a), swap_halves(b)
    g3k = jnp.where(low, a[0:32], br[0:32])
    g3v = jnp.where(low, ar[0:32], b[0:32])
    g3q = jnp.concatenate(
        [
            jnp.where(low16, a[32:48], br[32:48]),
            jnp.where(low16, ar[32:48], b[32:48]),
        ],
        axis=0,
    )
    work = (
        (dq_ref, dq1_ref[...].astype(F32), dq2_ref[...].astype(F32), g3q, q_out),
        (dk_ref, kv1_ref[0].astype(F32), kv2_ref[0].astype(F32), g3k, k_out),
        (dv_ref, kv1_ref[1].astype(F32), kv2_ref[1].astype(F32), g3v, v_out),
    )
    for index, (own, one, two, three, out) in enumerate(work):
        yield
        two = two + repeated(quarter_s.at[index], three * 0.5, 2)
        one = one + repeated(half_s.at[index], two * 0.5, 2)
        out[...] = (own[...].astype(F32) + repeated(full_s.at[index], one * 0.5, 2)).astype(BF16)


def pairs_of(mask, size):
    return [(source, source ^ mask) for source in range(size)]


def in_turn(kernel, steps):
    running = [kernel(*views) for views in steps]
    while running:
        running = [g for g in running if next(g, 0) is None]


class Tall:
    def __init__(self, rows):
        self.rows = rows

    def spec(self, step):
        return pl.BlockSpec((self.rows, LANES * step), lambda p: (0, p))

    def view(self, ref, i):
        return ref.at[:, LANES * i : LANES * (i + 1)]


class TwoTall(Tall):
    def spec(self, step):
        return pl.BlockSpec((2, self.rows, LANES * step), lambda p: (0, 0, p))

    def view(self, ref, i):
        return ref.at[:, :, LANES * i : LANES * (i + 1)]


class Slots(Tall):
    def spec(self, step):
        return pl.BlockSpec((2 * step, self.rows, LANES), lambda p: (p, 0, 0))

    def view(self, ref, i):
        return ref.at[2 * i : 2 * i + 2]


def over_pairs(
    kernel, outs, out_kinds, ins, in_kinds, scratch=(), step=2, flops=1e9, moved=5e6,
    joint=False,
):
    kinds = in_kinds + out_kinds

    def body(*refs):
        steps = [
            [kind.view(ref, i) for kind, ref in zip(kinds, refs)]
            + [ref.at[i] for ref in refs[len(kinds) :]]
            for i in range(step)
        ]
        if joint:
            kernel(steps)
        else:
            in_turn(kernel, steps)

    return pl.pallas_call(
        body,
        grid=(PAIRS // step,),
        out_shape=[jax.ShapeDtypeStruct(s, d) for s, d in outs],
        in_specs=[kind.spec(step) for kind in in_kinds],
        out_specs=[kind.spec(step) for kind in out_kinds],
        scratch_shapes=[pltpu.VMEM((step,) + shape + (LANES,), F32) for shape in scratch],
        compiler_params=pltpu.CompilerParams(vmem_limit_bytes=STEPS["limit"] * 1024 * 1024),
        cost_estimate=pl.CostEstimate(
            flops=int(flops), bytes_accessed=int(moved), transcendentals=0
        ),
    )(*ins)


STEPS = {"pool": 4, "local_forward": 4, "combine": 4, "local_backward": 4, "final": 4, "core_forward": 8, "core_backward": 4, "limit": 60}


def per_device(q, k, v, grad):
    size = lax.axis_size("seq")
    planes = size // RING
    rings = [[RING * g + i for i in range(RING)] for g in range(planes)]
    columns = [[RING * g + i for g in range(planes)] for i in range(RING)]
    me = (lax.axis_index("seq") // RING).astype(jnp.int32).reshape(1)
    rows, width = q.shape

    def exchange(x, groups):
        return lax.all_to_all(x, "seq", 0, 0, axis_index_groups=groups, tiled=True)

    def swapped(x, mask):
        return lax.ppermute(x, "seq", pairs_of(mask, size))

    quarter = (rows // 4, width)
    q1, kv1, q2, kv2, send1 = over_pairs(
        pool_kernel,
        [
            ((B, width), BF16),
            ((2, B, width), BF16),
            (quarter, BF16),
            ((2,) + quarter, BF16),
            ((RING, 48, LANES), BF16),
        ],
        [Tall(B), TwoTall(B), Tall(64), TwoTall(64), Slots(48)],
        (q, k, v),
        [Tall(rows)] * 3,
        scratch=((3, 256), (3, B), (3, 64)),
        step=STEPS["pool"],
    )
    kv1s = swapped(kv1, 1)
    recv1 = exchange(send1, rings)
    full = ((rows, width), F32)
    att0, lse0 = over_pairs(
        own_forward_kernel,
        [full, full],
        [Tall(rows)] * 2,
        (q, k, v),
        [Tall(rows)] * 3,
        step=STEPS["local_forward"],
        joint=True,
        flops=6e9,
        moved=1e7,
    )
    recv1, att0 = lax.optimization_barrier((recv1, att0))
    kvh, block, sendx = call(
        prepare_keys_kernel,
        [((STACK, LANES), BF16), ((B, LANES), BF16), ((RING, 64, LANES), BF16)],
        (me, recv1),
        smem_first=True,
    )
    sendx, recv1 = lax.optimization_barrier((sendx, recv1))
    (qh,) = call(prepare_queries_kernel, [((STACK, LANES), BF16)], (recv1,))
    sendx, kv2 = lax.optimization_barrier((sendx, kv2))
    beside = swapped(block, RING)
    kv2a = swapped(kv2, 2)
    kv2b = swapped(kv2a, 1)
    recvx = exchange(sendx, columns)
    half = (B, width)
    att1, lse1 = over_pairs(
        core_forward_kernel,
        [(half, F32), (half, F32)],
        [Tall(B)] * 2,
        (q1, kv1s),
        [Tall(B), TwoTall(B)],
        step=STEPS["core_forward"],
        joint=True,
        flops=2e9,
    )
    tops, sums = call(
        head_forward_kernel, [((512, LANES), F32)] * 2, (qh, kvh), flops=1e9
    )
    recvx, att1 = lax.optimization_barrier((recvx, att1))
    send2, siblings = call(
        head_merge_kernel,
        [((RING, 32, LANES), BF16), ((4, B, LANES), BF16)],
        (me, beside, recvx, qh, tops, sums),
        smem_first=True,
    )
    send2, q2_later = lax.optimization_barrier((send2, q2))
    recv2 = exchange(send2, rings)
    att2, lse2 = over_pairs(
        ring_forward_kernel,
        [(quarter, F32), (quarter, F32)],
        [Tall(64)] * 2,
        (q2_later, kv2a, kv2b),
        [Tall(64), TwoTall(64), TwoTall(64)],
        step=STEPS["core_forward"],
        joint=True,
        flops=2e9,
    )
    attended, stat, stat1, g1, stat2, g2, send3 = over_pairs(
        combine_kernel,
        [
            ((rows, width), BF16),
            full,
            (half, F32),
            (half, BF16),
            (quarter, F32),
            (quarter, BF16),
            ((RING, 32, LANES), BF16),
        ],
        [Tall(rows)] * 2 + [Tall(B)] * 2 + [Tall(64)] * 2 + [Slots(32)],
        (att0, lse0, att1, lse1, att2, lse2, recv2, grad),
        [Tall(rows)] * 2 + [Tall(B)] * 2 + [Tall(64)] * 2 + [Slots(32), Tall(rows)],
        scratch=((256,),) * 3 + ((B,),) * 3 + ((64,),) * 3 + ((6, 256),),
        step=STEPS["combine"],
    )
    recv3 = exchange(send3, rings)
    dq2, same, across = over_pairs(
        ring_backward_kernel,
        [(quarter, BF16), ((2,) + quarter, F32), ((2,) + quarter, BF16)],
        [Tall(64), TwoTall(64), TwoTall(64)],
        (q2, kv2a, kv2b, stat2, g2),
        [Tall(64), TwoTall(64), TwoTall(64), Tall(64), Tall(64)],
        step=STEPS["core_backward"],
        joint=True,
        flops=3e9,
    )
    recv3, dq2 = lax.optimization_barrier((recv3, dq2))
    partner = swapped(across, 1)
    back2 = swapped((same + partner.astype(F32)).astype(BF16), 2)
    stack = [pltpu.VMEM((STACK, LANES), F32)] * 2
    q5, part5, sendy = call(
        head_top_kernel,
        [((B, LANES), F32), ((B, LANES), BF16), ((RING, 64, LANES), BF16)],
        (me, recv3, qh, siblings),
        scratch=stack,
        smem_first=True,
    )
    part5, q1_late = lax.optimization_barrier((part5, q1))
    beside_grad = swapped(part5, RING)
    recvy = exchange(sendy, columns)
    query_low, other_low = call(
        head_low_kernel,
        [((512, LANES), F32)] * 2,
        (qh, kvh, recv3, q5),
        scratch=stack,
        flops=2e9,
    )
    dq1, dkv1 = over_pairs(
        core_backward_kernel,
        [(half, BF16), ((2, B, width), BF16)],
        [Tall(B), TwoTall(B)],
        (q1_late, kv1s, stat1, g1),
        [Tall(B), TwoTall(B)] + [Tall(B)] * 2,
        step=STEPS["core_backward"],
        joint=True,
        flops=3e9,
    )
    back1 = swapped(dkv1, 1)
    recvy, dq1 = lax.optimization_barrier((recvy, dq1))
    (send4,) = call(
        head_last_kernel,
        [((RING, 48, LANES), BF16)],
        (me, beside_grad, recvy, query_low, other_low),
        smem_first=True,
    )
    recv4 = exchange(send4, rings)
    dq, dk, dv = over_pairs(
        own_backward_kernel,
        [((rows, width), BF16)] * 3,
        [Tall(rows)] * 3,
        (q, k, v, grad, stat),
        [Tall(rows)] * 5,
        step=STEPS["local_backward"],
        joint=True,
        flops=9e9,
        moved=1e7,
    )
    query_grad, key_grad, value_grad = over_pairs(
        final_kernel,
        [((rows, width), BF16)] * 3,
        [Tall(rows)] * 3,
        (dq, dk, dv, dq1, back1, dq2, back2, recv4),
        [Tall(rows)] * 3 + [Tall(B), TwoTall(B), Tall(64), TwoTall(64), Slots(48)],
        scratch=((3, 64), (3, B), (3, 256)),
        step=STEPS["final"],
    )
    return attended, query_grad, key_grad, value_grad


def solution(mesh):
    return jax.shard_map(
        per_device,
        mesh=mesh,
        in_specs=(P("seq", None),) * 4,
        out_specs=(P("seq", None),) * 4,
        check_vma=False,
    )
```

```python
import functools
import math

import jax
import jax.numpy as jnp
from jax import lax
from jax.experimental import pallas as pl
from jax.experimental.pallas import tpu as pltpu
from jax.sharding import PartitionSpec as P

H = 16
E = 64
B = 128
LANES = 128
PAIRS = 8
RING = 16
LN2 = math.log(2.0)
F32 = jnp.float32
BF16 = jnp.bfloat16

ROWS = {l: 1024 >> (l - 2) for l in range(3, 9)}
FIRST = {3: 0, 4: 512, 5: 768, 6: 896, 7: 960, 8: 992}
STACK = 1024


def dot(a, b):
    return lax.dot_general(a, b, (((1,), (0,)), ((), ())), preferred_element_type=F32)


def dot_nt(a, b):
    return lax.dot_general(a, b, (((1,), (1,)), ((), ())), preferred_element_type=F32)


def dot_tn(a, b):
    return lax.dot_general(a, b, (((0,), (0,)), ((), ())), preferred_element_type=F32)


def lane_of(rows):
    return lax.broadcasted_iota(jnp.int32, (rows, LANES), 1)


def low_lanes(rows):
    return lane_of(rows) < E


def swap_halves(x):
    return pltpu.roll(x, E, 1)


def shift_of(factor):
    return factor.bit_length() - 1


def pool_matrix(rows_out, factor=2):
    r = lax.broadcasted_iota(jnp.int32, (rows_out, rows_out * factor), 0)
    c = lax.broadcasted_iota(jnp.int32, (rows_out, rows_out * factor), 1)
    return jnp.where(c >> shift_of(factor) == r, 1.0 / factor, 0.0).astype(BF16)


def spread_matrix(rows_in, factor, value=1.0):
    r = lax.broadcasted_iota(jnp.int32, (rows_in * factor, rows_in), 0)
    c = lax.broadcasted_iota(jnp.int32, (rows_in * factor, rows_in), 1)
    return jnp.where(r >> shift_of(factor) == c, value, 0.0).astype(BF16)


def pieces(x, count):
    out = []
    for _ in range(count):
        part = x.astype(BF16)
        out.append(part)
        x = x - part.astype(F32)
    return out


def spread(matrix, x, count):
    total = None
    for part in pieces(x, count):
        term = dot(matrix, part)
        total = term if total is None else total + term
    return total


def halved(scratch, x):
    rows = x.shape[0]
    scratch[0:rows, :] = x
    first = scratch[pl.ds(0, rows // 2, stride=2), :]
    second = scratch[pl.ds(1, rows // 2, stride=2), :]
    return ((first + second) * 0.5).astype(BF16)


def repeated(scratch, x, factor):
    rows = x.shape[0]
    for i in range(factor):
        scratch[pl.ds(i, rows, stride=factor), :] = x
    return scratch[0 : rows * factor, :]


def call(kernel, outs, ins, scratch=(), flops=1e8, smem_first=False):
    specs = [pl.BlockSpec(memory_space=pltpu.VMEM) for _ in ins]
    if smem_first:
        specs[0] = pl.BlockSpec(memory_space=pltpu.SMEM)
    return pl.pallas_call(
        kernel,
        out_shape=[jax.ShapeDtypeStruct(s, d) for s, d in outs],
        in_specs=specs,
        out_specs=[pl.BlockSpec(memory_space=pltpu.VMEM) for _ in outs],
        scratch_shapes=list(scratch),
        compiler_params=pltpu.CompilerParams(vmem_limit_bytes=40 * 1024 * 1024),
        cost_estimate=pl.CostEstimate(
            flops=int(flops), bytes_accessed=2_000_000, transcendentals=0
        ),
    )(*ins)


def place(x, diagonal):
    return jnp.sum(jnp.where(diagonal, x, 0.0), axis=0, keepdims=True)


def pool_kernel(
    q_ref, k_ref, v_ref, q1_ref, kv1_ref, q2_ref, kv2_ref, send_ref, one_s, two_s, three_s
):
    low = low_lanes(32)
    low16 = low_lanes(16)
    level3 = []
    for index, ref in enumerate((q_ref, k_ref, v_ref)):
        yield
        one = halved(one_s.at[index], ref[...].astype(F32))
        two = halved(two_s.at[index], one.astype(F32))
        if index == 0:
            q1_ref[...] = one
            q2_ref[...] = two
        else:
            kv1_ref[index - 1] = one
            kv2_ref[index - 1] = two
        level3.append(halved(three_s.at[index], two.astype(F32)).astype(F32))
    q, k, v = level3
    qr, kr, vr = swap_halves(q), swap_halves(k), swap_halves(v)
    send_ref[0, 0:32, :] = jnp.where(low, k, vr).astype(BF16)
    send_ref[1, 0:32, :] = jnp.where(low, kr, v).astype(BF16)
    send_ref[0, 32:48, :] = jnp.where(low16, q[0:16], qr[16:32]).astype(BF16)
    send_ref[1, 32:48, :] = jnp.where(low16, qr[0:16], q[16:32]).astype(BF16)


def sibling_slots(me, level):
    bit = level - 5
    first = ((me >> bit) ^ 1) << bit
    return [first + i for i in range(1 << bit)]


def pool_stack(ref):
    for level in range(3, 8):
        rows = ROWS[level]
        step = min(rows, 256)
        matrix = pool_matrix(step // 2)
        for start in range(0, rows, step):
            source = slice(FIRST[level] + start, FIRST[level] + start + step)
            at = FIRST[level + 1] + start // 2
            ref[at : at + step // 2, :] = dot(matrix, ref[source, :]).astype(BF16)
    end = FIRST[8] + ROWS[8]
    ref[end:STACK, :] = jnp.zeros((STACK - end, LANES), BF16)


def prepare_keys_kernel(me_ref, recv_ref, kv_ref, block_ref, send_ref):
    me = me_ref[0]
    for d in range(RING):
        kv_ref[32 * d : 32 * d + 32, :] = recv_ref[d, 0:32, :]
    pool_stack(kv_ref)
    block_ref[...] = kv_ref[FIRST[5] : FIRST[5] + B, :]
    send_ref[...] = jnp.zeros_like(send_ref)
    for level in range(6, 9):
        rows = ROWS[level]
        block = kv_ref[FIRST[level] : FIRST[level] + rows, :]
        for slot in sibling_slots(me, level):
            send_ref[slot, 0:rows, :] = block


def prepare_queries_kernel(recv_ref, q_ref):
    low16 = low_lanes(16)
    for d in range(RING):
        packed = recv_ref[d, 32:48, :].astype(F32) * 0.125
        q_ref[32 * d : 32 * d + 16, :] = jnp.where(low16, packed, 0.0).astype(BF16)
        q_ref[32 * d + 16 : 32 * d + 32, :] = jnp.where(
            low16, swap_halves(packed), 0.0
        ).astype(BF16)
    pool_stack(q_ref)


def heads_forward(pairs, bias):
    heads = []
    for q, k, v in pairs:
        low_q = low_lanes(q.shape[0])
        low_v = low_lanes(v.shape[0])
        scaled = q.astype(F32) * 0.125
        values = v.astype(F32)
        for mine_q, mine_v in (
            (low_q, low_v),
            (jnp.logical_not(low_q), jnp.logical_not(low_v)),
        ):
            heads.append(
                (
                    jnp.where(mine_q, scaled, 0.0).astype(BF16),
                    k,
                    jnp.where(mine_v, values, 1.0).astype(BF16),
                )
            )
    scores = [dot_nt(q, k) for q, k, _ in heads]
    tops = [jnp.max(s, axis=1, keepdims=True) for s in scores]
    raised = [jnp.exp(s - top).astype(BF16) for s, top in zip(scores, tops)]
    sums = [dot(r, head[2]) for r, head in zip(raised, heads)]
    results = []
    for p, (q, _, _) in enumerate(pairs):
        low = low_lanes(q.shape[0])
        weighted = jnp.where(low, sums[2 * p], sums[2 * p + 1])
        total = swap_halves(jnp.where(low, sums[2 * p + 1], sums[2 * p]))
        top = jnp.where(low, tops[2 * p], tops[2 * p + 1])
        results.append((weighted / total, top + jnp.log(total) + bias))
    return results


def own_forward_kernel(steps):
    pairs = [(q[...], k[...], v[...]) for q, k, v, _, _ in steps]
    for views, (att, lse) in zip(steps, heads_forward(pairs, 0.0)):
        views[3][...] = att
        views[4][...] = lse


def core_forward_kernel(steps):
    pairs = [(q[...], kv[0], kv[1]) for q, kv, _, _ in steps]
    for views, (att, lse) in zip(steps, heads_forward(pairs, LN2)):
        views[2][...] = att
        views[3][...] = lse


def ring_pair(kva, kvb):
    return (
        jnp.concatenate([kva[0], kvb[0]], axis=0),
        jnp.concatenate([kva[1], kvb[1]], axis=0),
    )


def ring_forward_kernel(steps):
    pairs = [(q[...],) + ring_pair(kva, kvb) for q, kva, kvb, _, _ in steps]
    for views, (att, lse) in zip(steps, heads_forward(pairs, 2.0 * LN2)):
        views[3][...] = att
        views[4][...] = lse


def attend(q, kv, level):
    s = dot_nt(q, kv)
    top = jnp.max(s, axis=1, keepdims=True)
    raised = jnp.exp(s - top)
    ones = jnp.where(low_lanes(B), 1.0, kv.astype(F32)).astype(BF16)
    tops = jnp.broadcast_to(top + level * LN2, (q.shape[0], LANES))
    return tops, dot(raised.astype(BF16), ones)


def join(top_a, sum_a, top_b, sum_b):
    high = jnp.maximum(top_a, top_b)
    return high, jnp.exp(top_a - high) * sum_a + jnp.exp(top_b - high) * sum_b


def head_forward_kernel(q_ref, kv_ref, top_ref, sum_ref):
    tops, sums = None, None
    double = spread_matrix(64, 2)
    for level in (4, 3):
        new_tops, new_sums = [], []
        for block in range(ROWS[level] // B):
            at = FIRST[level] + B * block
            beside = FIRST[level] + B * (block ^ 1)
            top, total = attend(q_ref[at : at + B, :], kv_ref[beside : beside + B, :], level)
            if tops is not None:
                half = slice(64 * (block % 2), 64 * (block % 2) + 64)
                up_top = spread(double, tops[block // 2][half], 3)
                up_sum = spread(double, sums[block // 2][half], 2)
                top, total = join(top, total, up_top, up_sum)
            new_sums.append(total)
            new_tops.append(top)
        tops, sums = new_tops, new_sums
    for block in range(4):
        top_ref[B * block : B * block + B, :] = tops[block]
        sum_ref[B * block : B * block + B, :] = sums[block]


def head_merge_kernel(
    me_ref, beside_ref, recv_ref, q_ref, top_ref, sum_ref, send_ref, sibling_ref
):
    me = me_ref[0]
    sibling_ref[0] = beside_ref[...]
    levels = (8, 7, 6, 5)
    for level in levels[:3]:
        rows = ROWS[level]
        for index, slot in enumerate(sibling_slots(me, level)):
            sibling_ref[level - 5, rows * index : rows * index + rows, :] = recv_ref[
                slot, 0:rows, :
            ]
    keys = [sibling_ref[level - 5] for level in levels]
    scores = [
        dot_nt(q_ref[FIRST[level] : FIRST[level] + ROWS[level], :], kv)
        for level, kv in zip(levels, keys)
    ]
    highest = [jnp.max(s, axis=1, keepdims=True) for s in scores]
    raised = [jnp.exp(s - top).astype(BF16) for s, top in zip(scores, highest)]
    totals = [
        dot(r, jnp.where(low_lanes(B), 1.0, kv.astype(F32)).astype(BF16))
        for r, kv in zip(raised, keys)
    ]
    tops, sums = None, None
    for level, top, total in zip(levels, highest, totals):
        rows = ROWS[level]
        top = jnp.broadcast_to(top + level * LN2, (rows, LANES))
        if tops is not None:
            double = spread_matrix(rows // 2, 2)
            top, total = join(top, total, spread(double, tops, 3), spread(double, sums, 2))
        tops, sums = top, total
    low = low_lanes(B)
    low16 = low_lanes(16)
    diagonal = lax.broadcasted_iota(jnp.int32, (32, LANES), 0) == lane_of(32)
    four = spread_matrix(32, 4)
    tail = jnp.zeros((13, LANES), F32)
    spreads = [
        (spread(four, tops[32 * i : 32 * i + 32], 3), spread(four, sums[32 * i : 32 * i + 32], 2))
        for i in range(4)
    ]
    for i, (up_top, up_sum) in enumerate(spreads):
        at = slice(B * i, B * i + B)
        high, total = join(top_ref[at, :], sum_ref[at, :], up_top, up_sum)
        count = jnp.where(low, total, swap_halves(total))
        att = total / count
        lse = high + jnp.log(count)
        moved = swap_halves(att)
        for j in range(4):
            d = 4 * i + j
            r = 32 * j
            send_ref[d, 0:16, :] = jnp.where(
                low16, moved[r : r + 16], att[r + 16 : r + 32]
            ).astype(BF16)
            line = place(lse[r : r + 32], diagonal)
            parts = [part.astype(F32) for part in pieces(line, 3)]
            send_ref[d, 16:32, :] = jnp.concatenate(parts + [tail], axis=0).astype(BF16)


def combine_kernel(
    att0_ref, lse0_ref, att1_ref, lse1_ref, att2_ref, lse2_ref, recv_ref, grad_ref,
    out_ref, stat_ref, stat1_ref, g1_ref, stat2_ref, g2_ref, send_ref,
    lse_s, grad_s, align_s, r_s, g_s, f_s, r2_s, g2_s, f2_s, up_s,
):
    low16 = low_lanes(16)
    r = lax.broadcasted_iota(jnp.int32, (LANES, LANES), 0)
    c = lax.broadcasted_iota(jnp.int32, (LANES, LANES), 1)
    per_head = jnp.where(r >> 6 == c >> 6, 1.0, 0.0).astype(BF16)
    own = lax.broadcasted_iota(jnp.int32, (32, LANES), 0) == lane_of(32)

    packed_a = recv_ref[0].astype(F32)
    packed_b = recv_ref[1].astype(F32)
    rows_a, rows_b = packed_a[0:16], packed_b[0:16]
    att3 = jnp.concatenate(
        [
            jnp.where(low16, rows_a, swap_halves(rows_b)),
            jnp.where(low16, swap_halves(rows_a), rows_b),
        ],
        axis=0,
    )
    columns = []
    for packed in (packed_a, packed_b):
        line = packed[16:17] + packed[17:18] + packed[18:19]
        columns.append(jnp.sum(jnp.where(own, line, 0.0), axis=1, keepdims=True))
    lse = jnp.where(low_lanes(32), columns[0], columns[1])
    att = att3
    yield
    for index, (att_ref, lse_ref) in enumerate(
        ((att2_ref, lse2_ref), (att1_ref, lse1_ref), (att0_ref, lse0_ref))
    ):
        att = repeated(up_s.at[2 * index], att, 2)
        lse = repeated(up_s.at[2 * index + 1], lse, 2)
        own_lse = lse_ref[...]
        high = jnp.maximum(lse, own_lse)
        e_up = jnp.exp(lse - high)
        e_own = jnp.exp(own_lse - high)
        den = e_up + e_own
        att = (e_up * att + e_own * att_ref[...]) / den
        lse = high + jnp.log(den)
        yield
    attended = att.astype(BF16)
    full = lse
    out_ref[...] = attended
    grad = grad_ref[...].astype(F32)
    product = grad * attended.astype(F32)
    align = None
    for part in pieces(product, 2):
        term = dot(part, per_head)
        align = term if align is None else align + term
    yield
    stat_ref[...] = jnp.where(lane_of(256) & 32 == 0, full, align)
    lse_s[...] = full
    grad_s[...] = grad
    align_s[...] = align

    def fold(lse, grads, aligns, rows):
        a, b = pl.ds(0, rows, stride=2), pl.ds(1, rows, stride=2)
        la, lb = lse[a, :], lse[b, :]
        least = jnp.minimum(la, lb)
        ea, eb = jnp.exp(least - la), jnp.exp(least - lb)
        return (
            least,
            ea * grads[a, :] + eb * grads[b, :],
            ea * aligns[a, :] + eb * aligns[b, :],
        )

    r1, g1, f1 = fold(lse_s, grad_s, align_s, 128)
    stat1_ref[...] = jnp.where(lane_of(B) & 32 == 0, r1, f1)
    g1_ref[...] = g1.astype(BF16)
    yield
    r_s[...] = r1
    g_s[...] = g1
    f_s[...] = f1
    r2, g2, f2 = fold(r_s, g_s, f_s, 64)
    stat2_ref[...] = jnp.where(lane_of(64) & 32 == 0, r2, f2)
    g2_ref[...] = g2.astype(BF16)
    yield
    r2_s[...] = r2
    g2_s[...] = g2
    f2_s[...] = f2
    r3, g3, f3 = fold(r2_s, g2_s, f2_s, 32)
    row32 = lax.broadcasted_iota(jnp.int32, (32, LANES), 0)
    diagonal = row32 == (lane_of(32) & (E - 1))
    line_r = place(r3, diagonal)
    line_f = place(f3, diagonal)
    yield
    low1 = low_lanes(1)
    wide_r = jnp.broadcast_to(line_r, (8, LANES))
    wide_f = jnp.broadcast_to(line_f, (8, LANES))
    lines = (
        jnp.where(low1, line_r, swap_halves(wide_f)[0:1]),
        jnp.where(low1, swap_halves(wide_r)[0:1], line_f),
    )
    moved = swap_halves(g3)
    tail = jnp.zeros((13, LANES), F32)
    send_ref[0, 0:16, :] = jnp.where(low16, g3[0:16], moved[16:32]).astype(BF16)
    send_ref[1, 0:16, :] = jnp.where(low16, moved[0:16], g3[16:32]).astype(BF16)
    for j in range(2):
        parts = [part.astype(F32) for part in pieces(lines[j], 3)]
        send_ref[j, 16:32, :] = jnp.concatenate(parts + [tail], axis=0).astype(BF16)


def levels_backward(items):
    scores = [dot_nt(q, kv) for q, kv, _, _, _ in items]
    cograds = [
        jnp.where(low_lanes(q.shape[0]), 0.0, grads).astype(BF16)
        for q, _, _, grads, _ in items
    ]
    through = [dot_nt(c, item[1]) for c, item in zip(cograds, items)]
    weights = [
        jnp.exp(s + (level * LN2 - least[:, 0:1]))
        for s, (_, _, least, _, level) in zip(scores, items)
    ]
    slopes = [
        (w * (t - item[3][:, 0:1])).astype(BF16)
        for w, t, item in zip(weights, through, items)
    ]
    return [
        (
            dot(slope, item[1]) * 0.125,
            dot_tn(slope, item[0]) + dot_tn(w.astype(BF16), c),
        )
        for slope, w, c, item in zip(slopes, weights, cograds, items)
    ]


def unpack_and_fold(recv_ref, r_ref, g_ref, last):
    low = low_lanes(32)
    row32 = lax.broadcasted_iota(jnp.int32, (32, LANES), 0)
    first = row32 == lane_of(32)
    second = row32 + E == lane_of(32)
    for d in range(RING):
        packed = recv_ref[d].astype(F32)
        line = packed[16:17] + packed[17:18] + packed[18:19]
        least = jnp.sum(jnp.where(first, line, 0.0), axis=1, keepdims=True)
        flow = jnp.sum(jnp.where(second, line, 0.0), axis=1, keepdims=True)
        grads = jnp.concatenate([swap_halves(packed[0:16]), packed[0:16]], axis=0)
        r_ref[32 * d : 32 * d + 32, :] = jnp.broadcast_to(least, (32, LANES))
        g_ref[32 * d : 32 * d + 32, :] = jnp.where(low, flow, grads)
    for level in range(3, last):
        rows = ROWS[level + 1]
        a = pl.ds(FIRST[level], rows, stride=2)
        b = pl.ds(FIRST[level] + 1, rows, stride=2)
        la, lb = r_ref[a, :], r_ref[b, :]
        least = jnp.minimum(la, lb)
        to = slice(FIRST[level + 1], FIRST[level + 1] + rows)
        r_ref[to, :] = least
        g_ref[to, :] = jnp.exp(least - la) * g_ref[a, :] + jnp.exp(least - lb) * g_ref[b, :]


def head_top_kernel(
    me_ref, recv_ref, q_ref, sibling_ref, q5_ref, beside_ref, send_ref, r_ref, g_ref
):
    me = me_ref[0]
    unpack_and_fold(recv_ref, r_ref, g_ref, 8)
    send_ref[...] = jnp.zeros_like(send_ref)
    running = None
    levels = (8, 7, 6, 5)
    spans = [slice(FIRST[level], FIRST[level] + ROWS[level]) for level in levels]
    results = levels_backward(
        [
            (q_ref[at, :], sibling_ref[level - 5], r_ref[at, :], g_ref[at, :], level)
            for level, at in zip(levels, spans)
        ]
    )
    for level, (query_part, other_part) in zip(levels, results):
        rows = ROWS[level]
        other_part = other_part.astype(BF16)
        if level == 5:
            beside_ref[...] = other_part
        for index, slot in enumerate(sibling_slots(me, level) if level > 5 else ()):
            send_ref[slot, 0:rows, :] = other_part[rows * index : rows * index + rows]
        if running is None:
            running = query_part
        else:
            running = query_part + spread(spread_matrix(rows // 2, 2, 0.5), running, 2)
    q5_ref[...] = running


def head_low_kernel(q_ref, kv_ref, recv_ref, q5_ref, query_ref, other_ref, r_ref, g_ref):
    unpack_and_fold(recv_ref, r_ref, g_ref, 4)
    double = spread_matrix(64, 2, 0.5)
    query_up = [q5_ref[...]]
    other_up = None
    for level in (4, 3):
        blocks = ROWS[level] // B
        query_parts = [None] * blocks
        other_parts = [None] * blocks
        results = levels_backward(
            [
                (
                    q_ref[FIRST[level] + B * i : FIRST[level] + B * i + B, :],
                    kv_ref[FIRST[level] + B * (i ^ 1) : FIRST[level] + B * (i ^ 1) + B, :],
                    r_ref[FIRST[level] + B * i : FIRST[level] + B * i + B, :],
                    g_ref[FIRST[level] + B * i : FIRST[level] + B * i + B, :],
                    level,
                )
                for i in range(blocks)
            ]
        )
        for block, (query_part, other_part) in enumerate(results):
            query_parts[block] = query_part
            other_parts[block ^ 1] = other_part
        for block in range(blocks):
            half = slice(64 * (block % 2), 64 * (block % 2) + 64)
            query_parts[block] = query_parts[block] + spread(
                double, query_up[block // 2][half], 2
            )
            if other_up is not None:
                other_parts[block] = other_parts[block] + spread(
                    double, other_up[block // 2][half], 2
                )
        query_up, other_up = query_parts, other_parts
    for block in range(4):
        query_ref[B * block : B * block + B, :] = query_up[block]
        other_ref[B * block : B * block + B, :] = other_up[block]


def head_last_kernel(me_ref, beside_ref, recv_ref, query_ref, other_ref, send_ref):
    me = me_ref[0]
    running = None
    for level in (8, 7, 6):
        rows = ROWS[level]
        total = None
        for slot in sibling_slots(me, level):
            term = recv_ref[slot, 0:rows, :].astype(F32)
            total = term if total is None else total + term
        if running is not None:
            total = total + spread(spread_matrix(rows // 2, 2, 0.5), running, 2)
        running = total
    running = beside_ref[...].astype(F32) + spread(spread_matrix(64, 2, 0.5), running, 2)
    four = spread_matrix(8, 4, 0.25)
    low16 = low_lanes(16)
    for d in range(RING):
        at = slice(32 * d, 32 * d + 32)
        other = other_ref[at, :] + spread(four, running[8 * d : 8 * d + 8], 2)
        query = query_ref[at, :]
        send_ref[d, 0:32, :] = other.astype(BF16)
        send_ref[d, 32:48, :] = jnp.where(
            low16, query[0:16], swap_halves(query)[16:32]
        ).astype(BF16)


def heads_backward(pairs, bias):
    heads = []
    scaled_pairs = []
    for q, k, v, grads, stat in pairs:
        low_q = low_lanes(q.shape[0])
        scaled = q.astype(F32) * 0.125
        wide = grads.astype(F32)
        scaled_pairs.append(scaled.astype(BF16))
        for j in range(2):
            mine = low_q if j == 0 else jnp.logical_not(low_q)
            heads.append(
                (
                    jnp.where(mine, scaled, 0.0).astype(BF16),
                    k,
                    jnp.where(mine, wide, 0.0).astype(BF16),
                    v,
                    bias - stat[:, E * j : E * j + 1],
                    stat[:, E * j + 32 : E * j + 33],
                )
            )
    scores = [dot_nt(head[0], head[1]) for head in heads]
    through = [dot_nt(head[2], head[3]) for head in heads]
    weights = [jnp.exp(s + head[4]) for s, head in zip(scores, heads)]
    slopes = [
        (w * (t - head[5])).astype(BF16) for w, t, head in zip(weights, through, heads)
    ]
    weights = [w.astype(BF16) for w in weights]
    results = []
    for p, (q, k, _, grads, _) in enumerate(pairs):
        low_q = low_lanes(q.shape[0])
        low_k = low_lanes(k.shape[0])
        one, two = slopes[2 * p : 2 * p + 2]
        results.append(
            (
                jnp.where(low_q, dot(one, k), dot(two, k)) * 0.125,
                jnp.where(
                    low_k, dot_tn(one, scaled_pairs[p]), dot_tn(two, scaled_pairs[p])
                ),
                jnp.where(
                    low_k, dot_tn(weights[2 * p], grads), dot_tn(weights[2 * p + 1], grads)
                ),
            )
        )
    return results


def own_backward_kernel(steps):
    pairs = [tuple(view[...] for view in views[:5]) for views in steps]
    for views, grads in zip(steps, heads_backward(pairs, 0.0)):
        for view, value in zip(views[5:], grads):
            view[...] = value.astype(BF16)


def core_backward_kernel(steps):
    pairs = [(q[...], kv[0], kv[1], g[...], stat[...]) for q, kv, stat, g, _, _ in steps]
    for views, (dq, dk, dv) in zip(steps, heads_backward(pairs, LN2)):
        views[4][...] = dq.astype(BF16)
        views[5][0] = dk.astype(BF16)
        views[5][1] = dv.astype(BF16)


def ring_backward_kernel(steps):
    pairs = [
        (views[0][...],) + ring_pair(views[1], views[2]) + (views[4][...], views[3][...])
        for views in steps
    ]
    for views, (dq, dk, dv) in zip(steps, heads_backward(pairs, 2.0 * LN2)):
        views[5][...] = dq.astype(BF16)
        views[6][0] = dk[0:64]
        views[6][1] = dv[0:64]
        views[7][0] = dk[64:128].astype(BF16)
        views[7][1] = dv[64:128].astype(BF16)


def final_kernel(
    dq_ref, dk_ref, dv_ref, dq1_ref, kv1_ref, dq2_ref, kv2_ref, recv_ref,
    q_out, k_out, v_out, quarter_s, half_s, full_s,
):
    low = low_lanes(32)
    low16 = low_lanes(16)
    a = recv_ref[0].astype(F32)
    b = recv_ref[1].astype(F32)
    ar, br = swap_halves(a), swap_halves(b)
    g3k = jnp.where(low, a[0:32], br[0:32])
    g3v = jnp.where(low, ar[0:32], b[0:32])
    g3q = jnp.concatenate(
        [
            jnp.where(low16, a[32:48], br[32:48]),
            jnp.where(low16, ar[32:48], b[32:48]),
        ],
        axis=0,
    )
    work = (
        (dq_ref, dq1_ref[...].astype(F32), dq2_ref[...].astype(F32), g3q, q_out),
        (dk_ref, kv1_ref[0].astype(F32), kv2_ref[0].astype(F32), g3k, k_out),
        (dv_ref, kv1_ref[1].astype(F32), kv2_ref[1].astype(F32), g3v, v_out),
    )
    for index, (own, one, two, three, out) in enumerate(work):
        yield
        two = two + repeated(quarter_s.at[index], three * 0.5, 2)
        one = one + repeated(half_s.at[index], two * 0.5, 2)
        out[...] = (own[...].astype(F32) + repeated(full_s.at[index], one * 0.5, 2)).astype(BF16)


def pairs_of(mask, size):
    return [(source, source ^ mask) for source in range(size)]


def in_turn(kernel, steps):
    running = [kernel(*views) for views in steps]
    while running:
        running = [g for g in running if next(g, 0) is None]


class Tall:
    def __init__(self, rows):
        self.rows = rows

    def spec(self, step):
        return pl.BlockSpec((self.rows, LANES * step), lambda p: (0, p))

    def view(self, ref, i):
        return ref.at[:, LANES * i : LANES * (i + 1)]


class TwoTall(Tall):
    def spec(self, step):
        return pl.BlockSpec((2, self.rows, LANES * step), lambda p: (0, 0, p))

    def view(self, ref, i):
        return ref.at[:, :, LANES * i : LANES * (i + 1)]


class Slots(Tall):
    def spec(self, step):
        return pl.BlockSpec((2 * step, self.rows, LANES), lambda p: (p, 0, 0))

    def view(self, ref, i):
        return ref.at[2 * i : 2 * i + 2]


def over_pairs(
    kernel, outs, out_kinds, ins, in_kinds, scratch=(), step=2, flops=1e9, moved=5e6,
    joint=False, limit=60,
):
    kinds = in_kinds + out_kinds

    def body(*refs):
        steps = [
            [kind.view(ref, i) for kind, ref in zip(kinds, refs)]
            + [ref.at[i] for ref in refs[len(kinds) :]]
            for i in range(step)
        ]
        if joint:
            kernel(steps)
        else:
            in_turn(kernel, steps)

    return pl.pallas_call(
        body,
        grid=(PAIRS // step,),
        out_shape=[jax.ShapeDtypeStruct(s, d) for s, d in outs],
        in_specs=[kind.spec(step) for kind in in_kinds],
        out_specs=[kind.spec(step) for kind in out_kinds],
        scratch_shapes=[pltpu.VMEM((step,) + shape + (LANES,), F32) for shape in scratch],
        compiler_params=pltpu.CompilerParams(vmem_limit_bytes=limit * 1024 * 1024),
        cost_estimate=pl.CostEstimate(
            flops=int(flops), bytes_accessed=int(moved), transcendentals=0
        ),
    )(*ins)


STEPS = {"pool": 4, "local_forward": 4, "combine": 4, "local_backward": 4, "final": 4, "core_forward": 8, "core_backward": 4, "limit": 60}


def per_device(q, k, v, grad):
    size = lax.axis_size("seq")
    planes = size // RING
    rings = [[RING * g + i for i in range(RING)] for g in range(planes)]
    columns = [[RING * g + i for g in range(planes)] for i in range(RING)]
    me = (lax.axis_index("seq") // RING).astype(jnp.int32).reshape(1)
    rows, width = q.shape

    def exchange(x, groups):
        return lax.all_to_all(x, "seq", 0, 0, axis_index_groups=groups, tiled=True)

    def swapped(x, mask):
        return lax.ppermute(x, "seq", pairs_of(mask, size))

    quarter = (rows // 4, width)
    q1, kv1, q2, kv2, send1 = over_pairs(
        pool_kernel,
        [
            ((B, width), BF16),
            ((2, B, width), BF16),
            (quarter, BF16),
            ((2,) + quarter, BF16),
            ((RING, 48, LANES), BF16),
        ],
        [Tall(B), TwoTall(B), Tall(64), TwoTall(64), Slots(48)],
        (q, k, v),
        [Tall(rows)] * 3,
        scratch=((3, 256), (3, B), (3, 64)),
        step=STEPS["pool"],
    )
    kv1s = swapped(kv1, 1)
    recv1 = exchange(send1, rings)
    full = ((rows, width), F32)
    att0, lse0 = over_pairs(
        own_forward_kernel,
        [full, full],
        [Tall(rows)] * 2,
        (q, k, v),
        [Tall(rows)] * 3,
        step=STEPS["local_forward"],
        joint=True,
        flops=6e9,
        moved=1e7,
    )
    recv1, att0 = lax.optimization_barrier((recv1, att0))
    kvh, block, sendx = call(
        prepare_keys_kernel,
        [((STACK, LANES), BF16), ((B, LANES), BF16), ((RING, 64, LANES), BF16)],
        (me, recv1),
        smem_first=True,
    )
    sendx, recv1 = lax.optimization_barrier((sendx, recv1))
    (qh,) = call(prepare_queries_kernel, [((STACK, LANES), BF16)], (recv1,))
    sendx, kv2 = lax.optimization_barrier((sendx, kv2))
    beside = swapped(block, RING)
    kv2a = swapped(kv2, 2)
    kv2b = swapped(kv2a, 1)
    recvx = exchange(sendx, columns)
    half = (B, width)
    att1, lse1 = over_pairs(
        core_forward_kernel,
        [(half, F32), (half, F32)],
        [Tall(B)] * 2,
        (q1, kv1s),
        [Tall(B), TwoTall(B)],
        step=STEPS["core_forward"],
        joint=True,
        flops=2e9,
    )
    tops, sums = call(
        head_forward_kernel, [((512, LANES), F32)] * 2, (qh, kvh), flops=1e9
    )
    recvx, att1 = lax.optimization_barrier((recvx, att1))
    send2, siblings = call(
        head_merge_kernel,
        [((RING, 32, LANES), BF16), ((4, B, LANES), BF16)],
        (me, beside, recvx, qh, tops, sums),
        smem_first=True,
    )
    send2, q2_later = lax.optimization_barrier((send2, q2))
    recv2 = exchange(send2, rings)
    att2, lse2 = over_pairs(
        ring_forward_kernel,
        [(quarter, F32), (quarter, F32)],
        [Tall(64)] * 2,
        (q2_later, kv2a, kv2b),
        [Tall(64), TwoTall(64), TwoTall(64)],
        step=STEPS["core_forward"],
        joint=True,
        flops=2e9,
    )
    attended, stat, stat1, g1, stat2, g2, send3 = over_pairs(
        combine_kernel,
        [
            ((rows, width), BF16),
            full,
            (half, F32),
            (half, BF16),
            (quarter, F32),
            (quarter, BF16),
            ((RING, 32, LANES), BF16),
        ],
        [Tall(rows)] * 2 + [Tall(B)] * 2 + [Tall(64)] * 2 + [Slots(32)],
        (att0, lse0, att1, lse1, att2, lse2, recv2, grad),
        [Tall(rows)] * 2 + [Tall(B)] * 2 + [Tall(64)] * 2 + [Slots(32), Tall(rows)],
        scratch=((256,),) * 3 + ((B,),) * 3 + ((64,),) * 3 + ((6, 256),),
        step=STEPS["combine"],
    )
    recv3 = exchange(send3, rings)
    dq2, same, across = over_pairs(
        ring_backward_kernel,
        [(quarter, BF16), ((2,) + quarter, F32), ((2,) + quarter, BF16)],
        [Tall(64), TwoTall(64), TwoTall(64)],
        (q2, kv2a, kv2b, stat2, g2),
        [Tall(64), TwoTall(64), TwoTall(64), Tall(64), Tall(64)],
        step=STEPS["core_backward"],
        joint=True,
        flops=3e9,
    )
    recv3, dq2 = lax.optimization_barrier((recv3, dq2))
    partner = swapped(across, 1)
    back2 = swapped((same + partner.astype(F32)).astype(BF16), 2)
    stack = [pltpu.VMEM((STACK, LANES), F32)] * 2
    q5, part5, sendy = call(
        head_top_kernel,
        [((B, LANES), F32), ((B, LANES), BF16), ((RING, 64, LANES), BF16)],
        (me, recv3, qh, siblings),
        scratch=stack,
        smem_first=True,
    )
    part5, q1_late = lax.optimization_barrier((part5, q1))
    beside_grad = swapped(part5, RING)
    recvy = exchange(sendy, columns)
    query_low, other_low = call(
        head_low_kernel,
        [((512, LANES), F32)] * 2,
        (qh, kvh, recv3, q5),
        scratch=stack,
        flops=2e9,
    )
    dq1, dkv1 = over_pairs(
        core_backward_kernel,
        [(half, BF16), ((2, B, width), BF16)],
        [Tall(B), TwoTall(B)],
        (q1_late, kv1s, stat1, g1),
        [Tall(B), TwoTall(B)] + [Tall(B)] * 2,
        step=STEPS["core_backward"],
        joint=True,
        flops=3e9,
    )
    back1 = swapped(dkv1, 1)
    recvy, dq1 = lax.optimization_barrier((recvy, dq1))
    (send4,) = call(
        head_last_kernel,
        [((RING, 48, LANES), BF16)],
        (me, beside_grad, recvy, query_low, other_low),
        smem_first=True,
    )
    recv4 = exchange(send4, rings)
    dq, dk, dv = over_pairs(
        own_backward_kernel,
        [((rows, width), BF16)] * 3,
        [Tall(rows)] * 3,
        (q, k, v, grad, stat),
        [Tall(rows)] * 5,
        step=STEPS["local_backward"],
        joint=True,
        flops=9e9,
        moved=1e7,
    )
    query_grad, key_grad, value_grad = over_pairs(
        final_kernel,
        [((rows, width), BF16)] * 3,
        [Tall(rows)] * 3,
        (dq, dk, dv, dq1, back1, dq2, back2, recv4),
        [Tall(rows)] * 3 + [Tall(B), TwoTall(B), Tall(64), TwoTall(64), Slots(48)],
        scratch=((3, 64), (3, B), (3, 256)),
        step=STEPS["final"],
        limit=24,
    )
    return attended, query_grad, key_grad, value_grad


def solution(mesh):
    return jax.shard_map(
        per_device,
        mesh=mesh,
        in_specs=(P("seq", None),) * 4,
        out_specs=(P("seq", None),) * 4,
        check_vma=False,
    )
```
